32 devices in a mesh: dp: 8 (over y, x, core), rep: 4 (over z).
Axes of the slice: x: 2, y: 2, z: 4, core: 2. Of those that a mesh axis runs over, the one named last changes fastest.
Arguments:
- image_input: bfloat16 [64, 16, 32, 1024], P(('dp', 'rep')), may hold values from -11 to 11
- heights: int32 [64], P(('dp', 'rep')), may hold values from 4 to 8
- widths: int32 [64], P(('dp', 'rep')), may hold values from 8 to 16
- w_reduce: bfloat16 [1024, 512], replicated, may hold values from -0.1875 to 0.1875
- w_spatial: bfloat16 [3, 3, 512, 512], replicated, may hold values from -0.09375 to 0.09375
- w_expand: bfloat16 [512, 2048], replicated, may hold values from -0.25 to 0.25
- w_shortcut: bfloat16 [1024, 2048], replicated, may hold values from -0.1875 to 0.1875
- gain_reduce: float32 [512], replicated, may hold values from 0.25 to 1.75
- shift_reduce: float32 [512], replicated, may hold values from -2.5 to 2.5
- gain_spatial: float32 [512], replicated, may hold values from 0.25 to 1.75
- shift_spatial: float32 [512], replicated, may hold values from -2.5 to 2.5
- gain_expand: float32 [2048], replicated, may hold values from 0.25 to 1.75
- shift_expand: float32 [2048], replicated, may hold values from -2.5 to 2.5
- gain_shortcut: float32 [2048], replicated, may hold values from 0.25 to 1.75
- shift_shortcut: float32 [2048], replicated, may hold values from -2.5 to 2.5
- w_squeeze: bfloat16 [2048, 512], replicated, may hold values from -0.125 to 0.125
- w_window: bfloat16 [3, 3, 512, 512], replicated, may hold values from -0.09375 to 0.09375
- w_widen: bfloat16 [512, 2048], replicated, may hold values from -0.25 to 0.25
- gain_squeeze: float32 [512], replicated, may hold values from 0.25 to 1.75
- shift_squeeze: float32 [512], replicated, may hold values from -2.5 to 2.5
- gain_window: float32 [512], replicated, may hold values from 0.25 to 1.75
- shift_window: float32 [512], replicated, may hold values from -2.5 to 2.5
- gain_widen: float32 [2048], replicated, may hold values from 0.25 to 1.75
- shift_widen: float32 [2048], replicated, may hold values from -2.5 to 2.5
- cotangent: bfloat16 [64, 8, 16, 2048], P(('dp', 'rep')), may hold values from -6 to 6
Outputs:
- block_out: bfloat16 [64, 8, 16, 2048], P(('dp', 'rep'))
- input_grad: bfloat16 [64, 16, 32, 1024], P(('dp', 'rep'))
- w_reduce_grad: float32 [1024, 512], replicated
- w_spatial_grad: float32 [3, 3, 512, 512], replicated
- w_expand_grad: float32 [512, 2048], replicated
- w_shortcut_grad: float32 [1024, 2048], replicated
- gain_reduce_grad: float32 [512], replicated
- shift_reduce_grad: float32 [512], replicated
- gain_spatial_grad: float32 [512], replicated
- shift_spatial_grad: float32 [512], replicated
- gain_expand_grad: float32 [2048], replicated
- shift_expand_grad: float32 [2048], replicated
- gain_shortcut_grad: float32 [2048], replicated
- shift_shortcut_grad: float32 [2048], replicated
- w_squeeze_grad: float32 [2048, 512], replicated
- w_window_grad: float32 [3, 3, 512, 512], replicated
- w_widen_grad: float32 [512, 2048], replicated
- gain_squeeze_grad: float32 [512], replicated
- shift_squeeze_grad: float32 [512], replicated
- gain_window_grad: float32 [512], replicated
- shift_window_grad: float32 [512], replicated
- gain_widen_grad: float32 [2048], replicated
- shift_widen_grad: float32 [2048], replicated
The draws below stay inside these ranges and needn't reach their ends.
All inputs are finite; a program needn't handle non-finite values.
Results may differ from the reference program's by a relative error of at most 0.02.
Values sent between devices are 32-bit elements; how exact they have to be, the bound alone decides.
No kernel may reach another device: no remote copies, remote signals or barrier semaphores. Data moves between devices by JAX's collectives and lax.ppermute only.
A program may use at most 320 MiB of HBM per device.

```python
import jax
import jax.numpy as jnp
from jax import lax

C_IN = 1024
MID = 512
C_OUT = 2048
HO = 8
WO = 16
IMG_DEV = 2
SPAN_DP = 8
SPAN_REP = 4
IMAGES = 64


def device_place(image_count):
    image_ids = jnp.arange(image_count, dtype=jnp.int32)
    device = image_ids // IMG_DEV
    return (device // SPAN_REP, device % SPAN_REP, image_ids % IMG_DEV)


def rising_extent(position, span_count, largest):
    smallest = largest // 2
    return largest - (largest - smallest) * (span_count - 1 - position) // max(span_count - 1, 1)


def draw_heights(key, part):
    key = jax.random.fold_in(key, 11)
    dp_place, rep_place, within = device_place(IMAGES)
    base_rows = rising_extent(dp_place, SPAN_DP, HO)
    jitter = jax.random.randint(key, (IMAGES,), 0, 2)
    jitter = jnp.where(within == 0, 0, jitter)
    return jnp.maximum(base_rows - jitter, HO // 2).astype(jnp.int32)


def draw_widths(key, part):
    key = jax.random.fold_in(key, 23)
    dp_place, rep_place, within = device_place(IMAGES)
    base_cols = rising_extent(rep_place, SPAN_REP, WO)
    jitter = jax.random.randint(key, (IMAGES,), 0, 2)
    jitter = jnp.where(within == 0, 0, jitter)
    return jnp.maximum(base_cols - jitter, WO // 2).astype(jnp.int32)


def draw_image_input(key, part):
    key = jax.random.fold_in(key, 37)
    key_mean, key_noise, key_level = jax.random.split(key, 3)
    dp_place, rep_place, within = device_place(IMAGES)
    level = 0.5 + dp_place / max(SPAN_DP - 1, 1) + rep_place / max(SPAN_REP - 1, 1)
    level = level.astype(jnp.float32) * jax.random.uniform(key_level, (IMAGES,), jnp.float32, 0.8, 1.2)
    channel_mean = jax.random.uniform(key_mean, (C_IN,), jnp.float32, -1.5, 1.5)
    shape = (IMAGES, 2 * HO, 2 * WO, C_IN)
    noise = jax.random.truncated_normal(key_noise, -6.0, 6.0, shape, jnp.float32)
    values = level[:, None, None, None] * channel_mean + noise
    return values.astype(jnp.bfloat16)


def block_scale(key, shape, pieces, least, top_value):
    def one(dim, parts):
        steps = jax.random.uniform(jax.random.fold_in(jax.random.fold_in(key, 6), dim), (parts,), jnp.float32, least / len(pieces), top_value / len(pieces))
        return jnp.repeat(jnp.exp(steps), shape[dim] // parts).reshape((-1,) + (1,) * (len(shape) - dim - 1))

    level = one(*pieces[0])
    for cut in pieces[1:]:
        level = level * one(*cut)
    return level


def centred(rng, dims, deviation, limit, cuts=(), kind=jnp.bfloat16):
    level = block_scale(rng, dims, cuts, -0.22, 0.18) if cuts else 1.0
    values = jax.random.normal(rng, dims, jnp.float32) * deviation * level
    return jnp.minimum(jnp.maximum(values, -limit), limit).astype(kind)


def setup_inputs(seed: int = 0) -> dict:
    key_list = jax.random.split(jax.random.key(seed), 26)
    image_input = draw_image_input(jax.random.fold_in(key_list[25], 71), 0)
    heights = draw_heights(jax.random.fold_in(key_list[25], 71), 0)
    widths = draw_widths(jax.random.fold_in(key_list[25], 71), 0)
    w_reduce = centred(key_list[3], (C_IN, MID), C_IN ** -0.5, 0.1875)
    w_spatial = centred(key_list[4], (3, 3, MID, MID), (9 * MID) ** -0.5, 0.09375)
    w_expand = centred(key_list[5], (MID, C_OUT), MID ** -0.5, 0.25)
    w_shortcut = centred(key_list[6], (C_IN, C_OUT), C_IN ** -0.5, 0.1875)
    gain_reduce = jnp.clip(1.0 + 0.15 * jax.random.normal(key_list[7], (MID,), jnp.float32), 0.25, 1.75)
    shift_reduce = centred(key_list[8], (MID,), 0.5, 2.5, (), jnp.float32)
    gain_spatial = jnp.clip(1.0 + 0.15 * jax.random.normal(key_list[9], (MID,), jnp.float32), 0.25, 1.75)
    shift_spatial = centred(key_list[10], (MID,), 0.5, 2.5, (), jnp.float32)
    gain_expand = jnp.clip(1.0 + 0.15 * jax.random.normal(key_list[11], (C_OUT,), jnp.float32), 0.25, 1.75)
    shift_expand = centred(key_list[12], (C_OUT,), 0.5, 2.5, (), jnp.float32)
    gain_shortcut = jnp.clip(1.0 + 0.15 * jax.random.normal(key_list[13], (C_OUT,), jnp.float32), 0.25, 1.75)
    shift_shortcut = centred(key_list[14], (C_OUT,), 0.5, 2.5, (), jnp.float32)
    w_squeeze = centred(key_list[15], (C_OUT, MID), C_OUT ** -0.5, 0.125)
    w_window = centred(key_list[16], (3, 3, MID, MID), (9 * MID) ** -0.5, 0.09375)
    w_widen = centred(key_list[17], (MID, C_OUT), MID ** -0.5, 0.25)
    gain_squeeze = jnp.clip(1.0 + 0.15 * jax.random.normal(key_list[18], (MID,), jnp.float32), 0.25, 1.75)
    shift_squeeze = centred(key_list[19], (MID,), 0.5, 2.5, (), jnp.float32)
    gain_window = jnp.clip(1.0 + 0.15 * jax.random.normal(key_list[20], (MID,), jnp.float32), 0.25, 1.75)
    shift_window = centred(key_list[21], (MID,), 0.5, 2.5, (), jnp.float32)
    gain_widen = jnp.clip(1.0 + 0.15 * jax.random.normal(key_list[22], (C_OUT,), jnp.float32), 0.25, 1.75)
    shift_widen = centred(key_list[23], (C_OUT,), 0.5, 2.5, (), jnp.float32)
    cotangent = centred(key_list[24], (IMAGES, HO, WO, C_OUT), 1.0, 6.0, ((0, 32),))
    return dict(image_input=image_input, heights=heights, widths=widths, w_reduce=w_reduce, w_spatial=w_spatial, w_expand=w_expand, w_shortcut=w_shortcut, gain_reduce=gain_reduce, shift_reduce=shift_reduce, gain_spatial=gain_spatial, shift_spatial=shift_spatial, gain_expand=gain_expand, shift_expand=shift_expand, gain_shortcut=gain_shortcut, shift_shortcut=shift_shortcut, w_squeeze=w_squeeze, w_window=w_window, w_widen=w_widen, gain_squeeze=gain_squeeze, shift_squeeze=shift_squeeze, gain_window=gain_window, shift_window=shift_window, gain_widen=gain_widen, shift_widen=shift_widen, cotangent=cotangent)


EPSILON = 1e-05
HIGHEST = lax.Precision.HIGHEST

@jax.custom_vjp
def low(v):
    return lax.optimization_barrier(v.astype(jnp.bfloat16)).astype(jnp.float32)

@jax.custom_vjp
def low_back(v):
    return v

def low_keep(v):
    return (low(v), None)

def low_pass(kept, grad):
    return (grad,)

def back_keep(v):
    return (v, None)

def back_low(kept, grad):
    return (low(grad),)
low.defvjp(low_keep, low_pass)
low_back.defvjp(back_keep, back_low)

def pixel_mask(heights, widths, row_count, col_count):
    row_ids = jnp.arange(row_count, dtype=jnp.int32)
    col_ids = jnp.arange(col_count, dtype=jnp.int32)
    inside = (row_ids[None, :, None] < heights[:, None, None]) & (col_ids[None, None, :] < widths[:, None, None])
    return jnp.where(inside, 1.0, 0.0).astype(jnp.float32)[..., None]

def batch_norm(values, masking, pixels, norm_gain, norm_shift):
    totals = lax.optimization_barrier(jnp.sum(values * masking, axis=(0, 1, 2)))
    squares = lax.optimization_barrier(jnp.sum(values * values * masking, axis=(0, 1, 2)))
    average = totals / pixels
    inverse = lax.rsqrt(squares / pixels - average * average + EPSILON)
    return (values - average) * inverse * norm_gain + norm_shift

def pointwise(left, right):
    return jnp.einsum('bhwc,cd->bhwd', left, right, precision=HIGHEST)

def conv_taps(active, kernel, stride):
    return lax.conv_general_dilated(active, kernel, (stride, stride), ((1, 1), (1, 1)), dimension_numbers=('NHWC', 'HWIO', 'NHWC'), precision=HIGHEST)

def block(params, mask_in, mask_out, pixels):
    image_input, w_reduce, w_spatial, w_expand, w_shortcut, gain_reduce, shift_reduce, gain_spatial, shift_spatial, gain_expand, shift_expand, gain_shortcut, shift_shortcut, w_squeeze, w_window, w_widen, gain_squeeze, shift_squeeze, gain_window, shift_window, gain_widen, shift_widen = params
    masked_in = image_input * mask_in
    pre_reduce = low_back(pointwise(masked_in, w_reduce))
    norm_reduce = batch_norm(pre_reduce, mask_in, 4.0 * pixels, gain_reduce, shift_reduce)
    act_reduce = low(jax.nn.silu(norm_reduce) * mask_in)
    pre_spatial = low_back(conv_taps(act_reduce, w_spatial, 2))
    norm_spatial = batch_norm(pre_spatial, mask_out, pixels, gain_spatial, shift_spatial)
    act_spatial = low(jax.nn.silu(norm_spatial) * mask_out)
    pre_expand = low_back(pointwise(act_spatial, w_expand))
    pre_short = low_back(pointwise(masked_in[:, ::2, ::2, :], w_shortcut))
    joined = batch_norm(pre_expand, mask_out, pixels, gain_expand, shift_expand) + batch_norm(pre_short, mask_out, pixels, gain_shortcut, shift_shortcut)
    first_out = low(jax.nn.silu(joined) * mask_out)
    pre_squeeze = low_back(pointwise(first_out, w_squeeze))
    norm_squeeze = batch_norm(pre_squeeze, mask_out, pixels, gain_squeeze, shift_squeeze)
    act_squeeze = low(jax.nn.silu(norm_squeeze) * mask_out)
    pre_window = low_back(conv_taps(act_squeeze, w_window, 1))
    norm_window = batch_norm(pre_window, mask_out, pixels, gain_window, shift_window)
    act_window = low(jax.nn.silu(norm_window) * mask_out)
    pre_widen = low_back(pointwise(act_window, w_widen))
    final = batch_norm(pre_widen, mask_out, pixels, gain_widen, shift_widen) + first_out
    return jax.nn.silu(final) * mask_out

def reference(image_input, heights, widths, w_reduce, w_spatial, w_expand, w_shortcut, gain_reduce, shift_reduce, gain_spatial, shift_spatial, gain_expand, shift_expand, gain_shortcut, shift_shortcut, w_squeeze, w_window, w_widen, gain_squeeze, shift_squeeze, gain_window, shift_window, gain_widen, shift_widen, cotangent):
    mask_in = pixel_mask(2 * heights, 2 * widths, 2 * HO, 2 * WO)
    mask_out = pixel_mask(heights, widths, HO, WO)
    pixels = jnp.sum(mask_out)
    floats = (image_input, w_reduce, w_spatial, w_expand, w_shortcut, gain_reduce, shift_reduce, gain_spatial, shift_spatial, gain_expand, shift_expand, gain_shortcut, shift_shortcut, w_squeeze, w_window, w_widen, gain_squeeze, shift_squeeze, gain_window, shift_window, gain_widen, shift_widen)
    floats = tuple((element.astype(jnp.float32) for element in floats))

    def forward(params):
        return block(params, mask_in, mask_out, pixels)
    result, pullback = jax.vjp(forward, floats)
    grads, = pullback(cotangent.astype(jnp.float32))
    return (result.astype(jnp.bfloat16), grads[0].astype(jnp.bfloat16), grads[1], grads[2], grads[3], grads[4], grads[5], grads[6], grads[7], grads[8], grads[9], grads[10], grads[11], grads[12], grads[13], grads[14], grads[15], grads[16], grads[17], grads[18], grads[19], grads[20], grads[21])
```

```python
import functools

import jax
import jax.numpy as jnp
import numpy as np
from jax import lax
from jax.experimental import pallas as pl
from jax.experimental.pallas import tpu as pltpu
from jax.sharding import PartitionSpec as P

EPSILON = 1e-05
F32 = jnp.float32
BF16 = jnp.bfloat16
AXES = ("dp", "rep")
LANES = 128
TILE = 512
ROWS = TILE // LANES


def dot(left, right):
    return jnp.dot(left, right, preferred_element_type=F32)


def dot_nt(left, right):
    return lax.dot_general(left, right, (((1,), (1,)), ((), ())), preferred_element_type=F32)


def pack(vector):
    return jnp.concatenate(
        [vector[:, LANES * k : LANES * (k + 1)] for k in range(vector.shape[1] // LANES)], axis=0
    )


def unpack(rows):
    return jnp.concatenate([rows[k : k + 1, :] for k in range(rows.shape[0])], axis=1)


def col_sum(values):
    return jnp.sum(values, axis=0, keepdims=True)


def stat_tile(first, second):
    return jnp.concatenate([pack(col_sum(first)), pack(col_sum(second))], axis=0)


def coefficients(stat_ref, count_ref, param_ref, factor=1.0):
    stat, param = stat_ref[...], param_ref[...]
    count = count_ref[0:ROWS, :] * factor
    average = stat[0:ROWS] / count
    inverse = lax.rsqrt(stat[ROWS : 2 * ROWS] / count - average * average + EPSILON)
    return (
        unpack(average),
        unpack(inverse),
        unpack(param[0:ROWS]),
        unpack(param[ROWS : 2 * ROWS]),
    )


def back_coefficients(grad_rows_shift, grad_rows_gain, count_ref, factor=1.0):
    count = count_ref[0:ROWS, :] * factor
    return unpack(grad_rows_shift / count), unpack(grad_rows_gain / count)


def logistic(values):
    return 0.5 * jnp.tanh(0.5 * values) + 0.5


def silu(values):
    return values * logistic(values)


def slope(values):
    gate = logistic(values)
    return gate * (1.0 + values * (1.0 - gate))


def column(mask_ref):
    return mask_ref[:, 0:1]


def pixel_ids(pixels, width):
    return lax.broadcasted_iota(jnp.int32, (pixels, 1), 0)


def shift_cols(values, step, width):
    pixels = values.shape[0]
    place = lax.rem(pixel_ids(pixels, width), width)
    rolled = pltpu.roll(values, (-step) % pixels, 0)
    keep = place < width - step if step > 0 else place >= -step
    return jnp.where(keep, rolled, 0.0)


def shift_rows(values, step, width, height):
    pixels = values.shape[0]
    place = lax.rem(lax.div(pixel_ids(pixels, width), width), height)
    rolled = pltpu.roll(values, (-step * width) % pixels, 0)
    keep = place < height - step if step > 0 else place >= -step
    return jnp.where(keep, rolled, 0.0)


def full(shape):
    zeros = (0,) * len(shape)
    return pl.BlockSpec(shape, lambda *_: zeros)


def cols(rows, width):
    return pl.BlockSpec((rows, width), lambda n, *_: (0, n))


def tile_at(index, rows=8):
    return pl.BlockSpec((rows, LANES), lambda *_: (index, 0))


def tile_n(offset=0, rows=8):
    return pl.BlockSpec((rows, LANES), lambda n, *_: (offset + n, 0))


def call(kernel, grid, in_specs, out_specs, out_shape, scratch=(), mib=40, flops=0, nbytes=0):
    return pl.pallas_call(
        kernel,
        grid=grid,
        in_specs=in_specs,
        out_specs=out_specs,
        out_shape=out_shape,
        scratch_shapes=scratch,
        compiler_params=pltpu.CompilerParams(
            vmem_limit_bytes=mib << 20, dimension_semantics=("arbitrary",) * len(grid)
        ),
        cost_estimate=pl.CostEstimate(flops=flops, bytes_accessed=nbytes, transcendentals=0),
    )


def shaped(shape, dtype=F32):
    return jax.ShapeDtypeStruct(shape, dtype)


def reduce_kernel(quarter, x_ref, perm_ref, mask_ref, all_mask_ref, w_ref, xp_ref, pre_ref, stat_ref, acc_ref):
    step = pl.program_id(0)
    mask = column(mask_ref)
    masking = jnp.concatenate([mask] * 4, axis=0)
    planes = (dot(perm_ref[...], x_ref[...]) * masking).astype(BF16)
    pre = dot(planes, w_ref[...])
    for q in range(4):
        xp_ref[q] = planes[q * quarter : (q + 1) * quarter]
        pre_ref[q] = pre[q * quarter : (q + 1) * quarter]

    @pl.when(step == 0)
    def _():
        acc_ref[...] = jnp.zeros_like(acc_ref)

    acc_ref[0:1, :] += col_sum(pre)
    acc_ref[1:2, :] += col_sum(pre * pre)

    @pl.when(step == pl.num_programs(0) - 1)
    def _():
        stat_ref[0:8, :] = jnp.concatenate([pack(acc_ref[0:1, :]), pack(acc_ref[1:2, :])], axis=0)
        stat_ref[8:16, :] = jnp.broadcast_to(col_sum(all_mask_ref[...]), (8, LANES))


def product_kernel(x_ref, w_ref, out_ref, stat_ref):
    pre = dot(x_ref[0], w_ref[...])
    out_ref[...] = pre
    stat_ref[...] = stat_tile(pre, pre * pre)


def spatial_kernel(width, height, pre_ref, stat_ref, count_ref, param_ref, mask_ref, w_ref, act_ref, out_ref, out_stat_ref, y_ref):
    r = pl.program_id(0)
    mask = column(mask_ref)

    @pl.when(r == 0)
    def _():
        average, inverse, gain, shift = coefficients(stat_ref, count_ref, param_ref, 4.0)
        for q in range(4):
            norm = (pre_ref[q] - average) * inverse * gain + shift
            act_ref[q] = (silu(norm) * mask).astype(BF16)

    row_parity = jnp.where(r == 1, 0, 1)
    row_shift = jnp.where(r == 0, 1, 0)
    even, odd = act_ref[2 * row_parity], act_ref[2 * row_parity + 1]
    straight = dot(even, w_ref[0, 1]) + dot(odd, w_ref[0, 2])
    moved = dot(odd, w_ref[0, 0])

    @pl.when(r < 2)
    def _():
        y_ref[2 * row_shift] = straight
        y_ref[2 * row_shift + 1] = moved

    @pl.when(r == 2)
    def _():
        upper = y_ref[2] + shift_cols(y_ref[3], -1, width)
        lower = y_ref[0] + straight + shift_cols(y_ref[1] + moved, -1, width)
        pre = lower + shift_rows(upper, -1, width, height)
        out_ref[...] = pre
        masked = pre * mask
        out_stat_ref[...] = stat_tile(masked, masked * pre)


def expand_kernel(pre_ref, stat_ref, count_ref, param_ref, mask_ref, w_ref, act_ref, out_ref, out_stat_ref):
    @pl.when(pl.program_id(0) == 0)
    def _():
        average, inverse, gain, shift = coefficients(stat_ref, count_ref, param_ref)
        norm = (pre_ref[...] - average) * inverse * gain + shift
        act_ref[...] = (silu(norm) * column(mask_ref)).astype(BF16)

    pre = dot(act_ref[...], w_ref[...])
    out_ref[...] = pre
    out_stat_ref[...] = stat_tile(pre, pre * pre)


def join_kernel(pe_ref, ps_ref, se_ref, ss_ref, count_ref, qe_ref, qs_ref, mask_ref, w_ref, first_ref, out_ref, out_stat_ref):
    n = pl.program_id(0)
    average_e, inverse_e, gain_e, shift_e = coefficients(se_ref, count_ref, qe_ref)
    average_s, inverse_s, gain_s, shift_s = coefficients(ss_ref, count_ref, qs_ref)
    joined = (pe_ref[...] - average_e) * inverse_e * gain_e + shift_e
    joined += (ps_ref[...] - average_s) * inverse_s * gain_s + shift_s
    first = (silu(joined) * column(mask_ref)).astype(BF16)
    first_ref[...] = first
    part = dot(first, w_ref[...])

    @pl.when(n == 0)
    def _():
        out_ref[...] = part

    @pl.when(n > 0)
    def _():
        out_ref[...] += part

    @pl.when(n == pl.num_programs(0) - 1)
    def _():
        pre = out_ref[...]
        out_stat_ref[...] = stat_tile(pre, pre * pre)


def store_padded(target_ref, values, step, width, height, images):
    area = width * height
    channels = values.shape[1]
    zeros = jnp.zeros((width, channels), BF16)
    for k in range(3):
        moved = values if k == 1 else shift_cols(values, step * (k - 1), width)
        moved = moved.astype(BF16)
        for b in range(images):
            target_ref[k, b, 0:width, :] = zeros
            target_ref[k, b, area + width : area + 2 * width, :] = zeros
            target_ref[k, b, width : area + width, :] = moved[b * area : (b + 1) * area]


def window_rows(ref, k, first, area, images):
    return jnp.concatenate([ref[k, b, pl.ds(first, area), :] for b in range(images)], axis=0)


def window_kernel(width, height, images, pre_ref, stat_ref, count_ref, param_ref, mask_ref, w_ref, act_ref, out_ref, out_stat_ref, pad_ref):
    r = pl.program_id(0)

    @pl.when(r == 0)
    def _():
        average, inverse, gain, shift = coefficients(stat_ref, count_ref, param_ref)
        norm = (pre_ref[...] - average) * inverse * gain + shift
        act = silu(norm) * column(mask_ref)
        act_ref[...] = act.astype(BF16)
        store_padded(pad_ref, act, 1, width, height, images)

    first = pl.multiple_of(r * width, width)
    part = dot(window_rows(pad_ref, 0, first, width * height, images), w_ref[0, 0])
    for k in (1, 2):
        part += dot(window_rows(pad_ref, k, first, width * height, images), w_ref[0, k])

    @pl.when(r == 0)
    def _():
        out_ref[...] = part

    @pl.when(r > 0)
    def _():
        out_ref[...] += part

    @pl.when(r == 2)
    def _():
        pre = out_ref[...]
        masked = pre * column(mask_ref)
        out_stat_ref[...] = stat_tile(masked, masked * pre)


def final_kernel(pre_ref, stat_ref, count_ref, param_ref, mask_ref, first_ref, cot_ref, out_ref, grad_ref, sum_ref):
    average, inverse, gain, shift = coefficients(stat_ref, count_ref, param_ref)
    mask = column(mask_ref)
    hat = (pre_ref[...] - average) * inverse
    final = hat * gain + shift + first_ref[...].astype(F32)
    gate = logistic(final)
    out_ref[...] = (final * gate * mask).astype(BF16)
    grad = cot_ref[...].astype(F32) * mask * (gate * (1.0 + final * (1.0 - gate)))
    grad_ref[...] = grad
    sum_ref[...] = stat_tile(grad, grad * hat)


def norm_back(grad, hat, scale, shift_term, gain_term, mask):
    return ((grad - mask * (shift_term + hat * gain_term)) * scale).astype(BF16)


def widen_back_kernel(
    grad_ref, pre_ref, stat_ref, gsum_ref, count_ref, param_ref, mask_ref, w_ref, in_ref, in_stat_ref, in_param_ref,
    gpre_ref, out_ref, sum_ref,
):
    n = pl.program_id(0)
    mask = column(mask_ref)
    average, inverse, gain, _ = coefficients(stat_ref, count_ref, param_ref)
    gsum = gsum_ref[...]
    shift_term, gain_term = back_coefficients(gsum[0:ROWS], gsum[ROWS : 2 * ROWS], count_ref)
    hat = (pre_ref[...] - average) * inverse
    gpre = norm_back(grad_ref[...], hat, inverse * gain, shift_term, gain_term, mask)
    gpre_ref[...] = gpre
    part = dot_nt(gpre, w_ref[...])

    @pl.when(n == 0)
    def _():
        out_ref[...] = part

    @pl.when(n > 0)
    def _():
        out_ref[...] += part

    @pl.when(n == pl.num_programs(0) - 1)
    def _():
        finish_back(in_ref[...], in_stat_ref, count_ref, in_param_ref, mask, out_ref, sum_ref)


def finish_back(pre, stat_ref, count_ref, param_ref, mask, out_ref, sum_ref):
    average, inverse, gain, shift = coefficients(stat_ref, count_ref, param_ref)
    hat = (pre - average) * inverse
    grad = out_ref[...] * mask * slope(hat * gain + shift)
    out_ref[...] = grad
    sum_ref[...] = stat_tile(grad, grad * hat)


def pre_grad(grad_ref, pre_ref, stat_ref, gsum_ref, count_ref, param_ref, mask):
    average, inverse, gain, _ = coefficients(stat_ref, count_ref, param_ref)
    gsum = gsum_ref[...]
    shift_term, gain_term = back_coefficients(gsum[0:ROWS], gsum[ROWS : 2 * ROWS], count_ref)
    hat = (pre_ref[...] - average) * inverse
    return norm_back(grad_ref[...], hat, inverse * gain, shift_term, gain_term, mask)


def window_back_kernel(
    width, height, images,
    grad_ref, pre_ref, stat_ref, gsum_ref, count_ref, param_ref, mask_ref, w_ref, in_ref, in_stat_ref, in_param_ref,
    pad_ref, out_ref, sum_ref,
):
    r = pl.program_id(0)
    mask = column(mask_ref)

    @pl.when(r == 0)
    def _():
        gpre = pre_grad(grad_ref, pre_ref, stat_ref, gsum_ref, count_ref, param_ref, mask)
        store_padded(pad_ref, gpre.astype(F32), -1, width, height, images)

    first = pl.multiple_of((2 - r) * width, width)
    part = dot_nt(window_rows(pad_ref, 0, first, width * height, images), w_ref[0, 0])
    for k in (1, 2):
        part += dot_nt(window_rows(pad_ref, k, first, width * height, images), w_ref[0, k])

    @pl.when(r == 0)
    def _():
        out_ref[...] = part

    @pl.when(r > 0)
    def _():
        out_ref[...] += part

    @pl.when(r == 2)
    def _():
        finish_back(in_ref[...], in_stat_ref, count_ref, in_param_ref, mask, out_ref, sum_ref)


def squeeze_back_kernel(
    grad_ref, pre_ref, stat_ref, gsum_ref, count_ref, param_ref, mask_ref, w_ref,
    gfinal_ref, pe_ref, ps_ref, se_ref, ss_ref, qe_ref, qs_ref,
    gpre_ref, gj_ref, sum_ref,
):
    mask = column(mask_ref)

    @pl.when(pl.program_id(0) == 0)
    def _():
        gpre_ref[...] = pre_grad(grad_ref, pre_ref, stat_ref, gsum_ref, count_ref, param_ref, mask)

    gfirst = gfinal_ref[...] + dot_nt(gpre_ref[...], w_ref[...])
    average_e, inverse_e, gain_e, shift_e = coefficients(se_ref, count_ref, qe_ref)
    average_s, inverse_s, gain_s, shift_s = coefficients(ss_ref, count_ref, qs_ref)
    hat_e = (pe_ref[...] - average_e) * inverse_e
    hat_s = (ps_ref[...] - average_s) * inverse_s
    joined = hat_e * gain_e + shift_e + (hat_s * gain_s + shift_s)
    grad = gfirst * mask * slope(joined)
    gj_ref[...] = grad
    sum_ref[...] = jnp.concatenate(
        [stat_tile(grad, grad * hat_e), pack(col_sum(grad * hat_s)), jnp.zeros((ROWS, LANES), F32)], axis=0
    )


def expand_back_kernel(
    gj_ref, pe_ref, ps_ref, se_ref, ss_ref, gsum_ref, count_ref, qe_ref, qs_ref, mask_ref, w_ref,
    in_ref, in_stat_ref, in_param_ref,
    ge_ref, gs_ref, out_ref, sum_ref,
):
    n = pl.program_id(0)
    mask = column(mask_ref)
    average_e, inverse_e, gain_e, _ = coefficients(se_ref, count_ref, qe_ref)
    average_s, inverse_s, gain_s, _ = coefficients(ss_ref, count_ref, qs_ref)
    gsum = gsum_ref[...]
    shift_term, gain_e_term = back_coefficients(gsum[0:ROWS], gsum[ROWS : 2 * ROWS], count_ref)
    _, gain_s_term = back_coefficients(gsum[0:ROWS], gsum[2 * ROWS : 3 * ROWS], count_ref)
    grad = gj_ref[...]
    hat_e = (pe_ref[...] - average_e) * inverse_e
    hat_s = (ps_ref[...] - average_s) * inverse_s
    ge = norm_back(grad, hat_e, inverse_e * gain_e, shift_term, gain_e_term, mask)
    ge_ref[...] = ge
    gs_ref[...] = norm_back(grad, hat_s, inverse_s * gain_s, shift_term, gain_s_term, mask)
    part = dot_nt(ge, w_ref[...])

    @pl.when(n == 0)
    def _():
        out_ref[...] = part

    @pl.when(n > 0)
    def _():
        out_ref[...] += part

    @pl.when(n == pl.num_programs(0) - 1)
    def _():
        finish_back(in_ref[...], in_stat_ref, count_ref, in_param_ref, mask, out_ref, sum_ref)


def spatial_back_kernel(
    width, height,
    grad_ref, pre_ref, stat_ref, gsum_ref, count_ref, param_ref, mask_ref, w_ref, in_ref, in_stat_ref, in_param_ref,
    shift_ref, out_ref, sum_ref,
):
    r = pl.program_id(0)
    mask = column(mask_ref)

    @pl.when(r == 0)
    def _():
        gpre = pre_grad(grad_ref, pre_ref, stat_ref, gsum_ref, count_ref, param_ref, mask).astype(F32)
        below = shift_rows(gpre, 1, width, height)
        shift_ref[0] = gpre.astype(BF16)
        shift_ref[1] = shift_cols(gpre, 1, width).astype(BF16)
        shift_ref[2] = below.astype(BF16)
        shift_ref[3] = shift_cols(below, 1, width).astype(BF16)

    row_parity = jnp.where(r == 1, 0, 1)
    row_shift = jnp.where(r == 0, 1, 0)
    straight, moved = shift_ref[2 * row_shift], shift_ref[2 * row_shift + 1]
    even = dot_nt(straight, w_ref[0, 1])
    odd = dot_nt(moved, w_ref[0, 0]) + dot_nt(straight, w_ref[0, 2])

    @pl.when(r < 2)
    def _():
        out_ref[2 * row_parity] = even
        out_ref[2 * row_parity + 1] = odd

    @pl.when(r == 2)
    def _():
        out_ref[2] += even
        out_ref[3] += odd
        average, inverse, gain, shift = coefficients(in_stat_ref, count_ref, in_param_ref, 4.0)
        total = total_hat = jnp.zeros((1, out_ref.shape[2]), F32)
        for q in range(4):
            hat = (in_ref[q] - average) * inverse
            grad = out_ref[q] * mask * slope(hat * gain + shift)
            out_ref[q] = grad
            total += col_sum(grad)
            total_hat += col_sum(grad * hat)
        sum_ref[...] = jnp.concatenate([pack(total), pack(total_hat)], axis=0)


def short_back_kernel(g_ref, w_ref, out_ref):
    part = dot_nt(g_ref[...], w_ref[...])

    @pl.when(pl.program_id(0) == 0)
    def _():
        out_ref[...] = part

    @pl.when(pl.program_id(0) > 0)
    def _():
        out_ref[...] += part


def reduce_back_kernel(
    quarter, grad_ref, pre_ref, stat_ref, gsum_ref, count_ref, param_ref, mask_ref, w_ref, short_ref, perm_ref,
    gpre_ref, out_ref,
):
    mask = column(mask_ref)
    masking = jnp.concatenate([mask] * 4, axis=0)
    average, inverse, gain, _ = coefficients(stat_ref, count_ref, param_ref, 4.0)
    gsum = gsum_ref[...]
    shift_term, gain_term = back_coefficients(gsum[0:ROWS], gsum[ROWS : 2 * ROWS], count_ref, 4.0)
    grad = jnp.concatenate([grad_ref[q] for q in range(4)], axis=0)
    pre = jnp.concatenate([pre_ref[q] for q in range(4)], axis=0)
    hat = (pre - average) * inverse
    gpre = norm_back(grad, hat, inverse * gain, shift_term, gain_term, masking)
    for q in range(4):
        gpre_ref[q] = gpre[q * quarter : (q + 1) * quarter]
    image = dot_nt(gpre, w_ref[...])
    image = jnp.concatenate([image[0:quarter] + short_ref[...], image[quarter:]], axis=0)
    image = (image * masking).astype(BF16)
    out_ref[...] = dot(perm_ref[...], image).astype(BF16)


def outer_kernel(pick, left_blocks, core_ref, *refs):
    left_ref, right_ref = refs[0], refs[1]
    keep_ref, send_ref, turned_ref = refs[-3], refs[-2], refs[-1]
    b = pl.program_id(0)

    @pl.when(lax.rem(b, left_blocks[1]) == 0)
    def _():
        left = left_ref[...] if len(left_ref.shape) == 2 else left_ref[0]
        turned_ref[...] = left.T

    half = TILE // 2
    right = pick(right_ref, b)
    core = core_ref[0]
    keep_ref[...] = dot(turned_ref[pl.ds(pl.multiple_of(core * half, half), half), :], right)
    send_ref[...] = dot(turned_ref[pl.ds(pl.multiple_of((1 - core) * half, half), half), :], right)


def outer(core, left, left_spec, right, right_spec, pick, blocks, per_left, place, total, into):
    half = TILE // 2
    pixels = left_spec.block_shape[-2]
    shape = shaped((total * half, TILE))
    out_spec = pl.BlockSpec((half, TILE), lambda b, *_: (place + b, 0))
    aliases = {} if into is None else {3: 0, 4: 1}
    extra = () if into is None else tuple(into)
    return pl.pallas_call(
        functools.partial(outer_kernel, pick, (None, per_left)),
        grid_spec=pltpu.PrefetchScalarGridSpec(
            num_scalar_prefetch=1,
            grid=(blocks,),
            in_specs=[left_spec, right_spec] + [pl.BlockSpec(memory_space=pl.ANY)] * len(extra),
            out_specs=[out_spec, out_spec],
            scratch_shapes=[pltpu.VMEM((TILE, pixels), BF16)],
        ),
        out_shape=[shape, shape],
        input_output_aliases=aliases,
        compiler_params=pltpu.CompilerParams(
            vmem_limit_bytes=24 << 20, dimension_semantics=("arbitrary",)
        ),
        cost_estimate=pl.CostEstimate(
            flops=2 * blocks * pixels * TILE * TILE,
            bytes_accessed=blocks * TILE * TILE * 4,
            transcendentals=0,
        ),
    )(core, left, right, *extra)


def assemble_kernel(core_ref, mine_ref, other_ref, out_ref):
    half = TILE // 2
    core = core_ref[0]
    out_ref[pl.ds(pl.multiple_of(core * half, half), half), :] = mine_ref[...]
    out_ref[pl.ds(pl.multiple_of((1 - core) * half, half), half), :] = other_ref[...]


def assemble(core, mine, other, place, blocks, shape, where):
    half = TILE // 2
    in_spec = pl.BlockSpec((half, TILE), lambda b, *_: (place + b, 0))
    return pl.pallas_call(
        assemble_kernel,
        grid_spec=pltpu.PrefetchScalarGridSpec(
            num_scalar_prefetch=1,
            grid=(blocks,),
            in_specs=[in_spec, in_spec],
            out_specs=pl.BlockSpec((TILE, TILE), lambda b, *_: where(b)),
        ),
        out_shape=shaped(shape),
        compiler_params=pltpu.CompilerParams(
            vmem_limit_bytes=16 << 20, dimension_semantics=("arbitrary",)
        ),
        cost_estimate=pl.CostEstimate(
            flops=0, bytes_accessed=2 * blocks * TILE * TILE * 4, transcendentals=0
        ),
    )(core, mine, other)


def bits_of(first, size):
    found = []
    while size > 1:
        found.append(first)
        first, size = first * 2, size // 2
    return found


def mesh_bits(dp, rep):
    side = int(round(dp**0.5))
    if side * side == dp:
        return 1, bits_of(rep, side), bits_of(rep * side, side), bits_of(2, rep // 2)
    side = int(round((dp // 2) ** 0.5))
    return rep, bits_of(2 * rep, side), bits_of(2 * rep * side, side), bits_of(1, rep)


def swap(values, bit, devices):
    return lax.ppermute(values, AXES, [(i, i ^ bit) for i in range(devices)])


def sync_all(tile, devices):
    copies = jnp.broadcast_to(tile[None], (devices,) + tile.shape)
    return jnp.sum(lax.all_to_all(copies, AXES, 0, 0, tiled=True), axis=0)


def sync_hops(tile, bits, devices):
    for bit in bits:
        tile = tile + swap(tile, bit, devices)
    return tile


def device_bit(flat, bit):
    return lax.rem(lax.div(flat, bit), 2)


def scatter_sum(keep, send, flat, core, order, devices):
    received = swap(send, core, devices)
    for bit in order:
        rows = keep.shape[0] // 2
        own = device_bit(flat, bit)
        start, away = own * rows, (1 - own) * rows
        send = lax.dynamic_slice_in_dim(keep, away, rows) + lax.dynamic_slice_in_dim(received, away, rows)
        keep = lax.dynamic_slice_in_dim(keep, start, rows) + lax.dynamic_slice_in_dim(received, start, rows)
        received = swap(send, bit, devices)
    return keep + received


def gather_back(shard, flat, core, order, devices):
    for bit in reversed(order):
        other = swap(shard, bit, devices)
        own = device_bit(flat, bit)
        shard = jnp.where(
            own == 0, jnp.concatenate([shard, other], axis=0), jnp.concatenate([other, shard], axis=0)
        )
    return shard, swap(shard, core, devices)


def permutation(width):
    size = 8 * 2 * width
    matrix = np.zeros((size, size), np.float32)
    place = 0
    for row_parity in range(2):
        for col_parity in range(2):
            for i in range(4):
                for j in range(width):
                    matrix[place, (2 * i + row_parity) * 2 * width + 2 * j + col_parity] = 1.0
                    place += 1
    return matrix


def param_tiles(gain, shift):
    blocks = gain.shape[0] // TILE
    pair = jnp.stack([gain.reshape(blocks, ROWS, LANES), shift.reshape(blocks, ROWS, LANES)], axis=1)
    return pair.reshape(blocks * 8, LANES)


def vector(tiles, first, step):
    return tiles.reshape(-1, step, LANES)[:, first : first + ROWS].reshape(-1)


def on_device(dp, rep, *arrays):
    (image_input, heights, widths, w_reduce, w_spatial, w_expand, w_shortcut,
     gain_reduce, shift_reduce, gain_spatial, shift_spatial, gain_expand, shift_expand,
     gain_shortcut, shift_shortcut, w_squeeze, w_window, w_widen,
     gain_squeeze, shift_squeeze, gain_window, shift_window, gain_widen, shift_widen, cotangent) = arrays
    images, height, width, c_out = cotangent.shape
    c_in, mid = w_reduce.shape
    pixels = images * height * width
    quarter = 64
    steps = pixels // quarter
    blocks = c_out // TILE
    devices = dp * rep
    core_bit, x_bits, y_bits, z_bits = mesh_bits(dp, rep)
    hop_bits = [core_bit] + y_bits + x_bits + z_bits
    flat = lax.axis_index(AXES)
    core = device_bit(flat, core_bit).astype(jnp.int32).reshape(1)
    sync = functools.partial(sync_all, devices=devices)
    sync_wide = functools.partial(sync_hops, bits=hop_bits, devices=devices)

    row_ids = lax.broadcasted_iota(jnp.int32, (1, height, 1, LANES), 1)
    col_ids = lax.broadcasted_iota(jnp.int32, (1, 1, width, LANES), 2)
    inside = (row_ids < heights[:, None, None, None]) & (col_ids < widths[:, None, None, None])
    mask = jnp.where(inside, 1.0, 0.0).astype(F32).reshape(pixels, LANES)
    params = jnp.concatenate(
        [
            param_tiles(gain_reduce, shift_reduce), param_tiles(gain_spatial, shift_spatial),
            param_tiles(gain_squeeze, shift_squeeze), param_tiles(gain_window, shift_window),
            param_tiles(gain_expand, shift_expand), param_tiles(gain_shortcut, shift_shortcut),
            param_tiles(gain_widen, shift_widen),
        ],
        axis=0,
    )
    p_reduce, p_spatial, p_squeeze, p_window = (tile_at(k) for k in range(4))
    p_expand, p_short, p_widen = (tile_n(4 + blocks * k) for k in range(3))
    turn = permutation(width)
    perm, perm_back = jnp.asarray(turn, BF16), jnp.asarray(turn.T.copy(), BF16)
    image = image_input.reshape(images * 4 * height * width, c_in)
    cot = cotangent.reshape(pixels, c_out)

    mask_spec, wide_f32 = full((pixels, LANES)), shaped((pixels, c_out))
    mid_f32, mid_spec = shaped((pixels, mid)), full((pixels, mid))
    wide_spec, tap_spec = cols(pixels, TILE), pl.BlockSpec((1, 3, mid, mid), lambda r: (r, 0, 0, 0))
    plane_block = lambda c: pl.BlockSpec((4, quarter, c), lambda k: (0, k, 0))
    one_tile, wide_tiles = shaped((8, LANES)), shaped((8 * blocks, LANES))
    padded = (3, images, (height + 2) * width, mid)

    planes, pre_reduce, stat = call(
        functools.partial(reduce_kernel, quarter),
        (steps,),
        [
            pl.BlockSpec((4 * quarter, c_in), lambda k: (k, 0)), full(perm.shape),
            pl.BlockSpec((quarter, LANES), lambda k: (k, 0)), mask_spec, full((c_in, mid)),
        ],
        [plane_block(c_in), plane_block(mid), full((16, LANES))],
        [shaped((4, pixels, c_in), BF16), shaped((4, pixels, mid)), shaped((16, LANES))],
        [pltpu.VMEM((8, mid), F32)],
        flops=8 * pixels * c_in * mid, nbytes=8 << 20,
    )(image, perm, mask, mask, w_reduce)
    s_reduce = sync(stat)
    count_spec = tile_at(1)

    pre_short, stat_short = call(
        product_kernel,
        (blocks,),
        [pl.BlockSpec((1, pixels, c_in), lambda n: (0, 0, 0)), cols(c_in, TILE)],
        [wide_spec, tile_n()],
        [wide_f32, wide_tiles],
        flops=2 * pixels * c_in * c_out, nbytes=6 << 20,
    )(planes, w_shortcut)

    act_reduce, pre_spatial, stat = call(
        functools.partial(spatial_kernel, width, height),
        (3,),
        [full((4, pixels, mid)), tile_at(0), count_spec, p_reduce, mask_spec, tap_spec],
        [full((4, pixels, mid)), mid_spec, full((8, LANES))],
        [shaped((4, pixels, mid), BF16), mid_f32, one_tile],
        [pltpu.VMEM((4, pixels, mid), F32)],
        flops=18 * pixels * mid * mid, nbytes=8 << 20,
    )(pre_reduce, s_reduce, s_reduce, params, mask, w_spatial)
    s_spatial = sync(stat)

    def widen_out(pre, stat, p_spec, weights):
        return call(
            expand_kernel,
            (blocks,),
            [mid_spec, tile_at(0), count_spec, p_spec, mask_spec, cols(mid, TILE)],
            [mid_spec, wide_spec, tile_n()],
            [shaped((pixels, mid), BF16), wide_f32, wide_tiles],
            flops=2 * pixels * mid * c_out, nbytes=5 << 20,
        )(pre, stat, s_reduce, params, mask, weights)

    act_spatial, pre_expand, stat = widen_out(pre_spatial, s_spatial, p_spatial, w_expand)
    s_both = sync_wide(jnp.concatenate([stat, stat_short], axis=0))
    e_spec, s_spec = tile_n(), tile_n(blocks)

    first_out, pre_squeeze, stat = call(
        join_kernel,
        (blocks,),
        [
            wide_spec, wide_spec, e_spec, s_spec, count_spec, p_expand, p_short, mask_spec,
            pl.BlockSpec((TILE, mid), lambda n: (n, 0)),
        ],
        [wide_spec, mid_spec, full((8, LANES))],
        [shaped((pixels, c_out), BF16), mid_f32, one_tile],
        flops=2 * pixels * mid * c_out, nbytes=8 << 20,
    )(pre_expand, pre_short, s_both, s_both, s_reduce, params, params, mask, w_squeeze)
    s_squeeze = sync(stat)

    act_squeeze, pre_window, stat = call(
        functools.partial(window_kernel, width, height, images),
        (3,),
        [mid_spec, tile_at(0), count_spec, p_squeeze, mask_spec, tap_spec],
        [mid_spec, mid_spec, full((8, LANES))],
        [shaped((pixels, mid), BF16), mid_f32, one_tile],
        [pltpu.VMEM(padded, BF16)],
        flops=18 * pixels * mid * mid, nbytes=6 << 20,
    )(pre_squeeze, s_squeeze, s_reduce, params, mask, w_window)
    s_window = sync(stat)

    act_window, pre_widen, stat = widen_out(pre_window, s_window, p_window, w_widen)
    s_widen = sync_wide(stat)

    block_out, grad_final, gsum = call(
        final_kernel,
        (blocks,),
        [wide_spec, tile_n(), count_spec, p_widen, mask_spec, wide_spec, wide_spec],
        [wide_spec, wide_spec, tile_n()],
        [shaped((pixels, c_out), BF16), wide_f32, wide_tiles],
        nbytes=7 << 20,
    )(pre_widen, s_widen, s_reduce, params, mask, first_out, cot)
    g_widen = sync_wide(gsum)

    gpre_widen, grad_window, gsum = call(
        widen_back_kernel,
        (blocks,),
        [
            wide_spec, wide_spec, tile_n(), tile_n(), count_spec, p_widen, mask_spec, cols(mid, TILE),
            mid_spec, tile_at(0), p_window,
        ],
        [wide_spec, mid_spec, full((8, LANES))],
        [shaped((pixels, c_out), BF16), mid_f32, one_tile],
        flops=2 * pixels * mid * c_out, nbytes=8 << 20,
    )(grad_final, pre_widen, s_widen, g_widen, s_reduce, params, mask, w_widen, pre_window, s_window, params)
    g_window = sync(gsum)

    gpad_window, grad_squeeze, gsum = call(
        functools.partial(window_back_kernel, width, height, images),
        (3,),
        [
            mid_spec, mid_spec, tile_at(0), tile_at(0), count_spec, p_window, mask_spec, tap_spec,
            mid_spec, tile_at(0), p_squeeze,
        ],
        [full(padded), mid_spec, full((8, LANES))],
        [shaped(padded, BF16), mid_f32, one_tile],
        flops=18 * pixels * mid * mid, nbytes=8 << 20,
    )(grad_window, pre_window, s_window, g_window, s_reduce, params, mask, w_window, pre_squeeze, s_squeeze, params)
    g_squeeze = sync(gsum)

    gpre_squeeze, grad_joined, gsum = call(
        squeeze_back_kernel,
        (blocks,),
        [
            mid_spec, mid_spec, tile_at(0), tile_at(0), count_spec, p_squeeze, mask_spec,
            pl.BlockSpec((TILE, mid), lambda n: (n, 0)),
            wide_spec, wide_spec, wide_spec, e_spec, s_spec, p_expand, p_short,
        ],
        [mid_spec, wide_spec, tile_n(rows=16)],
        [shaped((pixels, mid), BF16), wide_f32, shaped((16 * blocks, LANES))],
        flops=2 * pixels * mid * c_out, nbytes=11 << 20,
    )(
        grad_squeeze, pre_squeeze, s_squeeze, g_squeeze, s_reduce, params, mask, w_squeeze,
        grad_final, pre_expand, pre_short, s_both, s_both, params, params,
    )
    g_both = sync_wide(gsum)

    gpre_expand, gpre_short, grad_spatial, gsum = call(
        expand_back_kernel,
        (blocks,),
        [
            wide_spec, wide_spec, wide_spec, e_spec, s_spec, tile_n(rows=16), count_spec, p_expand, p_short,
            mask_spec, cols(mid, TILE), mid_spec, tile_at(0), p_spatial,
        ],
        [wide_spec, wide_spec, mid_spec, full((8, LANES))],
        [shaped((pixels, c_out), BF16), shaped((pixels, c_out), BF16), mid_f32, one_tile],
        flops=2 * pixels * mid * c_out, nbytes=11 << 20,
    )(
        grad_joined, pre_expand, pre_short, s_both, s_both, g_both, s_reduce, params, params, mask, w_expand,
        pre_spatial, s_spatial, params,
    )
    g_spatial = sync(gsum)

    gshift_spatial, grad_reduce, gsum = call(
        functools.partial(spatial_back_kernel, width, height),
        (3,),
        [
            mid_spec, mid_spec, tile_at(0), tile_at(0), count_spec, p_spatial, mask_spec, tap_spec,
            full((4, pixels, mid)), tile_at(0), p_reduce,
        ],
        [full((4, pixels, mid)), full((4, pixels, mid)), full((8, LANES))],
        [shaped((4, pixels, mid), BF16), shaped((4, pixels, mid)), one_tile],
        flops=18 * pixels * mid * mid, nbytes=12 << 20,
    )(grad_spatial, pre_spatial, s_spatial, g_spatial, s_reduce, params, mask, w_spatial, pre_reduce, s_reduce, params)
    g_reduce = sync(gsum)

    back_short = call(
        short_back_kernel,
        (blocks,),
        [wide_spec, cols(c_in, TILE)],
        full((pixels, c_in)),
        shaped((pixels, c_in)),
        flops=2 * pixels * c_in * c_out, nbytes=6 << 20,
    )(gpre_short, w_shortcut)

    gpre_reduce, image_grad = call(
        functools.partial(reduce_back_kernel, quarter),
        (steps,),
        [
            plane_block(mid), plane_block(mid), tile_at(0), tile_at(0), count_spec, p_reduce,
            pl.BlockSpec((quarter, LANES), lambda k: (k, 0)), full((c_in, mid)),
            pl.BlockSpec((quarter, c_in), lambda k: (k, 0)), full(perm.shape),
        ],
        [plane_block(mid), pl.BlockSpec((4 * quarter, c_in), lambda k: (k, 0))],
        [shaped((4, pixels, mid), BF16), shaped((images * 4 * height * width, c_in), BF16)],
        flops=8 * pixels * c_in * mid, nbytes=10 << 20,
    )(grad_reduce, pre_reduce, s_reduce, g_reduce, s_reduce, params, mask, w_reduce, back_short, perm_back)

    area = width * height

    def whole(ref, b):
        return ref[...]

    def window_taps(ref, b):
        r, c = lax.div(b, 3), lax.rem(b, 3)
        first = pl.multiple_of((2 - r) * width, width)
        return window_rows(ref, c, first, area, images)

    def spatial_taps(ref, b):
        r, c = lax.div(b, 3), lax.rem(b, 3)
        return ref[2 * jnp.where(r == 0, 1, 0) + jnp.where(c == 0, 1, 0)]

    def spatial_plane(b, *_):
        r, c = lax.div(b, 3), lax.rem(b, 3)
        return (2 * jnp.where(r == 1, 0, 1) + jnp.where(c == 1, 0, 1), 0, 0)

    in_blocks = c_in // TILE
    left_const = pl.BlockSpec((pixels, TILE), lambda b, *_: (0, 0))
    right_n = pl.BlockSpec((pixels, TILE), lambda b, *_: (0, b))
    made = outer(core, act_squeeze, left_const, gpad_window, full(padded), window_taps, 9, 9, 0, 9 + in_blocks * blocks, None)
    one = outer(
        core, planes.reshape(4 * pixels, c_in), pl.BlockSpec((pixels, TILE), lambda b, *_: (0, lax.div(b, blocks))),
        gpre_short, pl.BlockSpec((pixels, TILE), lambda b, *_: (0, lax.rem(b, blocks))),
        whole, in_blocks * blocks, blocks, 9, 9 + in_blocks * blocks, made,
    )
    made = outer(core, act_window, left_const, gpre_widen, right_n, whole, blocks, blocks, 0, 9 + blocks + in_blocks, None)
    made = outer(
        core, act_reduce, pl.BlockSpec((1, pixels, mid), spatial_plane), gshift_spatial, full((4, pixels, mid)),
        spatial_taps, 9, 1, blocks, 9 + blocks + in_blocks, made,
    )
    two = outer(
        core, planes.reshape(4 * pixels, c_in), pl.BlockSpec((4 * pixels, TILE), lambda b, *_: (0, b)),
        gpre_reduce.reshape(4 * pixels, mid), full((4 * pixels, mid)), whole, in_blocks, 1,
        9 + blocks, 9 + blocks + in_blocks, made,
    )
    made = outer(core, first_out, right_n, gpre_squeeze, full((pixels, mid)), whole, blocks, 1, 0, 2 * blocks, None)
    three = outer(core, act_spatial, left_const, gpre_expand, right_n, whole, blocks, blocks, blocks, 2 * blocks, made)

    order_one = x_bits + y_bits + z_bits
    order_two = y_bits + z_bits[:1] + x_bits + z_bits[1:]
    order_three = z_bits[:1] + x_bits + y_bits + z_bits[1:]
    orders = (order_one, order_two, order_three)
    shards = [
        scatter_sum(keep, send, flat, core_bit, order, devices)
        for (keep, send), order in zip((one, two, three), orders)
    ]
    halves = [gather_back(shard, flat, core_bit, order, devices) for shard, order in zip(shards, orders)]
    tall, flat_cols = lambda b: (b, 0), lambda b: (0, b)
    grad_w_window = assemble(core, *halves[0], 0, 9, (9 * mid, mid), tall).reshape(3, 3, mid, mid)
    grad_w_short = assemble(
        core, *halves[0], 9, in_blocks * blocks, (c_in, c_out), lambda b: (lax.div(b, blocks), lax.rem(b, blocks))
    )
    grad_w_widen = assemble(core, *halves[1], 0, blocks, (mid, c_out), flat_cols)
    grad_w_spatial = assemble(core, *halves[1], blocks, 9, (9 * mid, mid), tall).reshape(3, 3, mid, mid)
    grad_w_reduce = assemble(core, *halves[1], 9 + blocks, in_blocks, (c_in, mid), tall)
    grad_w_squeeze = assemble(core, *halves[2], 0, blocks, (c_out, mid), tall)
    grad_w_expand = assemble(core, *halves[2], blocks, blocks, (mid, c_out), flat_cols)

    shift_total = vector(g_both, 0, 16)
    return (
        block_out.reshape(cotangent.shape),
        image_grad.reshape(image_input.shape),
        grad_w_reduce,
        grad_w_spatial,
        grad_w_expand,
        grad_w_short,
        vector(g_reduce, ROWS, 8),
        vector(g_reduce, 0, 8),
        vector(g_spatial, ROWS, 8),
        vector(g_spatial, 0, 8),
        vector(g_both, ROWS, 16),
        shift_total,
        vector(g_both, 2 * ROWS, 16),
        shift_total,
        grad_w_squeeze,
        grad_w_window,
        grad_w_widen,
        vector(g_squeeze, ROWS, 8),
        vector(g_squeeze, 0, 8),
        vector(g_window, ROWS, 8),
        vector(g_window, 0, 8),
        vector(g_widen, ROWS, 8),
        vector(g_widen, 0, 8),
    )


def solution(mesh):
    split = P(AXES, None, None, None)
    return jax.shard_map(
        functools.partial(on_device, mesh.shape["dp"], mesh.shape["rep"]),
        mesh=mesh,
        in_specs=(split, P(AXES), P(AXES)) + (P(),) * 21 + (split,),
        out_specs=(split, split) + (P(),) * 21,
        check_vma=False,
    )
```

```python
import functools

import jax
import jax.numpy as jnp
import numpy as np
from jax import lax
from jax.experimental import pallas as pl
from jax.experimental.pallas import tpu as pltpu
from jax.sharding import PartitionSpec as P

EPSILON = 1e-05
F32 = jnp.float32
BF16 = jnp.bfloat16
AXES = ("dp", "rep")
LANES = 128
TILE = 512
ROWS = TILE // LANES
MIB = 60
SCHEDULE = (
    7, 2, 3, 1, 0, 4, 5, 6, 7, 4, 2, 6, 3, 5, 7, 0, 1, 3, 2, 4, 3, 6, 2, 5, 3, 0, 2, 1, 0, 5,
    1, 4, 0, 6, 5, 4, 1, 6, 5, 5, 4, 4, 6, 6, 5, 4, 6, 5, 4, 6, 5, 4, 6, 6, 5, 4,
)
FIRST = 5


def dot(left, right):
    return jnp.dot(left, right, preferred_element_type=F32)


def dot_nt(left, right):
    return lax.dot_general(left, right, (((1,), (1,)), ((), ())), preferred_element_type=F32)


def pack(vector):
    return jnp.concatenate(
        [vector[:, LANES * k : LANES * (k + 1)] for k in range(vector.shape[1] // LANES)], axis=0
    )


def unpack(rows):
    return jnp.concatenate([rows[k : k + 1, :] for k in range(rows.shape[0])], axis=1)


def col_sum(values):
    return jnp.sum(values, axis=0, keepdims=True)


def stat_tile(first, second):
    return jnp.concatenate([pack(col_sum(first)), pack(col_sum(second))], axis=0)


def put(ref, tile):
    ref[...] = jnp.broadcast_to(tile, ref.shape)


def total(ref):
    return ref[...] if len(ref.shape) == 2 else jnp.sum(ref[...], axis=0)


def coefficients(stat_ref, count_ref, param_ref, factor=1.0):
    stat, param = total(stat_ref), param_ref[...]
    count = total(count_ref)[0:ROWS, :] * factor
    average = stat[0:ROWS] / count
    inverse = lax.rsqrt(stat[ROWS : 2 * ROWS] / count - average * average + EPSILON)
    return (
        unpack(average),
        unpack(inverse),
        unpack(param[0:ROWS]),
        unpack(param[ROWS : 2 * ROWS]),
    )


def back_coefficients(grad_rows_shift, grad_rows_gain, count_ref, factor=1.0):
    count = total(count_ref)[0:ROWS, :] * factor
    return unpack(grad_rows_shift / count), unpack(grad_rows_gain / count)


def logistic(values):
    return 0.5 * jnp.tanh(0.5 * values) + 0.5


def silu(values):
    return values * logistic(values)


def slope(values):
    gate = logistic(values)
    return gate * (1.0 + values * (1.0 - gate))


def column(mask_ref):
    return mask_ref[:, 0:1]


def pixel_ids(pixels, width):
    return lax.broadcasted_iota(jnp.int32, (pixels, 1), 0)


def shift_cols(values, step, width):
    pixels = values.shape[0]
    place = lax.rem(pixel_ids(pixels, width), width)
    rolled = pltpu.roll(values, (-step) % pixels, 0)
    keep = place < width - step if step > 0 else place >= -step
    return jnp.where(keep, rolled, 0.0)


def shift_rows(values, step, width, height):
    pixels = values.shape[0]
    place = lax.rem(lax.div(pixel_ids(pixels, width), width), height)
    rolled = pltpu.roll(values, (-step * width) % pixels, 0)
    keep = place < height - step if step > 0 else place >= -step
    return jnp.where(keep, rolled, 0.0)


def full(shape):
    zeros = (0,) * len(shape)
    return pl.BlockSpec(shape, lambda *_: zeros)


def cols(rows, width):
    return pl.BlockSpec((rows, width), lambda n, *_: (0, n))


def tile_at(index, rows=8):
    return pl.BlockSpec((rows, LANES), lambda *_: (index, 0))


def tile_n(offset=0, rows=8):
    return pl.BlockSpec((rows, LANES), lambda n, *_: (offset + n, 0))


def call(kernel, grid, in_specs, out_specs, out_shape, scratch=(), mib=MIB, flops=0, nbytes=0):
    return pl.pallas_call(
        kernel,
        grid=grid,
        in_specs=in_specs,
        out_specs=out_specs,
        out_shape=out_shape,
        scratch_shapes=scratch,
        compiler_params=pltpu.CompilerParams(
            vmem_limit_bytes=mib << 20, dimension_semantics=("arbitrary",) * len(grid)
        ),
        cost_estimate=pl.CostEstimate(flops=flops, bytes_accessed=nbytes, transcendentals=0),
    )


def shaped(shape, dtype=F32):
    return jax.ShapeDtypeStruct(shape, dtype)


def reduce_kernel(quarter, x_ref, perm_ref, mask_ref, all_mask_ref, w_ref, xp_ref, pre_ref, stat_ref, acc_ref):
    step = pl.program_id(0)
    mask = column(mask_ref)
    masking = jnp.concatenate([mask] * 4, axis=0)
    planes = (dot(perm_ref[...], x_ref[...]) * masking).astype(BF16)
    pre = dot(planes, w_ref[...])
    for q in range(4):
        xp_ref[q] = planes[q * quarter : (q + 1) * quarter]
        pre_ref[q] = pre[q * quarter : (q + 1) * quarter]

    @pl.when(step == 0)
    def _():
        acc_ref[...] = jnp.zeros_like(acc_ref)

    acc_ref[0:1, :] += col_sum(pre)
    acc_ref[1:2, :] += col_sum(pre * pre)

    @pl.when(step == pl.num_programs(0) - 1)
    def _():
        count = jnp.broadcast_to(col_sum(all_mask_ref[...]), (8, LANES))
        put(stat_ref, jnp.concatenate([pack(acc_ref[0:1, :]), pack(acc_ref[1:2, :]), count], axis=0))


def product_kernel(x_ref, w_ref, out_ref, stat_ref):
    pre = dot(x_ref[0], w_ref[...])
    out_ref[...] = pre
    stat_ref[...] = stat_tile(pre, pre * pre)


def spatial_kernel(width, height, pre_ref, stat_ref, count_ref, param_ref, mask_ref, w_ref, act_ref, out_ref, out_stat_ref, y_ref):
    r = pl.program_id(0)
    mask = column(mask_ref)

    @pl.when(r == 0)
    def _():
        average, inverse, gain, shift = coefficients(stat_ref, count_ref, param_ref, 4.0)
        for q in range(4):
            norm = (pre_ref[q] - average) * inverse * gain + shift
            act_ref[q] = (silu(norm) * mask).astype(BF16)

    row_parity = jnp.where(r == 1, 0, 1)
    row_shift = jnp.where(r == 0, 1, 0)
    even, odd = act_ref[2 * row_parity], act_ref[2 * row_parity + 1]
    straight = dot(even, w_ref[0, 1]) + dot(odd, w_ref[0, 2])
    moved = dot(odd, w_ref[0, 0])

    @pl.when(r < 2)
    def _():
        y_ref[2 * row_shift] = straight
        y_ref[2 * row_shift + 1] = moved

    @pl.when(r == 2)
    def _():
        upper = y_ref[2] + shift_cols(y_ref[3], -1, width)
        lower = y_ref[0] + straight + shift_cols(y_ref[1] + moved, -1, width)
        pre = lower + shift_rows(upper, -1, width, height)
        out_ref[...] = pre
        masked = pre * mask
        put(out_stat_ref, stat_tile(masked, masked * pre))


def expand_kernel(pre_ref, stat_ref, count_ref, param_ref, mask_ref, w_ref, act_ref, out_ref, out_stat_ref):
    @pl.when(pl.program_id(0) == 0)
    def _():
        average, inverse, gain, shift = coefficients(stat_ref, count_ref, param_ref)
        norm = (pre_ref[...] - average) * inverse * gain + shift
        act_ref[...] = (silu(norm) * column(mask_ref)).astype(BF16)

    pre = dot(act_ref[...], w_ref[...])
    out_ref[...] = pre
    put(out_stat_ref, stat_tile(pre, pre * pre))


def join_kernel(pe_ref, ps_ref, se_ref, ss_ref, count_ref, qe_ref, qs_ref, mask_ref, w_ref, first_ref, out_ref, out_stat_ref):
    n = pl.program_id(0)
    average_e, inverse_e, gain_e, shift_e = coefficients(se_ref, count_ref, qe_ref)
    average_s, inverse_s, gain_s, shift_s = coefficients(ss_ref, count_ref, qs_ref)
    joined = (pe_ref[...] - average_e) * inverse_e * gain_e + shift_e
    joined += (ps_ref[...] - average_s) * inverse_s * gain_s + shift_s
    first = (silu(joined) * column(mask_ref)).astype(BF16)
    first_ref[...] = first
    part = dot(first, w_ref[...])

    @pl.when(n == 0)
    def _():
        out_ref[...] = part

    @pl.when(n > 0)
    def _():
        out_ref[...] += part

    @pl.when(n == pl.num_programs(0) - 1)
    def _():
        pre = out_ref[...]
        put(out_stat_ref, stat_tile(pre, pre * pre))


def store_padded(target_ref, values, step, width, height, images):
    area = width * height
    channels = values.shape[1]
    zeros = jnp.zeros((width, channels), BF16)
    for k in range(3):
        moved = values if k == 1 else shift_cols(values, step * (k - 1), width)
        moved = moved.astype(BF16)
        for b in range(images):
            target_ref[k, b, 0:width, :] = zeros
            target_ref[k, b, area + width : area + 2 * width, :] = zeros
            target_ref[k, b, width : area + width, :] = moved[b * area : (b + 1) * area]


def window_rows(ref, k, first, area, images):
    return jnp.concatenate([ref[k, b, pl.ds(first, area), :] for b in range(images)], axis=0)


def window_kernel(width, height, images, pre_ref, stat_ref, count_ref, param_ref, mask_ref, w_ref, act_ref, out_ref, out_stat_ref, pad_ref):
    r = pl.program_id(0)

    @pl.when(r == 0)
    def _():
        average, inverse, gain, shift = coefficients(stat_ref, count_ref, param_ref)
        norm = (pre_ref[...] - average) * inverse * gain + shift
        act = silu(norm) * column(mask_ref)
        act_ref[...] = act.astype(BF16)
        store_padded(pad_ref, act, 1, width, height, images)

    first = pl.multiple_of(r * width, width)
    part = dot(window_rows(pad_ref, 0, first, width * height, images), w_ref[0, 0])
    for k in (1, 2):
        part += dot(window_rows(pad_ref, k, first, width * height, images), w_ref[0, k])

    @pl.when(r == 0)
    def _():
        out_ref[...] = part

    @pl.when(r > 0)
    def _():
        out_ref[...] += part

    @pl.when(r == 2)
    def _():
        pre = out_ref[...]
        masked = pre * column(mask_ref)
        put(out_stat_ref, stat_tile(masked, masked * pre))


def final_kernel(pre_ref, stat_ref, count_ref, param_ref, mask_ref, first_ref, cot_ref, out_ref, grad_ref, sum_ref):
    average, inverse, gain, shift = coefficients(stat_ref, count_ref, param_ref)
    mask = column(mask_ref)
    hat = (pre_ref[...] - average) * inverse
    final = hat * gain + shift + first_ref[...].astype(F32)
    gate = logistic(final)
    out_ref[...] = (final * gate * mask).astype(BF16)
    grad = cot_ref[...].astype(F32) * mask * (gate * (1.0 + final * (1.0 - gate)))
    grad_ref[...] = grad
    put(sum_ref, stat_tile(grad, grad * hat))


def norm_back(grad, hat, scale, shift_term, gain_term, mask):
    return ((grad - mask * (shift_term + hat * gain_term)) * scale).astype(BF16)


def widen_back_kernel(
    grad_ref, pre_ref, stat_ref, gsum_ref, count_ref, param_ref, mask_ref, w_ref, in_ref, in_stat_ref, in_param_ref,
    gpre_ref, out_ref, sum_ref,
):
    n = pl.program_id(0)
    mask = column(mask_ref)
    average, inverse, gain, _ = coefficients(stat_ref, count_ref, param_ref)
    gsum = total(gsum_ref)
    shift_term, gain_term = back_coefficients(gsum[0:ROWS], gsum[ROWS : 2 * ROWS], count_ref)
    hat = (pre_ref[...] - average) * inverse
    gpre = norm_back(grad_ref[...], hat, inverse * gain, shift_term, gain_term, mask)
    gpre_ref[...] = gpre
    part = dot_nt(gpre, w_ref[...])

    @pl.when(n == 0)
    def _():
        out_ref[...] = part

    @pl.when(n > 0)
    def _():
        out_ref[...] += part

    @pl.when(n == pl.num_programs(0) - 1)
    def _():
        finish_back(in_ref[...], in_stat_ref, count_ref, in_param_ref, mask, out_ref, sum_ref)


def finish_back(pre, stat_ref, count_ref, param_ref, mask, out_ref, sum_ref):
    average, inverse, gain, shift = coefficients(stat_ref, count_ref, param_ref)
    hat = (pre - average) * inverse
    grad = out_ref[...] * mask * slope(hat * gain + shift)
    out_ref[...] = grad
    put(sum_ref, stat_tile(grad, grad * hat))


def pre_grad(grad_ref, pre_ref, stat_ref, gsum_ref, count_ref, param_ref, mask):
    average, inverse, gain, _ = coefficients(stat_ref, count_ref, param_ref)
    gsum = total(gsum_ref)
    shift_term, gain_term = back_coefficients(gsum[0:ROWS], gsum[ROWS : 2 * ROWS], count_ref)
    hat = (pre_ref[...] - average) * inverse
    return norm_back(grad_ref[...], hat, inverse * gain, shift_term, gain_term, mask)


def window_back_kernel(
    width, height, images,
    grad_ref, pre_ref, stat_ref, gsum_ref, count_ref, param_ref, mask_ref, w_ref, in_ref, in_stat_ref, in_param_ref,
    pad_ref, out_ref, sum_ref,
):
    r = pl.program_id(0)
    mask = column(mask_ref)

    @pl.when(r == 0)
    def _():
        gpre = pre_grad(grad_ref, pre_ref, stat_ref, gsum_ref, count_ref, param_ref, mask)
        store_padded(pad_ref, gpre.astype(F32), -1, width, height, images)

    first = pl.multiple_of((2 - r) * width, width)
    part = dot_nt(window_rows(pad_ref, 0, first, width * height, images), w_ref[0, 0])
    for k in (1, 2):
        part += dot_nt(window_rows(pad_ref, k, first, width * height, images), w_ref[0, k])

    @pl.when(r == 0)
    def _():
        out_ref[...] = part

    @pl.when(r > 0)
    def _():
        out_ref[...] += part

    @pl.when(r == 2)
    def _():
        finish_back(in_ref[...], in_stat_ref, count_ref, in_param_ref, mask, out_ref, sum_ref)


def squeeze_back_kernel(
    grad_ref, pre_ref, stat_ref, gsum_ref, count_ref, param_ref, mask_ref, w_ref,
    gfinal_ref, pe_ref, ps_ref, se_ref, ss_ref, qe_ref, qs_ref,
    gpre_ref, gj_ref, sum_ref,
):
    mask = column(mask_ref)

    @pl.when(pl.program_id(0) == 0)
    def _():
        gpre_ref[...] = pre_grad(grad_ref, pre_ref, stat_ref, gsum_ref, count_ref, param_ref, mask)

    gfirst = gfinal_ref[...] + dot_nt(gpre_ref[...], w_ref[...])
    average_e, inverse_e, gain_e, shift_e = coefficients(se_ref, count_ref, qe_ref)
    average_s, inverse_s, gain_s, shift_s = coefficients(ss_ref, count_ref, qs_ref)
    hat_e = (pe_ref[...] - average_e) * inverse_e
    hat_s = (ps_ref[...] - average_s) * inverse_s
    joined = hat_e * gain_e + shift_e + (hat_s * gain_s + shift_s)
    grad = gfirst * mask * slope(joined)
    gj_ref[...] = grad
    sum_ref[...] = jnp.concatenate(
        [stat_tile(grad, grad * hat_e), pack(col_sum(grad * hat_s)), jnp.zeros((ROWS, LANES), F32)], axis=0
    )


def expand_back_kernel(
    gj_ref, pe_ref, ps_ref, se_ref, ss_ref, gsum_ref, count_ref, qe_ref, qs_ref, mask_ref, w_ref,
    in_ref, in_stat_ref, in_param_ref,
    ge_ref, gs_ref, out_ref, sum_ref,
):
    n = pl.program_id(0)
    mask = column(mask_ref)
    average_e, inverse_e, gain_e, _ = coefficients(se_ref, count_ref, qe_ref)
    average_s, inverse_s, gain_s, _ = coefficients(ss_ref, count_ref, qs_ref)
    gsum = total(gsum_ref)
    shift_term, gain_e_term = back_coefficients(gsum[0:ROWS], gsum[ROWS : 2 * ROWS], count_ref)
    _, gain_s_term = back_coefficients(gsum[0:ROWS], gsum[2 * ROWS : 3 * ROWS], count_ref)
    grad = gj_ref[...]
    hat_e = (pe_ref[...] - average_e) * inverse_e
    hat_s = (ps_ref[...] - average_s) * inverse_s
    ge = norm_back(grad, hat_e, inverse_e * gain_e, shift_term, gain_e_term, mask)
    ge_ref[...] = ge
    gs_ref[...] = norm_back(grad, hat_s, inverse_s * gain_s, shift_term, gain_s_term, mask)
    part = dot_nt(ge, w_ref[...])

    @pl.when(n == 0)
    def _():
        out_ref[...] = part

    @pl.when(n > 0)
    def _():
        out_ref[...] += part

    @pl.when(n == pl.num_programs(0) - 1)
    def _():
        finish_back(in_ref[...], in_stat_ref, count_ref, in_param_ref, mask, out_ref, sum_ref)


def spatial_back_kernel(
    width, height,
    grad_ref, pre_ref, stat_ref, gsum_ref, count_ref, param_ref, mask_ref, w_ref, in_ref, in_stat_ref, in_param_ref,
    shift_ref, out_ref, sum_ref,
):
    r = pl.program_id(0)
    mask = column(mask_ref)

    @pl.when(r == 0)
    def _():
        gpre = pre_grad(grad_ref, pre_ref, stat_ref, gsum_ref, count_ref, param_ref, mask).astype(F32)
        below = shift_rows(gpre, 1, width, height)
        shift_ref[0] = gpre.astype(BF16)
        shift_ref[1] = shift_cols(gpre, 1, width).astype(BF16)
        shift_ref[2] = below.astype(BF16)
        shift_ref[3] = shift_cols(below, 1, width).astype(BF16)

    row_parity = jnp.where(r == 1, 0, 1)
    row_shift = jnp.where(r == 0, 1, 0)
    straight, moved = shift_ref[2 * row_shift], shift_ref[2 * row_shift + 1]
    even = dot_nt(straight, w_ref[0, 1])
    odd = dot_nt(moved, w_ref[0, 0]) + dot_nt(straight, w_ref[0, 2])

    @pl.when(r < 2)
    def _():
        out_ref[2 * row_parity] = even
        out_ref[2 * row_parity + 1] = odd

    @pl.when(r == 2)
    def _():
        out_ref[2] += even
        out_ref[3] += odd
        average, inverse, gain, shift = coefficients(in_stat_ref, count_ref, in_param_ref, 4.0)
        whole_sum = whole_hat = jnp.zeros((1, out_ref.shape[2]), F32)
        for q in range(4):
            hat = (in_ref[q] - average) * inverse
            grad = out_ref[q] * mask * slope(hat * gain + shift)
            out_ref[q] = grad
            whole_sum += col_sum(grad)
            whole_hat += col_sum(grad * hat)
        put(sum_ref, jnp.concatenate([pack(whole_sum), pack(whole_hat)], axis=0))


def short_back_kernel(g_ref, w_ref, out_ref):
    part = dot_nt(g_ref[...], w_ref[...])

    @pl.when(pl.program_id(0) == 0)
    def _():
        out_ref[...] = part

    @pl.when(pl.program_id(0) > 0)
    def _():
        out_ref[...] += part


def reduce_back_kernel(
    quarter, grad_ref, pre_ref, stat_ref, gsum_ref, count_ref, param_ref, mask_ref, w_ref, short_ref, perm_ref,
    gpre_ref, out_ref,
):
    mask = column(mask_ref)
    masking = jnp.concatenate([mask] * 4, axis=0)
    average, inverse, gain, _ = coefficients(stat_ref, count_ref, param_ref, 4.0)
    gsum = total(gsum_ref)
    shift_term, gain_term = back_coefficients(gsum[0:ROWS], gsum[ROWS : 2 * ROWS], count_ref, 4.0)
    grad = jnp.concatenate([grad_ref[q] for q in range(4)], axis=0)
    pre = jnp.concatenate([pre_ref[q] for q in range(4)], axis=0)
    hat = (pre - average) * inverse
    gpre = norm_back(grad, hat, inverse * gain, shift_term, gain_term, masking)
    for q in range(4):
        gpre_ref[q] = gpre[q * quarter : (q + 1) * quarter]
    image = dot_nt(gpre, w_ref[...])
    image = jnp.concatenate([image[0:quarter] + short_ref[...], image[quarter:]], axis=0)
    image = (image * masking).astype(BF16)
    out_ref[...] = dot(perm_ref[...], image).astype(BF16)


def turn_left(left_ref, turned_ref, per_left):
    @pl.when(lax.rem(pl.program_id(0), per_left) == 0)
    def _():
        left = left_ref[...] if len(left_ref.shape) == 2 else left_ref[0]
        turned_ref[...] = left.T


def halves_kernel(pick, per_left, core_ref, left_ref, right_ref, keep_ref, send_ref, turned_ref):
    turn_left(left_ref, turned_ref, per_left)
    half = TILE // 2
    right = pick(right_ref, pl.program_id(0))
    mine = pl.multiple_of(core_ref[0] * half, half)
    away = pl.multiple_of((1 - core_ref[0]) * half, half)
    send_ref[0] = dot(turned_ref[pl.ds(away, half), :], right)
    keep_ref[0] = dot(turned_ref[pl.ds(mine, half), :], right)


def outer_halves(core, left, left_spec, right, right_spec, pick, blocks, per_left):
    half = TILE // 2
    pixels = left_spec.block_shape[-2]
    shape = shaped((blocks, half, TILE))
    out_spec = pl.BlockSpec((1, half, TILE), lambda b, *_: (b, 0, 0))
    return pl.pallas_call(
        functools.partial(halves_kernel, pick, per_left),
        grid_spec=pltpu.PrefetchScalarGridSpec(
            num_scalar_prefetch=1,
            grid=(blocks,),
            in_specs=[left_spec, right_spec],
            out_specs=[out_spec, out_spec],
            scratch_shapes=[pltpu.VMEM((TILE, pixels), BF16)],
        ),
        out_shape=[shape, shape],
        compiler_params=outer_params(),
        cost_estimate=outer_cost(blocks, pixels),
    )(core, left, right)


def outer_params():
    return pltpu.CompilerParams(vmem_limit_bytes=MIB << 20, dimension_semantics=("arbitrary",))


def outer_cost(blocks, pixels):
    return pl.CostEstimate(
        flops=2 * blocks * pixels * TILE * TILE, bytes_accessed=blocks * TILE * TILE * 4, transcendentals=0
    )


def spread_kernel(pick, per_left, left_ref, right_ref, *refs):
    out_ref, turned_ref = refs[-2], refs[-1]
    turn_left(left_ref, turned_ref, per_left)
    out_ref[...] = dot(turned_ref[...], pick(right_ref, pl.program_id(0))).reshape(out_ref.shape)


def outer_spread(shares, left, left_spec, right, right_spec, pick, blocks, per_left, place, total, into):
    rows = TILE // shares
    pixels = left_spec.block_shape[-2]
    extra = () if into is None else (into,)
    return pl.pallas_call(
        functools.partial(spread_kernel, pick, per_left),
        grid=(blocks,),
        in_specs=[left_spec, right_spec] + [pl.BlockSpec(memory_space=pl.ANY)] * len(extra),
        out_specs=pl.BlockSpec((shares, rows, TILE), lambda b: (0, place + b, 0)),
        out_shape=shaped((shares, total * rows, TILE)),
        scratch_shapes=[pltpu.VMEM((TILE, pixels), BF16)],
        input_output_aliases={2: 0} if extra else {},
        compiler_params=outer_params(),
        cost_estimate=outer_cost(blocks, pixels),
    )(left, right, *extra)


def assemble_kernel(chunks, place_ref, own_ref, near_ref, far_ref, both_ref, *refs):
    out_ref = refs[-1]
    rows = TILE // 4 // chunks
    for k, ref in enumerate((own_ref, near_ref, far_ref, both_ref)):
        for c in range(chunks):
            start = pl.multiple_of(place_ref[k * chunks + c], rows)
            out_ref[pl.ds(start, rows), :] = ref[0, c * rows : (c + 1) * rows, :]


def assemble(places, pieces, first, blocks, shape, where, chunks=1, into=None):
    in_spec = pl.BlockSpec((1, TILE // 4, TILE), lambda b, *_: (first + b, 0, 0))
    extra = () if into is None else (into,)
    return pl.pallas_call(
        functools.partial(assemble_kernel, chunks),
        grid_spec=pltpu.PrefetchScalarGridSpec(
            num_scalar_prefetch=1,
            grid=(blocks,),
            in_specs=[in_spec] * 4 + [pl.BlockSpec(memory_space=pl.ANY)] * len(extra),
            out_specs=pl.BlockSpec((TILE, TILE), lambda b, *_: where(b)),
        ),
        out_shape=shaped(shape),
        input_output_aliases={5: 0} if extra else {},
        compiler_params=outer_params(),
        cost_estimate=pl.CostEstimate(
            flops=0, bytes_accessed=2 * blocks * TILE * TILE * 4, transcendentals=0
        ),
    )(places, *pieces, *extra)


def regroup_kernel(starts, in_ref, *refs):
    out_ref, rows = refs[-1], in_ref.shape[1]
    for k, start in enumerate(starts):
        out_ref[start : start + rows, :] = in_ref[k]


def regroup(gathered, starts, total, place, blocks, shape, where, into=None):
    devices, rows = gathered.shape[0], gathered.shape[1] // total
    extra = () if into is None else (into,)
    if rows % 8:
        order = np.argsort(np.asarray(starts))
        gathered = gathered.reshape(devices, total, rows, TILE)[order].transpose(1, 0, 2, 3)
        gathered = gathered.reshape(1, total * TILE, TILE)
        devices, rows, starts = 1, TILE, (0,)
    return pl.pallas_call(
        functools.partial(regroup_kernel, starts),
        grid=(blocks,),
        in_specs=[pl.BlockSpec((devices, rows, TILE), lambda b: (0, place + b, 0))]
        + [pl.BlockSpec(memory_space=pl.ANY)] * len(extra),
        out_specs=pl.BlockSpec((TILE, TILE), where),
        out_shape=shaped(shape),
        input_output_aliases={1: 0} if extra else {},
        compiler_params=outer_params(),
        cost_estimate=pl.CostEstimate(
            flops=0, bytes_accessed=2 * blocks * TILE * TILE * 4, transcendentals=0
        ),
    )(gathered, *extra)


def bits_of(first, size):
    found = []
    while size > 1:
        found.append(first)
        first, size = first * 2, size // 2
    return found


def mesh_bits(dp, rep):
    side = int(round(dp**0.5))
    if side * side == dp:
        return 1, bits_of(rep, side), bits_of(rep * side, side), bits_of(2, rep // 2)
    side = int(round((dp // 2) ** 0.5))
    return rep, bits_of(2 * rep, side), bits_of(2 * rep * side, side), bits_of(1, rep)


def swap(values, bit, devices):
    return lax.ppermute(values, AXES, [(i, i ^ bit) for i in range(devices)])


def sync_all(tile, devices):
    return lax.all_to_all(tile, AXES, 0, 0, tiled=True)


def sync_hops(tile, bits, devices):
    for bit in bits:
        tile = tile + swap(tile, bit, devices)
    return tile


def device_bit(flat, bit):
    return lax.rem(lax.div(flat, bit), 2)


def after(values, *others):
    return lax.optimization_barrier((values,) + others)[0]


def half_sum(keep, received, which):
    rows = keep.shape[1] // 2
    first = lax.dynamic_slice_in_dim(keep, which * rows, rows, axis=1)
    return first + lax.dynamic_slice_in_dim(received, which * rows, rows, axis=1)


def join_halves(own, values, other):
    return jnp.where(
        own == 0, jnp.concatenate([values, other], axis=1), jnp.concatenate([other, values], axis=1)
    )


class Halving:
    def __init__(self, keep, order, flat, devices, send=None, core=None):
        self.keep, self.order, self.flat, self.devices = keep, list(order), flat, devices
        self.received = None
        self.moves = []
        if send is not None:
            self.moves.append(lambda token: self.cross(send, core, token))
        self.moves += [functools.partial(self.halve, bit) for bit in self.order] + [self.add]

    def cross(self, send, core, token):
        send = after(send, token)
        self.received = swap(send, core, self.devices)
        return send

    def halve(self, bit, token):
        own = device_bit(self.flat, bit)
        if self.received is None:
            keep, rows = after(self.keep, token), self.keep.shape[1] // 2
            send = lax.dynamic_slice_in_dim(keep, (1 - own) * rows, rows, axis=1)
            self.received = swap(send, bit, self.devices)
            self.keep = lax.dynamic_slice_in_dim(keep, own * rows, rows, axis=1)
            return send
        keep, received = after((self.keep, self.received), token)
        send = half_sum(keep, received, 1 - own)
        self.received = swap(send, bit, self.devices)
        keep, received = after((keep, received), send)
        self.keep = half_sum(keep, received, own)
        return send

    def add(self, token):
        keep, received = after((self.keep, self.received), token)
        self.keep = keep + received
        return self.keep


class Return:
    def __init__(self, source, core, flat, devices):
        self.source, self.core, self.flat, self.devices = source, core, flat, devices
        self.order = source.order
        back = list(reversed(self.order))
        self.moves = [functools.partial(self.widen, a, b) for a, b in zip([None] + back[:-1], back)]
        self.moves.append(self.cross)

    def widen(self, joined, bit, token):
        if joined is None:
            self.own = after(self.source.keep, token)
        else:
            own, other = after((self.own, self.near), token)
            self.own = join_halves(device_bit(self.flat, joined), own, other)
        self.near = swap(self.own, bit, self.devices)
        if bit == self.order[0]:
            self.far = swap(self.own, self.core, self.devices)
        return self.own

    def cross(self, token):
        self.near = after(self.near, token)
        self.both = swap(self.near, self.core, self.devices)
        return self.near

    def pieces(self):
        return self.own, self.near, self.far, self.both

    def places(self):
        half, quarter = TILE // 2, TILE // 4
        core, own = device_bit(self.flat, self.core), device_bit(self.flat, self.order[0])
        return jnp.stack(
            [c * half + o * quarter for c in (core, 1 - core) for o in (own, 1 - own)]
        ).astype(jnp.int32)


def run_streams(streams, schedule, token, to_end=True):
    for k in schedule:
        if streams[k].moves:
            token = streams[k].moves.pop(0)(token)
    while to_end and any(s.moves for s in streams):
        for s in streams:
            if s.moves:
                token = s.moves.pop(0)(token)
    return token


def permutation(width):
    size = 8 * 2 * width
    matrix = np.zeros((size, size), np.float32)
    place = 0
    for row_parity in range(2):
        for col_parity in range(2):
            for i in range(4):
                for j in range(width):
                    matrix[place, (2 * i + row_parity) * 2 * width + 2 * j + col_parity] = 1.0
                    place += 1
    return matrix


def param_tiles(gain, shift):
    blocks = gain.shape[0] // TILE
    pair = jnp.stack([gain.reshape(blocks, ROWS, LANES), shift.reshape(blocks, ROWS, LANES)], axis=1)
    return pair.reshape(blocks * 8, LANES)


def vector(tiles, first, step):
    return tiles.reshape(-1, step, LANES)[:, first : first + ROWS].reshape(-1)


def on_device(dp, rep, *arrays):
    (image_input, heights, widths, w_reduce, w_spatial, w_expand, w_shortcut,
     gain_reduce, shift_reduce, gain_spatial, shift_spatial, gain_expand, shift_expand,
     gain_shortcut, shift_shortcut, w_squeeze, w_window, w_widen,
     gain_squeeze, shift_squeeze, gain_window, shift_window, gain_widen, shift_widen, cotangent) = arrays
    images, height, width, c_out = cotangent.shape
    c_in, mid = w_reduce.shape
    pixels = images * height * width
    quarter = 64
    steps = pixels // quarter
    blocks = c_out // TILE
    devices = dp * rep
    core_bit, x_bits, y_bits, z_bits = mesh_bits(dp, rep)
    hop_bits = [core_bit] + y_bits + x_bits + z_bits
    xs, ys, zs, rep_bits = x_bits, y_bits, z_bits, bits_of(1, rep)
    flat = lax.axis_index(AXES)
    core = device_bit(flat, core_bit).astype(jnp.int32).reshape(1)
    sync = functools.partial(sync_all, devices=devices)
    sync_wide = functools.partial(sync_hops, bits=hop_bits, devices=devices)

    row_ids = lax.broadcasted_iota(jnp.int32, (1, height, 1, LANES), 1)
    col_ids = lax.broadcasted_iota(jnp.int32, (1, 1, width, LANES), 2)
    inside = (row_ids < heights[:, None, None, None]) & (col_ids < widths[:, None, None, None])
    mask = jnp.where(inside, 1.0, 0.0).astype(F32).reshape(pixels, LANES)
    params = jnp.concatenate(
        [
            param_tiles(gain_reduce, shift_reduce), param_tiles(gain_spatial, shift_spatial),
            param_tiles(gain_squeeze, shift_squeeze), param_tiles(gain_window, shift_window),
            param_tiles(gain_expand, shift_expand), param_tiles(gain_shortcut, shift_shortcut),
            param_tiles(gain_widen, shift_widen),
        ],
        axis=0,
    )
    p_reduce, p_spatial, p_squeeze, p_window = (tile_at(k) for k in range(4))
    p_expand, p_short, p_widen = (tile_n(4 + blocks * k) for k in range(3))
    turn = permutation(width)
    perm, perm_back = jnp.asarray(turn, BF16), jnp.asarray(turn.T.copy(), BF16)
    image = image_input.reshape(images * 4 * height * width, c_in)
    cot = cotangent.reshape(pixels, c_out)

    mask_spec, wide_f32 = full((pixels, LANES)), shaped((pixels, c_out))
    mid_f32, mid_spec = shaped((pixels, mid)), full((pixels, mid))
    wide_spec, tap_spec = cols(pixels, TILE), pl.BlockSpec((1, 3, mid, mid), lambda r: (r, 0, 0, 0))
    plane_block = lambda c: pl.BlockSpec((4, quarter, c), lambda k: (0, k, 0))
    area, in_blocks = width * height, c_in // TILE
    left_const = pl.BlockSpec((pixels, TILE), lambda b, *_: (0, 0))
    right_n = pl.BlockSpec((pixels, TILE), lambda b, *_: (0, b))

    def whole(ref, b):
        return ref[...]

    def window_taps(ref, b):
        r, c = lax.div(b, 3), lax.rem(b, 3)
        first = pl.multiple_of((2 - r) * width, width)
        return window_rows(ref, c, first, area, images)

    def spatial_taps(place, ref, b):
        r, c = lax.div(place + b, 3), lax.rem(place + b, 3)
        return ref[2 * jnp.where(r == 0, 1, 0) + jnp.where(c == 0, 1, 0)]

    def spatial_plane(place, b, *_):
        r, c = lax.div(place + b, 3), lax.rem(place + b, 3)
        return (2 * jnp.where(r == 1, 0, 1) + jnp.where(c == 1, 0, 1), 0, 0)

    one_tile, wide_tiles = shaped((devices, 8, LANES)), shaped((8 * blocks, LANES))
    all_tiles = full((devices, 8, LANES))
    count_spec = pl.BlockSpec((devices, 8, LANES), lambda *_: (0, 1, 0))
    padded = (3, images, (height + 2) * width, mid)

    planes, pre_reduce, stat = call(
        functools.partial(reduce_kernel, quarter),
        (steps,),
        [
            pl.BlockSpec((4 * quarter, c_in), lambda k: (k, 0)), full(perm.shape),
            pl.BlockSpec((quarter, LANES), lambda k: (k, 0)), mask_spec, full((c_in, mid)),
        ],
        [plane_block(c_in), plane_block(mid), full((devices, 16, LANES))],
        [shaped((4, pixels, c_in), BF16), shaped((4, pixels, mid)), shaped((devices, 16, LANES))],
        [pltpu.VMEM((8, mid), F32)],
        flops=8 * pixels * c_in * mid, nbytes=8 << 20,
    )(image, perm, mask, mask, w_reduce)
    s_reduce = sync(stat)

    pre_short, stat_short = call(
        product_kernel,
        (blocks,),
        [pl.BlockSpec((1, pixels, c_in), lambda n: (0, 0, 0)), cols(c_in, TILE)],
        [wide_spec, tile_n()],
        [wide_f32, wide_tiles],
        flops=2 * pixels * c_in * c_out, nbytes=6 << 20,
    )(planes, w_shortcut)

    act_reduce, pre_spatial, stat = call(
        functools.partial(spatial_kernel, width, height),
        (3,),
        [full((4, pixels, mid)), all_tiles, count_spec, p_reduce, mask_spec, tap_spec],
        [full((4, pixels, mid)), mid_spec, all_tiles],
        [shaped((4, pixels, mid), BF16), mid_f32, one_tile],
        [pltpu.VMEM((4, pixels, mid), F32)],
        flops=18 * pixels * mid * mid, nbytes=8 << 20,
    )(pre_reduce, s_reduce, s_reduce, params, mask, w_spatial)
    s_spatial = sync(stat)

    def widen_out(pre, stat, p_spec, weights):
        return call(
            expand_kernel,
            (blocks,),
            [mid_spec, all_tiles, count_spec, p_spec, mask_spec, cols(mid, TILE)],
            [mid_spec, wide_spec, tile_n()],
            [shaped((pixels, mid), BF16), wide_f32, wide_tiles],
            flops=2 * pixels * mid * c_out, nbytes=5 << 20,
        )(pre, stat, s_reduce, params, mask, weights)

    act_spatial, pre_expand, stat = widen_out(pre_spatial, s_spatial, p_spatial, w_expand)
    s_both = sync_wide(jnp.concatenate([stat, stat_short], axis=0))
    e_spec, s_spec = tile_n(), tile_n(blocks)

    first_out, pre_squeeze, stat = call(
        join_kernel,
        (blocks,),
        [
            wide_spec, wide_spec, e_spec, s_spec, count_spec, p_expand, p_short, mask_spec,
            pl.BlockSpec((TILE, mid), lambda n: (n, 0)),
        ],
        [wide_spec, mid_spec, all_tiles],
        [shaped((pixels, c_out), BF16), mid_f32, one_tile],
        flops=2 * pixels * mid * c_out, nbytes=8 << 20,
    )(pre_expand, pre_short, s_both, s_both, s_reduce, params, params, mask, w_squeeze)
    s_squeeze = sync(stat)

    act_squeeze, pre_window, stat = call(
        functools.partial(window_kernel, width, height, images),
        (3,),
        [mid_spec, all_tiles, count_spec, p_squeeze, mask_spec, tap_spec],
        [mid_spec, mid_spec, all_tiles],
        [shaped((pixels, mid), BF16), mid_f32, one_tile],
        [pltpu.VMEM(padded, BF16)],
        flops=18 * pixels * mid * mid, nbytes=6 << 20,
    )(pre_squeeze, s_squeeze, s_reduce, params, mask, w_window)
    s_window = sync(stat)

    act_window, pre_widen, stat = widen_out(pre_window, s_window, p_window, w_widen)
    s_widen = sync_wide(stat)

    block_out, grad_final, gsum = call(
        final_kernel,
        (blocks,),
        [wide_spec, tile_n(), count_spec, p_widen, mask_spec, wide_spec, wide_spec],
        [wide_spec, wide_spec, tile_n()],
        [shaped((pixels, c_out), BF16), wide_f32, wide_tiles],
        nbytes=7 << 20,
    )(pre_widen, s_widen, s_reduce, params, mask, first_out, cot)
    g_widen = sync_wide(gsum)

    gpre_widen, grad_window, gsum = call(
        widen_back_kernel,
        (blocks,),
        [
            wide_spec, wide_spec, tile_n(), tile_n(), count_spec, p_widen, mask_spec, cols(mid, TILE),
            mid_spec, all_tiles, p_window,
        ],
        [wide_spec, mid_spec, all_tiles],
        [shaped((pixels, c_out), BF16), mid_f32, one_tile],
        flops=2 * pixels * mid * c_out, nbytes=8 << 20,
    )(grad_final, pre_widen, s_widen, g_widen, s_reduce, params, mask, w_widen, pre_window, s_window, params)
    early_made = outer_spread(dp, act_window, left_const, gpre_widen, right_n, whole, blocks, blocks, 0, 9 + blocks, None)
    g_window = after(sync(gsum), early_made)

    gpad_window, grad_squeeze, gsum = call(
        functools.partial(window_back_kernel, width, height, images),
        (3,),
        [
            mid_spec, mid_spec, all_tiles, all_tiles, count_spec, p_window, mask_spec, tap_spec,
            mid_spec, all_tiles, p_squeeze,
        ],
        [full(padded), mid_spec, all_tiles],
        [shaped(padded, BF16), mid_f32, one_tile],
        flops=18 * pixels * mid * mid, nbytes=8 << 20,
    )(grad_window, pre_window, s_window, g_window, s_reduce, params, mask, w_window, pre_squeeze, s_squeeze, params)
    early_made = outer_spread(
        dp, act_squeeze, left_const, gpad_window, full(padded), window_taps, 9, 9, blocks, 9 + blocks, early_made
    )
    early_sum = lax.psum_scatter(early_made.reshape(-1, TILE), "dp", scatter_dimension=0, tiled=True)
    g_squeeze = sync(gsum)

    gpre_squeeze, grad_joined, gsum = call(
        squeeze_back_kernel,
        (blocks,),
        [
            mid_spec, mid_spec, all_tiles, all_tiles, count_spec, p_squeeze, mask_spec,
            pl.BlockSpec((TILE, mid), lambda n: (n, 0)),
            wide_spec, wide_spec, wide_spec, e_spec, s_spec, p_expand, p_short,
        ],
        [mid_spec, wide_spec, tile_n(rows=16)],
        [shaped((pixels, mid), BF16), wide_f32, shaped((16 * blocks, LANES))],
        flops=2 * pixels * mid * c_out, nbytes=11 << 20,
    )(
        grad_squeeze, pre_squeeze, s_squeeze, g_squeeze, s_reduce, params, mask, w_squeeze,
        grad_final, pre_expand, pre_short, s_both, s_both, params, params,
    )
    g_both = sync_wide(gsum)
    order_squeeze, order_expand = xs + ys + zs, ys + xs + zs
    order_short = (xs + ys + zs, ys + xs + zs)
    halving = lambda made, order: Halving(made[0], order, flat, devices, made[1], core_bit)
    s_squeeze_grad = halving(
        outer_halves(core, first_out, right_n, gpre_squeeze, full((pixels, mid)), whole, blocks, 1), order_squeeze
    )
    g_both = after(g_both, s_squeeze_grad.keep)
    token = s_squeeze_grad.moves.pop(0)(g_both)

    gpre_expand, gpre_short, grad_spatial, gsum = call(
        expand_back_kernel,
        (blocks,),
        [
            wide_spec, wide_spec, wide_spec, e_spec, s_spec, tile_n(rows=16), count_spec, p_expand, p_short,
            mask_spec, cols(mid, TILE), mid_spec, all_tiles, p_spatial,
        ],
        [wide_spec, wide_spec, mid_spec, all_tiles],
        [shaped((pixels, c_out), BF16), shaped((pixels, c_out), BF16), mid_f32, one_tile],
        flops=2 * pixels * mid * c_out, nbytes=11 << 20,
    )(
        grad_joined, pre_expand, pre_short, s_both, s_both, g_both, s_reduce, params, params, mask, w_expand,
        pre_spatial, s_spatial, params,
    )
    s_expand_grad = halving(
        outer_halves(core, act_spatial, left_const, gpre_expand, right_n, whole, blocks, blocks), order_expand
    )
    s_short_grad = [
        halving(
            outer_halves(
                core, planes.reshape(4 * pixels, c_in), pl.BlockSpec((pixels, TILE), lambda b, *_, k=k: (0, k)),
                gpre_short, right_n, whole, blocks, blocks,
            ),
            order_short[k % 2],
        )
        for k in range(in_blocks)
    ]
    g_spatial = after(
        sync(gsum), s_expand_grad.keep, [s.keep for s in s_short_grad], s_squeeze_grad.received
    )
    for stream in [s_expand_grad] + s_short_grad:
        token = stream.moves.pop(0)(g_spatial)

    gshift_spatial, grad_reduce, gsum = call(
        functools.partial(spatial_back_kernel, width, height),
        (3,),
        [
            mid_spec, mid_spec, all_tiles, all_tiles, count_spec, p_spatial, mask_spec, tap_spec,
            full((4, pixels, mid)), all_tiles, p_reduce,
        ],
        [full((4, pixels, mid)), full((4, pixels, mid)), all_tiles],
        [shaped((4, pixels, mid), BF16), shaped((4, pixels, mid)), one_tile],
        flops=18 * pixels * mid * mid, nbytes=12 << 20,
    )(grad_spatial, pre_spatial, s_spatial, g_spatial, s_reduce, params, mask, w_spatial, pre_reduce, s_reduce, params)
    order_spatial, order_reduce = (zs[:1] + xs + ys + zs[1:], xs + ys + zs), ys + xs + zs
    spatial_parts = ((0, 5), (5, 4))
    late = [
        halving(
            outer_halves(
                core, act_reduce, pl.BlockSpec((1, pixels, mid), functools.partial(spatial_plane, place)),
                gshift_spatial, full((4, pixels, mid)), functools.partial(spatial_taps, place), count, 1,
            ),
            order,
        )
        for (place, count), order in zip(spatial_parts, order_spatial)
    ]

    back_short = call(
        short_back_kernel,
        (blocks,),
        [wide_spec, cols(c_in, TILE)],
        full((pixels, c_in)),
        shaped((pixels, c_in)),
        flops=2 * pixels * c_in * c_out, nbytes=6 << 20,
    )(gpre_short, w_shortcut)
    crossed = [s.received for s in [s_expand_grad] + s_short_grad]
    g_reduce = after(sync(gsum), [s.keep for s in late], back_short, crossed)
    spread = TILE // dp
    early = Halving(early_sum.reshape(9 + blocks, spread, TILE), rep_bits, flat, devices)
    middle = [s_squeeze_grad, s_expand_grad] + s_short_grad
    token = run_streams(middle + late + [None, early], SCHEDULE[:FIRST], g_reduce, False)
    g_reduce = after(g_reduce, token)

    gpre_reduce, image_grad = call(
        functools.partial(reduce_back_kernel, quarter),
        (steps,),
        [
            plane_block(mid), plane_block(mid), all_tiles, all_tiles, count_spec, p_reduce,
            pl.BlockSpec((quarter, LANES), lambda k: (k, 0)), full((c_in, mid)),
            pl.BlockSpec((quarter, c_in), lambda k: (k, 0)), full(perm.shape),
        ],
        [plane_block(mid), pl.BlockSpec((4 * quarter, c_in), lambda k: (k, 0))],
        [shaped((4, pixels, mid), BF16), shaped((images * 4 * height * width, c_in), BF16)],
        flops=8 * pixels * c_in * mid, nbytes=10 << 20,
    )(grad_reduce, pre_reduce, s_reduce, g_reduce, s_reduce, params, mask, w_reduce, back_short, perm_back)
    late.append(
        halving(
            outer_halves(
                core, planes.reshape(4 * pixels, c_in), pl.BlockSpec((4 * pixels, TILE), lambda b, *_: (0, b)),
                gpre_reduce.reshape(4 * pixels, mid), full((4 * pixels, mid)), whole, in_blocks, 1,
            ),
            order_reduce,
        )
    )

    tall, flat_cols = lambda b: (b, 0), lambda b: (0, b)
    backs = [Return(stream, core_bit, flat, devices) for stream in late]
    for stream, back in zip(late, backs):
        stream.moves.extend(back.moves)
    token = run_streams(middle + late + [early], SCHEDULE[FIRST:], after(token, late[2].keep))

    def starts_of(first, order, rows):
        found = []
        for k in range(devices):
            start, left = first(k), rows
            for bit in order:
                left //= 2
                start += (k // bit % 2) * left
            found.append(start)
        return tuple(found)

    spread_starts = starts_of(lambda k: (k // rep) * spread, rep_bits, spread)

    def gathered(shard):
        everything = lax.all_gather(shard.reshape(-1, TILE), AXES, axis=0, tiled=False)
        return functools.partial(regroup, everything, total=shard.shape[0])

    regrouped = gathered(early.keep)
    grad_w_widen = regrouped(spread_starts, place=0, blocks=blocks, shape=(mid, c_out), where=flat_cols)
    grad_w_window = regrouped(spread_starts, place=blocks, blocks=9, shape=(9 * mid, mid), where=tall)

    half_starts = lambda order: starts_of(lambda k: (k // core_bit % 2) * (TILE // 2), order, TILE // 2)
    regrouped = gathered(jnp.concatenate([s.keep for s in middle], axis=0))
    grad_w_squeeze = regrouped(half_starts(order_squeeze), place=0, blocks=blocks, shape=(c_out, mid), where=tall)
    grad_w_expand = regrouped(
        half_starts(order_expand), place=blocks, blocks=blocks, shape=(mid, c_out), where=flat_cols
    )
    grad_w_short = None
    for k in range(in_blocks):
        grad_w_short = regrouped(
            half_starts(order_short[k % 2]), place=(2 + k) * blocks, blocks=blocks, shape=(c_in, c_out),
            where=lambda b, k=k: (k, b), into=grad_w_short,
        )

    grad_w_spatial = None
    for (place, count), back in zip(spatial_parts, backs):
        grad_w_spatial = assemble(
            back.places(), back.pieces(), 0, count, (9 * mid, mid), lambda b, place=place: (place + b, 0),
            into=grad_w_spatial,
        )
    grad_w_reduce = assemble(backs[2].places(), backs[2].pieces(), 0, in_blocks, (c_in, mid), tall)
    grad_w_window, grad_w_spatial = (g.reshape(3, 3, mid, mid) for g in (grad_w_window, grad_w_spatial))

    shift_total = vector(g_both, 0, 16)
    return (
        block_out.reshape(cotangent.shape),
        image_grad.reshape(image_input.shape),
        grad_w_reduce,
        grad_w_spatial,
        grad_w_expand,
        grad_w_short,
        vector(jnp.sum(g_reduce, axis=0), ROWS, 8),
        vector(jnp.sum(g_reduce, axis=0), 0, 8),
        vector(jnp.sum(g_spatial, axis=0), ROWS, 8),
        vector(jnp.sum(g_spatial, axis=0), 0, 8),
        vector(g_both, ROWS, 16),
        shift_total,
        vector(g_both, 2 * ROWS, 16),
        shift_total,
        grad_w_squeeze,
        grad_w_window,
        grad_w_widen,
        vector(jnp.sum(g_squeeze, axis=0), ROWS, 8),
        vector(jnp.sum(g_squeeze, axis=0), 0, 8),
        vector(jnp.sum(g_window, axis=0), ROWS, 8),
        vector(jnp.sum(g_window, axis=0), 0, 8),
        vector(g_widen, ROWS, 8),
        vector(g_widen, 0, 8),
    )


def solution(mesh):
    split = P(AXES, None, None, None)
    return jax.shard_map(
        functools.partial(on_device, mesh.shape["dp"], mesh.shape["rep"]),
        mesh=mesh,
        in_specs=(split, P(AXES), P(AXES)) + (P(),) * 21 + (split,),
        out_specs=(split, split) + (P(),) * 21,
        check_vma=False,
    )
```

```python
import functools

import jax
import jax.numpy as jnp
import numpy as np
from jax import lax
from jax.experimental import pallas as pl
from jax.experimental.pallas import tpu as pltpu
from jax.sharding import PartitionSpec as P

EPSILON = 1e-05
F32 = jnp.float32
BF16 = jnp.bfloat16
AXES = ("dp", "rep")
LANES = 128
TILE = 512
ROWS = TILE // LANES
MIB = 60
SCHEDULE = (
    0, 1, 2, 3, 7, 4, 5, 9, 0, 1, 7, 6, 2, 3, 7, 6, 0, 1, 2, 3, 4, 5, 6, 0, 1, 6, 2, 3, 5, 4,
    6, 0, 1, 2, 3, 6, 5, 4, 5, 4, 5, 4, 5, 4, 5, 4, 5, 4, 8, 5, 4, 8, 5, 4,
)


def dot(left, right):
    return jnp.dot(left, right, preferred_element_type=F32)


def dot_nt(left, right):
    return lax.dot_general(left, right, (((1,), (1,)), ((), ())), preferred_element_type=F32)


def pack(vector):
    return jnp.concatenate(
        [vector[:, LANES * k : LANES * (k + 1)] for k in range(vector.shape[1] // LANES)], axis=0
    )


def unpack(rows):
    return jnp.concatenate([rows[k : k + 1, :] for k in range(rows.shape[0])], axis=1)


def col_sum(values):
    return jnp.sum(values, axis=0, keepdims=True)


def stat_tile(first, second):
    return jnp.concatenate([pack(col_sum(first)), pack(col_sum(second))], axis=0)


def put(ref, tile):
    ref[...] = jnp.broadcast_to(tile, ref.shape)


def total(ref):
    return ref[...] if len(ref.shape) == 2 else jnp.sum(ref[...], axis=0)


def coefficients(stat_ref, count_ref, param_ref, factor=1.0):
    stat, param = total(stat_ref), param_ref[...]
    count = total(count_ref)[0:ROWS, :] * factor
    average = stat[0:ROWS] / count
    inverse = lax.rsqrt(stat[ROWS : 2 * ROWS] / count - average * average + EPSILON)
    return (
        unpack(average),
        unpack(inverse),
        unpack(param[0:ROWS]),
        unpack(param[ROWS : 2 * ROWS]),
    )


def back_coefficients(grad_rows_shift, grad_rows_gain, count_ref, factor=1.0):
    count = total(count_ref)[0:ROWS, :] * factor
    return unpack(grad_rows_shift / count), unpack(grad_rows_gain / count)


def logistic(values):
    return 0.5 * jnp.tanh(0.5 * values) + 0.5


def silu(values):
    return values * logistic(values)


def slope(values):
    gate = logistic(values)
    return gate * (1.0 + values * (1.0 - gate))


def column(mask_ref):
    return mask_ref[:, 0:1]


def pixel_ids(pixels, width):
    return lax.broadcasted_iota(jnp.int32, (pixels, 1), 0)


def shift_cols(values, step, width):
    pixels = values.shape[0]
    place = lax.rem(pixel_ids(pixels, width), width)
    rolled = pltpu.roll(values, (-step) % pixels, 0)
    keep = place < width - step if step > 0 else place >= -step
    return jnp.where(keep, rolled, 0.0)


def shift_rows(values, step, width, height):
    pixels = values.shape[0]
    place = lax.rem(lax.div(pixel_ids(pixels, width), width), height)
    rolled = pltpu.roll(values, (-step * width) % pixels, 0)
    keep = place < height - step if step > 0 else place >= -step
    return jnp.where(keep, rolled, 0.0)


def full(shape):
    zeros = (0,) * len(shape)
    return pl.BlockSpec(shape, lambda *_: zeros)


def cols(rows, width):
    return pl.BlockSpec((rows, width), lambda n, *_: (0, n))


def tile_at(index, rows=8):
    return pl.BlockSpec((rows, LANES), lambda *_: (index, 0))


def tile_n(offset=0, rows=8):
    return pl.BlockSpec((rows, LANES), lambda n, *_: (offset + n, 0))


def call(kernel, grid, in_specs, out_specs, out_shape, scratch=(), mib=MIB, flops=0, nbytes=0):
    return pl.pallas_call(
        kernel,
        grid=grid,
        in_specs=in_specs,
        out_specs=out_specs,
        out_shape=out_shape,
        scratch_shapes=scratch,
        compiler_params=pltpu.CompilerParams(
            vmem_limit_bytes=mib << 20, dimension_semantics=("arbitrary",) * len(grid)
        ),
        cost_estimate=pl.CostEstimate(flops=flops, bytes_accessed=nbytes, transcendentals=0),
    )


def shaped(shape, dtype=F32):
    return jax.ShapeDtypeStruct(shape, dtype)


def reduce_kernel(quarter, x_ref, perm_ref, mask_ref, all_mask_ref, w_ref, xp_ref, pre_ref, stat_ref, acc_ref):
    step = pl.program_id(0)
    mask = column(mask_ref)
    masking = jnp.concatenate([mask] * 4, axis=0)
    planes = (dot(perm_ref[...], x_ref[...]) * masking).astype(BF16)
    pre = dot(planes, w_ref[...])
    for q in range(4):
        xp_ref[q] = planes[q * quarter : (q + 1) * quarter]
        pre_ref[q] = pre[q * quarter : (q + 1) * quarter]

    @pl.when(step == 0)
    def _():
        acc_ref[...] = jnp.zeros_like(acc_ref)

    acc_ref[0:1, :] += col_sum(pre)
    acc_ref[1:2, :] += col_sum(pre * pre)

    @pl.when(step == pl.num_programs(0) - 1)
    def _():
        count = jnp.broadcast_to(col_sum(all_mask_ref[...]), (8, LANES))
        put(stat_ref, jnp.concatenate([pack(acc_ref[0:1, :]), pack(acc_ref[1:2, :]), count], axis=0))


def product_kernel(x_ref, w_ref, out_ref, stat_ref):
    pre = dot(x_ref[0], w_ref[...])
    out_ref[...] = pre
    stat_ref[...] = stat_tile(pre, pre * pre)


def spatial_kernel(width, height, pre_ref, stat_ref, count_ref, param_ref, mask_ref, w_ref, act_ref, out_ref, out_stat_ref, y_ref):
    r = pl.program_id(0)
    mask = column(mask_ref)

    @pl.when(r == 0)
    def _():
        average, inverse, gain, shift = coefficients(stat_ref, count_ref, param_ref, 4.0)
        for q in range(4):
            norm = (pre_ref[q] - average) * inverse * gain + shift
            act_ref[q] = (silu(norm) * mask).astype(BF16)

    row_parity = jnp.where(r == 1, 0, 1)
    row_shift = jnp.where(r == 0, 1, 0)
    even, odd = act_ref[2 * row_parity], act_ref[2 * row_parity + 1]
    straight = dot(even, w_ref[0, 1]) + dot(odd, w_ref[0, 2])
    moved = dot(odd, w_ref[0, 0])

    @pl.when(r < 2)
    def _():
        y_ref[2 * row_shift] = straight
        y_ref[2 * row_shift + 1] = moved

    @pl.when(r == 2)
    def _():
        upper = y_ref[2] + shift_cols(y_ref[3], -1, width)
        lower = y_ref[0] + straight + shift_cols(y_ref[1] + moved, -1, width)
        pre = lower + shift_rows(upper, -1, width, height)
        out_ref[...] = pre
        masked = pre * mask
        put(out_stat_ref, stat_tile(masked, masked * pre))


def expand_kernel(pre_ref, stat_ref, count_ref, param_ref, mask_ref, w_ref, act_ref, out_ref, out_stat_ref):
    @pl.when(pl.program_id(0) == 0)
    def _():
        average, inverse, gain, shift = coefficients(stat_ref, count_ref, param_ref)
        norm = (pre_ref[...] - average) * inverse * gain + shift
        act_ref[...] = (silu(norm) * column(mask_ref)).astype(BF16)

    pre = dot(act_ref[...], w_ref[...])
    out_ref[...] = pre
    put(out_stat_ref, stat_tile(pre, pre * pre))


def join_kernel(pe_ref, ps_ref, se_ref, ss_ref, count_ref, qe_ref, qs_ref, mask_ref, w_ref, first_ref, out_ref, out_stat_ref):
    n = pl.program_id(0)
    average_e, inverse_e, gain_e, shift_e = coefficients(se_ref, count_ref, qe_ref)
    average_s, inverse_s, gain_s, shift_s = coefficients(ss_ref, count_ref, qs_ref)
    joined = (pe_ref[...] - average_e) * inverse_e * gain_e + shift_e
    joined += (ps_ref[...] - average_s) * inverse_s * gain_s + shift_s
    first = (silu(joined) * column(mask_ref)).astype(BF16)
    first_ref[...] = first
    part = dot(first, w_ref[...])

    @pl.when(n == 0)
    def _():
        out_ref[...] = part

    @pl.when(n > 0)
    def _():
        out_ref[...] += part

    @pl.when(n == pl.num_programs(0) - 1)
    def _():
        pre = out_ref[...]
        put(out_stat_ref, stat_tile(pre, pre * pre))


def store_padded(target_ref, values, step, width, height, images):
    area = width * height
    channels = values.shape[1]
    zeros = jnp.zeros((width, channels), BF16)
    for k in range(3):
        moved = values if k == 1 else shift_cols(values, step * (k - 1), width)
        moved = moved.astype(BF16)
        for b in range(images):
            target_ref[k, b, 0:width, :] = zeros
            target_ref[k, b, area + width : area + 2 * width, :] = zeros
            target_ref[k, b, width : area + width, :] = moved[b * area : (b + 1) * area]


def window_rows(ref, k, first, area, images):
    return jnp.concatenate([ref[k, b, pl.ds(first, area), :] for b in range(images)], axis=0)


def window_kernel(width, height, images, pre_ref, stat_ref, count_ref, param_ref, mask_ref, w_ref, act_ref, out_ref, out_stat_ref, pad_ref):
    r = pl.program_id(0)

    @pl.when(r == 0)
    def _():
        average, inverse, gain, shift = coefficients(stat_ref, count_ref, param_ref)
        norm = (pre_ref[...] - average) * inverse * gain + shift
        act = silu(norm) * column(mask_ref)
        act_ref[...] = act.astype(BF16)
        store_padded(pad_ref, act, 1, width, height, images)

    first = pl.multiple_of(r * width, width)
    part = dot(window_rows(pad_ref, 0, first, width * height, images), w_ref[0, 0])
    for k in (1, 2):
        part += dot(window_rows(pad_ref, k, first, width * height, images), w_ref[0, k])

    @pl.when(r == 0)
    def _():
        out_ref[...] = part

    @pl.when(r > 0)
    def _():
        out_ref[...] += part

    @pl.when(r == 2)
    def _():
        pre = out_ref[...]
        masked = pre * column(mask_ref)
        put(out_stat_ref, stat_tile(masked, masked * pre))


def final_kernel(pre_ref, stat_ref, count_ref, param_ref, mask_ref, first_ref, cot_ref, out_ref, grad_ref, sum_ref):
    average, inverse, gain, shift = coefficients(stat_ref, count_ref, param_ref)
    mask = column(mask_ref)
    hat = (pre_ref[...] - average) * inverse
    final = hat * gain + shift + first_ref[...].astype(F32)
    gate = logistic(final)
    out_ref[...] = (final * gate * mask).astype(BF16)
    grad = cot_ref[...].astype(F32) * mask * (gate * (1.0 + final * (1.0 - gate)))
    grad_ref[...] = grad
    put(sum_ref, stat_tile(grad, grad * hat))


def norm_back(grad, hat, scale, shift_term, gain_term, mask):
    return ((grad - mask * (shift_term + hat * gain_term)) * scale).astype(BF16)


def widen_back_kernel(
    grad_ref, pre_ref, stat_ref, gsum_ref, count_ref, param_ref, mask_ref, w_ref, in_ref, in_stat_ref, in_param_ref,
    gpre_ref, out_ref, sum_ref,
):
    n = pl.program_id(0)
    mask = column(mask_ref)
    average, inverse, gain, _ = coefficients(stat_ref, count_ref, param_ref)
    gsum = total(gsum_ref)
    shift_term, gain_term = back_coefficients(gsum[0:ROWS], gsum[ROWS : 2 * ROWS], count_ref)
    hat = (pre_ref[...] - average) * inverse
    gpre = norm_back(grad_ref[...], hat, inverse * gain, shift_term, gain_term, mask)
    gpre_ref[...] = gpre
    part = dot_nt(gpre, w_ref[...])

    @pl.when(n == 0)
    def _():
        out_ref[...] = part

    @pl.when(n > 0)
    def _():
        out_ref[...] += part

    @pl.when(n == pl.num_programs(0) - 1)
    def _():
        finish_back(in_ref[...], in_stat_ref, count_ref, in_param_ref, mask, out_ref, sum_ref)


def finish_back(pre, stat_ref, count_ref, param_ref, mask, out_ref, sum_ref):
    average, inverse, gain, shift = coefficients(stat_ref, count_ref, param_ref)
    hat = (pre - average) * inverse
    grad = out_ref[...] * mask * slope(hat * gain + shift)
    out_ref[...] = grad
    put(sum_ref, stat_tile(grad, grad * hat))


def pre_grad(grad_ref, pre_ref, stat_ref, gsum_ref, count_ref, param_ref, mask):
    average, inverse, gain, _ = coefficients(stat_ref, count_ref, param_ref)
    gsum = total(gsum_ref)
    shift_term, gain_term = back_coefficients(gsum[0:ROWS], gsum[ROWS : 2 * ROWS], count_ref)
    hat = (pre_ref[...] - average) * inverse
    return norm_back(grad_ref[...], hat, inverse * gain, shift_term, gain_term, mask)


def window_back_kernel(
    width, height, images,
    grad_ref, pre_ref, stat_ref, gsum_ref, count_ref, param_ref, mask_ref, w_ref, in_ref, in_stat_ref, in_param_ref,
    pad_ref, out_ref, sum_ref,
):
    r = pl.program_id(0)
    mask = column(mask_ref)

    @pl.when(r == 0)
    def _():
        gpre = pre_grad(grad_ref, pre_ref, stat_ref, gsum_ref, count_ref, param_ref, mask)
        store_padded(pad_ref, gpre.astype(F32), -1, width, height, images)

    first = pl.multiple_of((2 - r) * width, width)
    part = dot_nt(window_rows(pad_ref, 0, first, width * height, images), w_ref[0, 0])
    for k in (1, 2):
        part += dot_nt(window_rows(pad_ref, k, first, width * height, images), w_ref[0, k])

    @pl.when(r == 0)
    def _():
        out_ref[...] = part

    @pl.when(r > 0)
    def _():
        out_ref[...] += part

    @pl.when(r == 2)
    def _():
        finish_back(in_ref[...], in_stat_ref, count_ref, in_param_ref, mask, out_ref, sum_ref)


def squeeze_back_kernel(
    grad_ref, pre_ref, stat_ref, gsum_ref, count_ref, param_ref, mask_ref, w_ref,
    gfinal_ref, pe_ref, ps_ref, se_ref, ss_ref, qe_ref, qs_ref,
    gpre_ref, gj_ref, sum_ref,
):
    mask = column(mask_ref)

    @pl.when(pl.program_id(0) == 0)
    def _():
        gpre_ref[...] = pre_grad(grad_ref, pre_ref, stat_ref, gsum_ref, count_ref, param_ref, mask)

    gfirst = gfinal_ref[...] + dot_nt(gpre_ref[...], w_ref[...])
    average_e, inverse_e, gain_e, shift_e = coefficients(se_ref, count_ref, qe_ref)
    average_s, inverse_s, gain_s, shift_s = coefficients(ss_ref, count_ref, qs_ref)
    hat_e = (pe_ref[...] - average_e) * inverse_e
    hat_s = (ps_ref[...] - average_s) * inverse_s
    joined = hat_e * gain_e + shift_e + (hat_s * gain_s + shift_s)
    grad = gfirst * mask * slope(joined)
    gj_ref[...] = grad
    sum_ref[...] = jnp.concatenate(
        [stat_tile(grad, grad * hat_e), pack(col_sum(grad * hat_s)), jnp.zeros((ROWS, LANES), F32)], axis=0
    )


def expand_back_kernel(
    gj_ref, pe_ref, ps_ref, se_ref, ss_ref, gsum_ref, count_ref, qe_ref, qs_ref, mask_ref, w_ref,
    in_ref, in_stat_ref, in_param_ref,
    ge_ref, gs_ref, out_ref, sum_ref,
):
    n = pl.program_id(0)
    mask = column(mask_ref)
    average_e, inverse_e, gain_e, _ = coefficients(se_ref, count_ref, qe_ref)
    average_s, inverse_s, gain_s, _ = coefficients(ss_ref, count_ref, qs_ref)
    gsum = total(gsum_ref)
    shift_term, gain_e_term = back_coefficients(gsum[0:ROWS], gsum[ROWS : 2 * ROWS], count_ref)
    _, gain_s_term = back_coefficients(gsum[0:ROWS], gsum[2 * ROWS : 3 * ROWS], count_ref)
    grad = gj_ref[...]
    hat_e = (pe_ref[...] - average_e) * inverse_e
    hat_s = (ps_ref[...] - average_s) * inverse_s
    ge = norm_back(grad, hat_e, inverse_e * gain_e, shift_term, gain_e_term, mask)
    ge_ref[...] = ge
    gs_ref[...] = norm_back(grad, hat_s, inverse_s * gain_s, shift_term, gain_s_term, mask)
    part = dot_nt(ge, w_ref[...])

    @pl.when(n == 0)
    def _():
        out_ref[...] = part

    @pl.when(n > 0)
    def _():
        out_ref[...] += part

    @pl.when(n == pl.num_programs(0) - 1)
    def _():
        finish_back(in_ref[...], in_stat_ref, count_ref, in_param_ref, mask, out_ref, sum_ref)


def spatial_back_kernel(
    width, height,
    grad_ref, pre_ref, stat_ref, gsum_ref, count_ref, param_ref, mask_ref, w_ref, in_ref, in_stat_ref, in_param_ref,
    shift_ref, out_ref, sum_ref,
):
    r = pl.program_id(0)
    mask = column(mask_ref)

    @pl.when(r == 0)
    def _():
        gpre = pre_grad(grad_ref, pre_ref, stat_ref, gsum_ref, count_ref, param_ref, mask).astype(F32)
        below = shift_rows(gpre, 1, width, height)
        shift_ref[0] = gpre.astype(BF16)
        shift_ref[1] = shift_cols(gpre, 1, width).astype(BF16)
        shift_ref[2] = below.astype(BF16)
        shift_ref[3] = shift_cols(below, 1, width).astype(BF16)

    row_parity = jnp.where(r == 1, 0, 1)
    row_shift = jnp.where(r == 0, 1, 0)
    straight, moved = shift_ref[2 * row_shift], shift_ref[2 * row_shift + 1]
    even = dot_nt(straight, w_ref[0, 1])
    odd = dot_nt(moved, w_ref[0, 0]) + dot_nt(straight, w_ref[0, 2])

    @pl.when(r < 2)
    def _():
        out_ref[2 * row_parity] = even
        out_ref[2 * row_parity + 1] = odd

    @pl.when(r == 2)
    def _():
        out_ref[2] += even
        out_ref[3] += odd
        average, inverse, gain, shift = coefficients(in_stat_ref, count_ref, in_param_ref, 4.0)
        whole_sum = whole_hat = jnp.zeros((1, out_ref.shape[2]), F32)
        for q in range(4):
            hat = (in_ref[q] - average) * inverse
            grad = out_ref[q] * mask * slope(hat * gain + shift)
            out_ref[q] = grad
            whole_sum += col_sum(grad)
            whole_hat += col_sum(grad * hat)
        put(sum_ref, jnp.concatenate([pack(whole_sum), pack(whole_hat)], axis=0))


def short_back_kernel(g_ref, w_ref, out_ref):
    part = dot_nt(g_ref[...], w_ref[...])

    @pl.when(pl.program_id(0) == 0)
    def _():
        out_ref[...] = part

    @pl.when(pl.program_id(0) > 0)
    def _():
        out_ref[...] += part


def reduce_back_kernel(
    quarter, grad_ref, pre_ref, stat_ref, gsum_ref, count_ref, param_ref, mask_ref, w_ref, short_ref, perm_ref,
    gpre_ref, out_ref,
):
    mask = column(mask_ref)
    masking = jnp.concatenate([mask] * 4, axis=0)
    average, inverse, gain, _ = coefficients(stat_ref, count_ref, param_ref, 4.0)
    gsum = total(gsum_ref)
    shift_term, gain_term = back_coefficients(gsum[0:ROWS], gsum[ROWS : 2 * ROWS], count_ref, 4.0)
    grad = jnp.concatenate([grad_ref[q] for q in range(4)], axis=0)
    pre = jnp.concatenate([pre_ref[q] for q in range(4)], axis=0)
    hat = (pre - average) * inverse
    gpre = norm_back(grad, hat, inverse * gain, shift_term, gain_term, masking)
    for q in range(4):
        gpre_ref[q] = gpre[q * quarter : (q + 1) * quarter]
    image = dot_nt(gpre, w_ref[...])
    image = jnp.concatenate([image[0:quarter] + short_ref[...], image[quarter:]], axis=0)
    image = (image * masking).astype(BF16)
    out_ref[...] = dot(perm_ref[...], image).astype(BF16)


def turn_left(left_ref, turned_ref, per_left):
    @pl.when(lax.rem(pl.program_id(0), per_left) == 0)
    def _():
        left = left_ref[...] if len(left_ref.shape) == 2 else left_ref[0]
        turned_ref[...] = left.T


def halves_kernel(pick, per_left, core_ref, left_ref, right_ref, keep_ref, send_ref, turned_ref):
    turn_left(left_ref, turned_ref, per_left)
    half = TILE // 2
    right = pick(right_ref, pl.program_id(0))
    mine = pl.multiple_of(core_ref[0] * half, half)
    away = pl.multiple_of((1 - core_ref[0]) * half, half)
    send_ref[0] = dot(turned_ref[pl.ds(away, half), :], right)
    keep_ref[0] = dot(turned_ref[pl.ds(mine, half), :], right)


def outer_halves(core, left, left_spec, right, right_spec, pick, blocks, per_left):
    half = TILE // 2
    pixels = left_spec.block_shape[-2]
    shape = shaped((blocks, half, TILE))
    out_spec = pl.BlockSpec((1, half, TILE), lambda b, *_: (b, 0, 0))
    return pl.pallas_call(
        functools.partial(halves_kernel, pick, per_left),
        grid_spec=pltpu.PrefetchScalarGridSpec(
            num_scalar_prefetch=1,
            grid=(blocks,),
            in_specs=[left_spec, right_spec],
            out_specs=[out_spec, out_spec],
            scratch_shapes=[pltpu.VMEM((TILE, pixels), BF16)],
        ),
        out_shape=[shape, shape],
        compiler_params=outer_params(),
        cost_estimate=outer_cost(blocks, pixels),
    )(core, left, right)


def outer_params():
    return pltpu.CompilerParams(vmem_limit_bytes=MIB << 20, dimension_semantics=("arbitrary",))


def outer_cost(blocks, pixels):
    return pl.CostEstimate(
        flops=2 * blocks * pixels * TILE * TILE, bytes_accessed=blocks * TILE * TILE * 4, transcendentals=0
    )


def spread_kernel(pick, per_left, left_ref, right_ref, *refs):
    out_ref, turned_ref = refs[-2], refs[-1]
    turn_left(left_ref, turned_ref, per_left)
    out_ref[...] = dot(turned_ref[...], pick(right_ref, pl.program_id(0))).reshape(out_ref.shape)


def outer_spread(shares, left, left_spec, right, right_spec, pick, blocks, per_left, place, total, into):
    rows = TILE // shares
    pixels = left_spec.block_shape[-2]
    extra = () if into is None else (into,)
    return pl.pallas_call(
        functools.partial(spread_kernel, pick, per_left),
        grid=(blocks,),
        in_specs=[left_spec, right_spec] + [pl.BlockSpec(memory_space=pl.ANY)] * len(extra),
        out_specs=pl.BlockSpec((shares, rows, TILE), lambda b: (0, place + b, 0)),
        out_shape=shaped((shares, total * rows, TILE)),
        scratch_shapes=[pltpu.VMEM((TILE, pixels), BF16)],
        input_output_aliases={2: 0} if extra else {},
        compiler_params=outer_params(),
        cost_estimate=outer_cost(blocks, pixels),
    )(left, right, *extra)


def assemble_kernel(chunks, place_ref, own_ref, near_ref, far_ref, both_ref, *refs):
    out_ref = refs[-1]
    rows = TILE // 4 // chunks
    for k, ref in enumerate((own_ref, near_ref, far_ref, both_ref)):
        for c in range(chunks):
            start = pl.multiple_of(place_ref[k * chunks + c], rows)
            out_ref[pl.ds(start, rows), :] = ref[0, c * rows : (c + 1) * rows, :]


def assemble(places, pieces, first, blocks, shape, where, chunks=1, into=None):
    in_spec = pl.BlockSpec((1, TILE // 4, TILE), lambda b, *_: (first + b, 0, 0))
    extra = () if into is None else (into,)
    return pl.pallas_call(
        functools.partial(assemble_kernel, chunks),
        grid_spec=pltpu.PrefetchScalarGridSpec(
            num_scalar_prefetch=1,
            grid=(blocks,),
            in_specs=[in_spec] * 4 + [pl.BlockSpec(memory_space=pl.ANY)] * len(extra),
            out_specs=pl.BlockSpec((TILE, TILE), lambda b, *_: where(b)),
        ),
        out_shape=shaped(shape),
        input_output_aliases={5: 0} if extra else {},
        compiler_params=outer_params(),
        cost_estimate=pl.CostEstimate(
            flops=0, bytes_accessed=2 * blocks * TILE * TILE * 4, transcendentals=0
        ),
    )(places, *pieces, *extra)


def regroup_kernel(starts, in_ref, *refs):
    out_ref, rows = refs[-1], in_ref.shape[1]
    for k, start in enumerate(starts):
        out_ref[start : start + rows, :] = in_ref[k]


def regroup(gathered, starts, total, place, blocks, shape, where, into=None):
    devices, rows = gathered.shape[0], gathered.shape[1] // total
    extra = () if into is None else (into,)
    if rows % 8:
        order = np.argsort(np.asarray(starts))
        gathered = gathered.reshape(devices, total, rows, TILE)[order].transpose(1, 0, 2, 3)
        gathered = gathered.reshape(1, total * TILE, TILE)
        devices, rows, starts = 1, TILE, (0,)
    return pl.pallas_call(
        functools.partial(regroup_kernel, starts),
        grid=(blocks,),
        in_specs=[pl.BlockSpec((devices, rows, TILE), lambda b: (0, place + b, 0))]
        + [pl.BlockSpec(memory_space=pl.ANY)] * len(extra),
        out_specs=pl.BlockSpec((TILE, TILE), where),
        out_shape=shaped(shape),
        input_output_aliases={1: 0} if extra else {},
        compiler_params=outer_params(),
        cost_estimate=pl.CostEstimate(
            flops=0, bytes_accessed=2 * blocks * TILE * TILE * 4, transcendentals=0
        ),
    )(gathered, *extra)


def bits_of(first, size):
    found = []
    while size > 1:
        found.append(first)
        first, size = first * 2, size // 2
    return found


def mesh_bits(dp, rep):
    side = int(round(dp**0.5))
    if side * side == dp:
        return 1, bits_of(rep, side), bits_of(rep * side, side), bits_of(2, rep // 2)
    side = int(round((dp // 2) ** 0.5))
    return rep, bits_of(2 * rep, side), bits_of(2 * rep * side, side), bits_of(1, rep)


def swap(values, bit, devices):
    return lax.ppermute(values, AXES, [(i, i ^ bit) for i in range(devices)])


def sync_all(tile, devices):
    return lax.all_to_all(tile, AXES, 0, 0, tiled=True)


def sync_hops(tile, rounds, devices):
    for bits in rounds:
        near = [swap(tile, bit, devices) for bit in bits]
        if len(bits) == 2:
            across = swap(tile, bits[0] + bits[1], devices)
            tile = (tile + near[0]) + (near[1] + across)
        else:
            tile = tile + near[0]
    return tile


def device_bit(flat, bit):
    return lax.rem(lax.div(flat, bit), 2)


def after(values, *others):
    return lax.optimization_barrier((values,) + others)[0]


def half_sum(keep, received, which):
    rows = keep.shape[1] // 2
    first = lax.dynamic_slice_in_dim(keep, which * rows, rows, axis=1)
    return first + lax.dynamic_slice_in_dim(received, which * rows, rows, axis=1)


def join_halves(own, values, other):
    return jnp.where(
        own == 0, jnp.concatenate([values, other], axis=1), jnp.concatenate([other, values], axis=1)
    )


class Halving:
    def __init__(self, keep, order, flat, devices, send=None, core=None):
        self.keep, self.order, self.flat, self.devices = keep, list(order), flat, devices
        self.received = None
        self.moves = []
        if send is not None:
            self.moves.append(lambda token: self.cross(send, core, token))
        self.moves += [functools.partial(self.halve, bit) for bit in self.order] + [self.add]

    def cross(self, send, core, token):
        send = after(send, token)
        self.received = swap(send, core, self.devices)
        return send

    def halve(self, bit, token):
        own = device_bit(self.flat, bit)
        if self.received is None:
            keep, rows = after(self.keep, token), self.keep.shape[1] // 2
            send = lax.dynamic_slice_in_dim(keep, (1 - own) * rows, rows, axis=1)
            self.received = swap(send, bit, self.devices)
            self.keep = lax.dynamic_slice_in_dim(keep, own * rows, rows, axis=1)
            return send
        keep, received = after((self.keep, self.received), token)
        send = half_sum(keep, received, 1 - own)
        self.received = swap(send, bit, self.devices)
        keep, received = after((keep, received), send)
        self.keep = half_sum(keep, received, own)
        return send

    def add(self, token):
        keep, received = after((self.keep, self.received), token)
        self.keep = keep + received
        return self.keep


class Return:
    def __init__(self, source, core, flat, devices):
        self.source, self.core, self.flat, self.devices = source, core, flat, devices
        self.order = source.order
        back = list(reversed(self.order))
        self.moves = [functools.partial(self.widen, a, b) for a, b in zip([None] + back[:-1], back)]
        self.moves.append(self.cross)

    def widen(self, joined, bit, token):
        if joined is None:
            self.own = after(self.source.keep, token)
        else:
            own, other = after((self.own, self.near), token)
            self.own = join_halves(device_bit(self.flat, joined), own, other)
        self.near = swap(self.own, bit, self.devices)
        if bit == self.order[0]:
            self.far = swap(self.own, self.core, self.devices)
        return self.own

    def cross(self, token):
        self.near = after(self.near, token)
        self.both = swap(self.near, self.core, self.devices)
        return self.near

    def pieces(self):
        return self.own, self.near, self.far, self.both

    def places(self):
        half, quarter = TILE // 2, TILE // 4
        core, own = device_bit(self.flat, self.core), device_bit(self.flat, self.order[0])
        return jnp.stack(
            [c * half + o * quarter for c in (core, 1 - core) for o in (own, 1 - own)]
        ).astype(jnp.int32)


class Later:
    def __init__(self):
        self.moves = []


class Early:
    def __init__(self, source, make):
        self.source, self.make, self.whole = source, make, None
        self.moves, self.results = [], []

    def add_result(self, **how):
        self.moves.append(functools.partial(self.result, how))

    def gather(self):
        self.whole = lax.all_gather(self.source.keep.reshape(-1, TILE), AXES, axis=0, tiled=False)

    def result(self, how, token):
        if self.whole is None:
            self.gather()
        self.results.append(self.make(after(self.whole, token), **how))
        return self.results[-1]


def run_streams(streams, schedule, token, to_end=True):
    for k in schedule:
        if streams[k].moves:
            token = streams[k].moves.pop(0)(token)
    while to_end and any(s.moves for s in streams):
        for s in streams:
            if s.moves:
                token = s.moves.pop(0)(token)
    return token


def permutation(width):
    size = 8 * 2 * width
    matrix = np.zeros((size, size), np.float32)
    place = 0
    for row_parity in range(2):
        for col_parity in range(2):
            for i in range(4):
                for j in range(width):
                    matrix[place, (2 * i + row_parity) * 2 * width + 2 * j + col_parity] = 1.0
                    place += 1
    return matrix


def param_tiles(gain, shift):
    blocks = gain.shape[0] // TILE
    pair = jnp.stack([gain.reshape(blocks, ROWS, LANES), shift.reshape(blocks, ROWS, LANES)], axis=1)
    return pair.reshape(blocks * 8, LANES)


def vector(tiles, first, step):
    return tiles.reshape(-1, step, LANES)[:, first : first + ROWS].reshape(-1)


def on_device(dp, rep, *arrays):
    (image_input, heights, widths, w_reduce, w_spatial, w_expand, w_shortcut,
     gain_reduce, shift_reduce, gain_spatial, shift_spatial, gain_expand, shift_expand,
     gain_shortcut, shift_shortcut, w_squeeze, w_window, w_widen,
     gain_squeeze, shift_squeeze, gain_window, shift_window, gain_widen, shift_widen, cotangent) = arrays
    images, height, width, c_out = cotangent.shape
    c_in, mid = w_reduce.shape
    pixels = images * height * width
    quarter = 64
    steps = pixels // quarter
    blocks = c_out // TILE
    devices = dp * rep
    core_bit, x_bits, y_bits, z_bits = mesh_bits(dp, rep)
    hop_rounds = [(core_bit,)] + list(zip(y_bits, x_bits))
    hop_rounds += [tuple(z_bits[k : k + 2]) for k in range(0, len(z_bits), 2)]
    xs, ys, zs, rep_bits = x_bits, y_bits, z_bits, bits_of(1, rep)
    flat = lax.axis_index(AXES)
    core = device_bit(flat, core_bit).astype(jnp.int32).reshape(1)
    sync = functools.partial(sync_all, devices=devices)
    sync_wide = functools.partial(sync_hops, rounds=hop_rounds, devices=devices)

    row_ids = lax.broadcasted_iota(jnp.int32, (1, height, 1, LANES), 1)
    col_ids = lax.broadcasted_iota(jnp.int32, (1, 1, width, LANES), 2)
    inside = (row_ids < heights[:, None, None, None]) & (col_ids < widths[:, None, None, None])
    mask = jnp.where(inside, 1.0, 0.0).astype(F32).reshape(pixels, LANES)
    params = jnp.concatenate(
        [
            param_tiles(gain_reduce, shift_reduce), param_tiles(gain_spatial, shift_spatial),
            param_tiles(gain_squeeze, shift_squeeze), param_tiles(gain_window, shift_window),
            param_tiles(gain_expand, shift_expand), param_tiles(gain_shortcut, shift_shortcut),
            param_tiles(gain_widen, shift_widen),
        ],
        axis=0,
    )
    p_reduce, p_spatial, p_squeeze, p_window = (tile_at(k) for k in range(4))
    p_expand, p_short, p_widen = (tile_n(4 + blocks * k) for k in range(3))
    turn = permutation(width)
    perm, perm_back = jnp.asarray(turn, BF16), jnp.asarray(turn.T.copy(), BF16)
    image = image_input.reshape(images * 4 * height * width, c_in)
    cot = cotangent.reshape(pixels, c_out)

    mask_spec, wide_f32 = full((pixels, LANES)), shaped((pixels, c_out))
    mid_f32, mid_spec = shaped((pixels, mid)), full((pixels, mid))
    wide_spec, tap_spec = cols(pixels, TILE), pl.BlockSpec((1, 3, mid, mid), lambda r: (r, 0, 0, 0))
    plane_block = lambda c: pl.BlockSpec((4, quarter, c), lambda k: (0, k, 0))
    area, in_blocks = width * height, c_in // TILE
    left_const = pl.BlockSpec((pixels, TILE), lambda b, *_: (0, 0))
    right_n = pl.BlockSpec((pixels, TILE), lambda b, *_: (0, b))

    def whole(ref, b):
        return ref[...]

    def window_taps(ref, b):
        r, c = lax.div(b, 3), lax.rem(b, 3)
        first = pl.multiple_of((2 - r) * width, width)
        return window_rows(ref, c, first, area, images)

    def spatial_taps(place, ref, b):
        r, c = lax.div(place + b, 3), lax.rem(place + b, 3)
        return ref[2 * jnp.where(r == 0, 1, 0) + jnp.where(c == 0, 1, 0)]

    def spatial_plane(place, b, *_):
        r, c = lax.div(place + b, 3), lax.rem(place + b, 3)
        return (2 * jnp.where(r == 1, 0, 1) + jnp.where(c == 1, 0, 1), 0, 0)

    one_tile, wide_tiles = shaped((devices, 8, LANES)), shaped((8 * blocks, LANES))
    all_tiles = full((devices, 8, LANES))
    count_spec = pl.BlockSpec((devices, 8, LANES), lambda *_: (0, 1, 0))
    padded = (3, images, (height + 2) * width, mid)

    planes, pre_reduce, stat = call(
        functools.partial(reduce_kernel, quarter),
        (steps,),
        [
            pl.BlockSpec((4 * quarter, c_in), lambda k: (k, 0)), full(perm.shape),
            pl.BlockSpec((quarter, LANES), lambda k: (k, 0)), mask_spec, full((c_in, mid)),
        ],
        [plane_block(c_in), plane_block(mid), full((devices, 16, LANES))],
        [shaped((4, pixels, c_in), BF16), shaped((4, pixels, mid)), shaped((devices, 16, LANES))],
        [pltpu.VMEM((8, mid), F32)],
        flops=8 * pixels * c_in * mid, nbytes=8 << 20,
    )(image, perm, mask, mask, w_reduce)
    s_reduce = sync(stat)

    pre_short, stat_short = call(
        product_kernel,
        (blocks,),
        [pl.BlockSpec((1, pixels, c_in), lambda n: (0, 0, 0)), cols(c_in, TILE)],
        [wide_spec, tile_n()],
        [wide_f32, wide_tiles],
        flops=2 * pixels * c_in * c_out, nbytes=6 << 20,
    )(planes, w_shortcut)

    act_reduce, pre_spatial, stat = call(
        functools.partial(spatial_kernel, width, height),
        (3,),
        [full((4, pixels, mid)), all_tiles, count_spec, p_reduce, mask_spec, tap_spec],
        [full((4, pixels, mid)), mid_spec, all_tiles],
        [shaped((4, pixels, mid), BF16), mid_f32, one_tile],
        [pltpu.VMEM((4, pixels, mid), F32)],
        flops=18 * pixels * mid * mid, nbytes=8 << 20,
    )(pre_reduce, s_reduce, s_reduce, params, mask, w_spatial)
    s_spatial = sync(stat)

    def widen_out(pre, stat, p_spec, weights):
        return call(
            expand_kernel,
            (blocks,),
            [mid_spec, all_tiles, count_spec, p_spec, mask_spec, cols(mid, TILE)],
            [mid_spec, wide_spec, tile_n()],
            [shaped((pixels, mid), BF16), wide_f32, wide_tiles],
            flops=2 * pixels * mid * c_out, nbytes=5 << 20,
        )(pre, stat, s_reduce, params, mask, weights)

    act_spatial, pre_expand, stat = widen_out(pre_spatial, s_spatial, p_spatial, w_expand)
    s_both = sync_wide(jnp.concatenate([stat, stat_short], axis=0))
    e_spec, s_spec = tile_n(), tile_n(blocks)

    first_out, pre_squeeze, stat = call(
        join_kernel,
        (blocks,),
        [
            wide_spec, wide_spec, e_spec, s_spec, count_spec, p_expand, p_short, mask_spec,
            pl.BlockSpec((TILE, mid), lambda n: (n, 0)),
        ],
        [wide_spec, mid_spec, all_tiles],
        [shaped((pixels, c_out), BF16), mid_f32, one_tile],
        flops=2 * pixels * mid * c_out, nbytes=8 << 20,
    )(pre_expand, pre_short, s_both, s_both, s_reduce, params, params, mask, w_squeeze)
    s_squeeze = sync(stat)

    act_squeeze, pre_window, stat = call(
        functools.partial(window_kernel, width, height, images),
        (3,),
        [mid_spec, all_tiles, count_spec, p_squeeze, mask_spec, tap_spec],
        [mid_spec, mid_spec, all_tiles],
        [shaped((pixels, mid), BF16), mid_f32, one_tile],
        [pltpu.VMEM(padded, BF16)],
        flops=18 * pixels * mid * mid, nbytes=6 << 20,
    )(pre_squeeze, s_squeeze, s_reduce, params, mask, w_window)
    s_window = sync(stat)

    act_window, pre_widen, stat = widen_out(pre_window, s_window, p_window, w_widen)
    s_widen = sync_wide(stat)

    block_out, grad_final, gsum = call(
        final_kernel,
        (blocks,),
        [wide_spec, tile_n(), count_spec, p_widen, mask_spec, wide_spec, wide_spec],
        [wide_spec, wide_spec, tile_n()],
        [shaped((pixels, c_out), BF16), wide_f32, wide_tiles],
        nbytes=7 << 20,
    )(pre_widen, s_widen, s_reduce, params, mask, first_out, cot)
    g_widen = sync_wide(gsum)

    gpre_widen, grad_window, gsum = call(
        widen_back_kernel,
        (blocks,),
        [
            wide_spec, wide_spec, tile_n(), tile_n(), count_spec, p_widen, mask_spec, cols(mid, TILE),
            mid_spec, all_tiles, p_window,
        ],
        [wide_spec, mid_spec, all_tiles],
        [shaped((pixels, c_out), BF16), mid_f32, one_tile],
        flops=2 * pixels * mid * c_out, nbytes=8 << 20,
    )(grad_final, pre_widen, s_widen, g_widen, s_reduce, params, mask, w_widen, pre_window, s_window, params)
    early_made = outer_spread(dp, act_window, left_const, gpre_widen, right_n, whole, blocks, blocks, 0, 9 + blocks, None)
    g_window = after(sync(gsum), early_made)

    gpad_window, grad_squeeze, gsum = call(
        functools.partial(window_back_kernel, width, height, images),
        (3,),
        [
            mid_spec, mid_spec, all_tiles, all_tiles, count_spec, p_window, mask_spec, tap_spec,
            mid_spec, all_tiles, p_squeeze,
        ],
        [full(padded), mid_spec, all_tiles],
        [shaped(padded, BF16), mid_f32, one_tile],
        flops=18 * pixels * mid * mid, nbytes=8 << 20,
    )(grad_window, pre_window, s_window, g_window, s_reduce, params, mask, w_window, pre_squeeze, s_squeeze, params)
    early_made = outer_spread(
        dp, act_squeeze, left_const, gpad_window, full(padded), window_taps, 9, 9, blocks, 9 + blocks, early_made
    )
    g_squeeze = sync(gsum)
    early_sum = lax.psum_scatter(
        after(early_made, g_squeeze).reshape(-1, TILE), "dp", scatter_dimension=0, tiled=True
    )

    gpre_squeeze, grad_joined, gsum = call(
        squeeze_back_kernel,
        (blocks,),
        [
            mid_spec, mid_spec, all_tiles, all_tiles, count_spec, p_squeeze, mask_spec,
            pl.BlockSpec((TILE, mid), lambda n: (n, 0)),
            wide_spec, wide_spec, wide_spec, e_spec, s_spec, p_expand, p_short,
        ],
        [mid_spec, wide_spec, tile_n(rows=16)],
        [shaped((pixels, mid), BF16), wide_f32, shaped((16 * blocks, LANES))],
        flops=2 * pixels * mid * c_out, nbytes=11 << 20,
    )(
        grad_squeeze, pre_squeeze, s_squeeze, g_squeeze, s_reduce, params, mask, w_squeeze,
        grad_final, pre_expand, pre_short, s_both, s_both, params, params,
    )
    g_both = sync_wide(gsum)
    order_squeeze, order_expand = xs + ys + zs, ys + xs + zs
    order_short = (xs + ys + zs, ys + xs + zs)
    halving = lambda made, order: Halving(made[0], order, flat, devices, made[1], core_bit)
    s_squeeze_grad = halving(
        outer_halves(core, first_out, right_n, gpre_squeeze, full((pixels, mid)), whole, blocks, 1), order_squeeze
    )
    g_both = after(g_both, s_squeeze_grad.keep)
    token = s_squeeze_grad.moves.pop(0)(g_both)

    gpre_expand, gpre_short, grad_spatial, gsum = call(
        expand_back_kernel,
        (blocks,),
        [
            wide_spec, wide_spec, wide_spec, e_spec, s_spec, tile_n(rows=16), count_spec, p_expand, p_short,
            mask_spec, cols(mid, TILE), mid_spec, all_tiles, p_spatial,
        ],
        [wide_spec, wide_spec, mid_spec, all_tiles],
        [shaped((pixels, c_out), BF16), shaped((pixels, c_out), BF16), mid_f32, one_tile],
        flops=2 * pixels * mid * c_out, nbytes=11 << 20,
    )(
        grad_joined, pre_expand, pre_short, s_both, s_both, g_both, s_reduce, params, params, mask, w_expand,
        pre_spatial, s_spatial, params,
    )
    s_expand_grad = halving(
        outer_halves(core, act_spatial, left_const, gpre_expand, right_n, whole, blocks, blocks), order_expand
    )
    s_short_grad = [
        halving(
            outer_halves(
                core, planes.reshape(4 * pixels, c_in), pl.BlockSpec((pixels, TILE), lambda b, *_, k=k: (0, k)),
                gpre_short, right_n, whole, blocks, blocks,
            ),
            order_short[k % 2],
        )
        for k in range(in_blocks)
    ]
    g_spatial = after(
        sync(gsum), s_expand_grad.keep, [s.keep for s in s_short_grad], s_squeeze_grad.received
    )
    for stream in [s_expand_grad] + s_short_grad:
        token = stream.moves.pop(0)(g_spatial)

    gshift_spatial, grad_reduce, gsum = call(
        functools.partial(spatial_back_kernel, width, height),
        (3,),
        [
            mid_spec, mid_spec, all_tiles, all_tiles, count_spec, p_spatial, mask_spec, tap_spec,
            full((4, pixels, mid)), all_tiles, p_reduce,
        ],
        [full((4, pixels, mid)), full((4, pixels, mid)), all_tiles],
        [shaped((4, pixels, mid), BF16), shaped((4, pixels, mid)), one_tile],
        flops=18 * pixels * mid * mid, nbytes=12 << 20,
    )(grad_spatial, pre_spatial, s_spatial, g_spatial, s_reduce, params, mask, w_spatial, pre_reduce, s_reduce, params)
    order_spatial, order_reduce = (xs + ys + zs, ys + xs + zs), zs[:1] + xs + ys + zs[1:]
    spatial_parts = ((0, 5), (5, 4))
    late = [
        halving(
            outer_halves(
                core, act_reduce, pl.BlockSpec((1, pixels, mid), functools.partial(spatial_plane, place)),
                gshift_spatial, full((4, pixels, mid)), functools.partial(spatial_taps, place), count, 1,
            ),
            order,
        )
        for (place, count), order in zip(spatial_parts, order_spatial)
    ]

    back_short = call(
        short_back_kernel,
        (blocks,),
        [wide_spec, cols(c_in, TILE)],
        full((pixels, c_in)),
        shaped((pixels, c_in)),
        flops=2 * pixels * c_in * c_out, nbytes=6 << 20,
    )(gpre_short, w_shortcut)
    crossed = [s.received for s in [s_expand_grad] + s_short_grad]
    g_reduce = after(sync(gsum), [s.keep for s in late], back_short, crossed)
    spread = TILE // dp
    early = Halving(early_sum.reshape(9 + blocks, spread, TILE), rep_bits, flat, devices)
    middle = [s_squeeze_grad, s_expand_grad] + s_short_grad

    reduce_back_call = call(
        functools.partial(reduce_back_kernel, quarter),
        (steps,),
        [
            plane_block(mid), plane_block(mid), all_tiles, all_tiles, count_spec, p_reduce,
            pl.BlockSpec((quarter, LANES), lambda k: (k, 0)), full((c_in, mid)),
            pl.BlockSpec((quarter, c_in), lambda k: (k, 0)), full(perm.shape),
        ],
        [plane_block(mid), pl.BlockSpec((4 * quarter, c_in), lambda k: (k, 0))],
        [shaped((4, pixels, mid), BF16), shaped((images * 4 * height * width, c_in), BF16)],
        flops=8 * pixels * c_in * mid, nbytes=10 << 20,
    )

    def reduce_back(summed):
        return reduce_back_call(
            grad_reduce, pre_reduce, s_reduce, summed, s_reduce, params, mask, w_reduce, back_short, perm_back
        )

    last = Later()

    def input_back(token):
        gpre_reduce, last.image_grad = reduce_back(after(g_reduce, token))
        stream = halving(
            outer_halves(
                core, planes.reshape(4 * pixels, c_in), pl.BlockSpec((4 * pixels, TILE), lambda b, *_: (0, b)),
                gpre_reduce.reshape(4 * pixels, mid), full((4 * pixels, mid)), whole, in_blocks, 1,
            ),
            order_reduce,
        )
        last.stream = stream
        last.moves.extend(stream.moves)
        return stream.keep

    tall, flat_cols = lambda b: (b, 0), lambda b: (0, b)
    def starts_of(first, order, rows):
        found = []
        for k in range(devices):
            start, left = first(k), rows
            for bit in order:
                left //= 2
                start += (k // bit % 2) * left
            found.append(start)
        return tuple(found)

    spread_starts = starts_of(lambda k: (k // rep) * spread, rep_bits, spread)
    early_out = Early(early, functools.partial(regroup, starts=spread_starts, total=9 + blocks))
    early_out.add_result(place=0, blocks=blocks, shape=(mid, c_out), where=flat_cols)
    early_out.add_result(place=blocks, blocks=9, shape=(9 * mid, mid), where=tall)
    backs = [Return(stream, core_bit, flat, devices) for stream in late]
    for stream, back in zip(late, backs):
        stream.moves.extend(back.moves)
    input_step = Later()
    input_step.moves.append(input_back)
    token = run_streams(middle + late + [last, early, early_out, input_step], SCHEDULE, g_reduce)

    def gathered(shard):
        everything = lax.all_gather(shard.reshape(-1, TILE), AXES, axis=0, tiled=False)
        return functools.partial(regroup, everything, total=shard.shape[0])

    grad_w_widen, grad_w_window = early_out.results

    half_starts = lambda order: starts_of(lambda k: (k // core_bit % 2) * (TILE // 2), order, TILE // 2)
    regrouped = gathered(jnp.concatenate([s.keep for s in middle + [last.stream]], axis=0))
    grad_w_squeeze = regrouped(half_starts(order_squeeze), place=0, blocks=blocks, shape=(c_out, mid), where=tall)
    grad_w_expand = regrouped(
        half_starts(order_expand), place=blocks, blocks=blocks, shape=(mid, c_out), where=flat_cols
    )
    grad_w_short = None
    for k in range(in_blocks):
        grad_w_short = regrouped(
            half_starts(order_short[k % 2]), place=(2 + k) * blocks, blocks=blocks, shape=(c_in, c_out),
            where=lambda b, k=k: (k, b), into=grad_w_short,
        )

    grad_w_spatial = None
    for (place, count), back in zip(spatial_parts, backs):
        grad_w_spatial = assemble(
            back.places(), back.pieces(), 0, count, (9 * mid, mid), lambda b, place=place: (place + b, 0),
            into=grad_w_spatial,
        )
    grad_w_reduce = regrouped(
        half_starts(order_reduce), place=(2 + in_blocks) * blocks, blocks=in_blocks, shape=(c_in, mid), where=tall
    )
    grad_w_window, grad_w_spatial = (g.reshape(3, 3, mid, mid) for g in (grad_w_window, grad_w_spatial))

    shift_total = vector(g_both, 0, 16)
    return (
        block_out.reshape(cotangent.shape),
        last.image_grad.reshape(image_input.shape),
        grad_w_reduce,
        grad_w_spatial,
        grad_w_expand,
        grad_w_short,
        vector(jnp.sum(g_reduce, axis=0), ROWS, 8),
        vector(jnp.sum(g_reduce, axis=0), 0, 8),
        vector(jnp.sum(g_spatial, axis=0), ROWS, 8),
        vector(jnp.sum(g_spatial, axis=0), 0, 8),
        vector(g_both, ROWS, 16),
        shift_total,
        vector(g_both, 2 * ROWS, 16),
        shift_total,
        grad_w_squeeze,
        grad_w_window,
        grad_w_widen,
        vector(jnp.sum(g_squeeze, axis=0), ROWS, 8),
        vector(jnp.sum(g_squeeze, axis=0), 0, 8),
        vector(jnp.sum(g_window, axis=0), ROWS, 8),
        vector(jnp.sum(g_window, axis=0), 0, 8),
        vector(g_widen, ROWS, 8),
        vector(g_widen, 0, 8),
    )


def solution(mesh):
    split = P(AXES, None, None, None)
    return jax.shard_map(
        functools.partial(on_device, mesh.shape["dp"], mesh.shape["rep"]),
        mesh=mesh,
        in_specs=(split, P(AXES), P(AXES)) + (P(),) * 21 + (split,),
        out_specs=(split, split) + (P(),) * 21,
        check_vma=False,
    )
```

```python
import functools

import jax
import jax.numpy as jnp
import numpy as np
from jax import lax
from jax.experimental import pallas as pl
from jax.experimental.pallas import tpu as pltpu
from jax.sharding import PartitionSpec as P

EPSILON = 1e-05
F32 = jnp.float32
BF16 = jnp.bfloat16
AXES = ("dp", "rep")
LANES = 128
TILE = 512
ROWS = TILE // LANES
MIB = 60
SCHEDULE = (
    0, 1, 2, 3, 7, 4, 5, 9, 0, 1, 7, 6, 2, 3, 7, 6, 0, 1, 2, 3, 4, 5, 6, 0, 1, 6, 2, 3, 5, 4,
    6, 0, 1, 2, 3, 6, 5, 4, 5, 4, 5, 4, 5, 4, 5, 4, 5, 4, 8, 5, 4, 8, 5, 4,
)


def dot(left, right):
    return jnp.dot(left, right, preferred_element_type=F32)


def dot_nt(left, right):
    return lax.dot_general(left, right, (((1,), (1,)), ((), ())), preferred_element_type=F32)


def pack(vector):
    return jnp.concatenate(
        [vector[:, LANES * k : LANES * (k + 1)] for k in range(vector.shape[1] // LANES)], axis=0
    )


def unpack(rows):
    return jnp.concatenate([rows[k : k + 1, :] for k in range(rows.shape[0])], axis=1)


def col_sum(values):
    return jnp.sum(values, axis=0, keepdims=True)


def stat_tile(first, second):
    return jnp.concatenate([pack(col_sum(first)), pack(col_sum(second))], axis=0)


def put(ref, tile):
    ref[...] = jnp.broadcast_to(tile, ref.shape)


def total(ref):
    return ref[...] if len(ref.shape) == 2 else jnp.sum(ref[...], axis=0)


def coefficients(stat_ref, count_ref, param_ref, factor=1.0):
    stat, param = total(stat_ref), param_ref[...]
    count = total(count_ref)[0:ROWS, :] * factor
    average = stat[0:ROWS] / count
    inverse = lax.rsqrt(stat[ROWS : 2 * ROWS] / count - average * average + EPSILON)
    return (
        unpack(average),
        unpack(inverse),
        unpack(param[0:ROWS]),
        unpack(param[ROWS : 2 * ROWS]),
    )


def back_coefficients(grad_rows_shift, grad_rows_gain, count_ref, factor=1.0):
    count = total(count_ref)[0:ROWS, :] * factor
    return unpack(grad_rows_shift / count), unpack(grad_rows_gain / count)


def logistic(values):
    return 0.5 * jnp.tanh(0.5 * values) + 0.5


def silu(values):
    return values * logistic(values)


def slope(values):
    gate = logistic(values)
    return gate * (1.0 + values * (1.0 - gate))


def column(mask_ref):
    return mask_ref[:, 0:1]


def pixel_ids(pixels, width):
    return lax.broadcasted_iota(jnp.int32, (pixels, 1), 0)


def shift_cols(values, step, width):
    pixels = values.shape[0]
    place = lax.rem(pixel_ids(pixels, width), width)
    rolled = pltpu.roll(values, (-step) % pixels, 0)
    keep = place < width - step if step > 0 else place >= -step
    return jnp.where(keep, rolled, 0.0)


def shift_rows(values, step, width, height):
    pixels = values.shape[0]
    place = lax.rem(lax.div(pixel_ids(pixels, width), width), height)
    rolled = pltpu.roll(values, (-step * width) % pixels, 0)
    keep = place < height - step if step > 0 else place >= -step
    return jnp.where(keep, rolled, 0.0)


def full(shape):
    zeros = (0,) * len(shape)
    return pl.BlockSpec(shape, lambda *_: zeros)


def cols(rows, width):
    return pl.BlockSpec((rows, width), lambda n, *_: (0, n))


def tile_at(index, rows=8):
    return pl.BlockSpec((rows, LANES), lambda *_: (index, 0))


def tile_n(offset=0, rows=8):
    return pl.BlockSpec((rows, LANES), lambda n, *_: (offset + n, 0))


def call(kernel, grid, in_specs, out_specs, out_shape, scratch=(), mib=MIB, flops=0, nbytes=0):
    return pl.pallas_call(
        kernel,
        grid=grid,
        in_specs=in_specs,
        out_specs=out_specs,
        out_shape=out_shape,
        scratch_shapes=scratch,
        compiler_params=pltpu.CompilerParams(
            vmem_limit_bytes=mib << 20, dimension_semantics=("arbitrary",) * len(grid)
        ),
        cost_estimate=pl.CostEstimate(flops=flops, bytes_accessed=nbytes, transcendentals=0),
    )


def shaped(shape, dtype=F32):
    return jax.ShapeDtypeStruct(shape, dtype)


def reduce_kernel(quarter, x_ref, perm_ref, mask_ref, all_mask_ref, w_ref, xp_ref, pre_ref, stat_ref, acc_ref):
    step = pl.program_id(0)
    mask = column(mask_ref)
    masking = jnp.concatenate([mask] * 4, axis=0)
    planes = (dot(perm_ref[...], x_ref[...]) * masking).astype(BF16)
    pre = dot(planes, w_ref[...])
    for q in range(4):
        xp_ref[q] = planes[q * quarter : (q + 1) * quarter]
        pre_ref[q] = pre[q * quarter : (q + 1) * quarter]

    @pl.when(step == 0)
    def _():
        acc_ref[...] = jnp.zeros_like(acc_ref)

    acc_ref[0:1, :] += col_sum(pre)
    acc_ref[1:2, :] += col_sum(pre * pre)

    @pl.when(step == pl.num_programs(0) - 1)
    def _():
        count = jnp.broadcast_to(col_sum(all_mask_ref[...]), (8, LANES))
        put(stat_ref, jnp.concatenate([pack(acc_ref[0:1, :]), pack(acc_ref[1:2, :]), count], axis=0))


def product_kernel(x_ref, w_ref, out_ref, stat_ref):
    pre = dot(x_ref[0], w_ref[...])
    out_ref[...] = pre
    stat_ref[...] = stat_tile(pre, pre * pre)


def spatial_kernel(width, height, pre_ref, stat_ref, count_ref, param_ref, mask_ref, w_ref, act_ref, out_ref, out_stat_ref, y_ref):
    r = pl.program_id(0)
    mask = column(mask_ref)

    @pl.when(r == 0)
    def _():
        average, inverse, gain, shift = coefficients(stat_ref, count_ref, param_ref, 4.0)
        for q in range(4):
            norm = (pre_ref[q] - average) * inverse * gain + shift
            act_ref[q] = (silu(norm) * mask).astype(BF16)

    row_parity = jnp.where(r == 1, 0, 1)
    row_shift = jnp.where(r == 0, 1, 0)
    even, odd = act_ref[2 * row_parity], act_ref[2 * row_parity + 1]
    straight = dot(even, w_ref[0, 1]) + dot(odd, w_ref[0, 2])
    moved = dot(odd, w_ref[0, 0])

    @pl.when(r < 2)
    def _():
        y_ref[2 * row_shift] = straight
        y_ref[2 * row_shift + 1] = moved

    @pl.when(r == 2)
    def _():
        upper = y_ref[2] + shift_cols(y_ref[3], -1, width)
        lower = y_ref[0] + straight + shift_cols(y_ref[1] + moved, -1, width)
        pre = lower + shift_rows(upper, -1, width, height)
        out_ref[...] = pre
        masked = pre * mask
        put(out_stat_ref, stat_tile(masked, masked * pre))


def expand_kernel(pre_ref, stat_ref, count_ref, param_ref, mask_ref, w_ref, act_ref, out_ref, out_stat_ref):
    @pl.when(pl.program_id(0) == 0)
    def _():
        average, inverse, gain, shift = coefficients(stat_ref, count_ref, param_ref)
        norm = (pre_ref[...] - average) * inverse * gain + shift
        act_ref[...] = (silu(norm) * column(mask_ref)).astype(BF16)

    pre = dot(act_ref[...], w_ref[...])
    out_ref[...] = pre
    put(out_stat_ref, stat_tile(pre, pre * pre))


def join_kernel(pe_ref, ps_ref, se_ref, ss_ref, count_ref, qe_ref, qs_ref, mask_ref, w_ref, first_ref, out_ref, out_stat_ref):
    n = pl.program_id(0)
    average_e, inverse_e, gain_e, shift_e = coefficients(se_ref, count_ref, qe_ref)
    average_s, inverse_s, gain_s, shift_s = coefficients(ss_ref, count_ref, qs_ref)
    joined = (pe_ref[...] - average_e) * inverse_e * gain_e + shift_e
    joined += (ps_ref[...] - average_s) * inverse_s * gain_s + shift_s
    first = (silu(joined) * column(mask_ref)).astype(BF16)
    first_ref[...] = first
    part = dot(first, w_ref[...])

    @pl.when(n == 0)
    def _():
        out_ref[...] = part

    @pl.when(n > 0)
    def _():
        out_ref[...] += part

    @pl.when(n == pl.num_programs(0) - 1)
    def _():
        pre = out_ref[...]
        put(out_stat_ref, stat_tile(pre, pre * pre))


def store_padded(target_ref, values, step, width, height, images):
    area = width * height
    channels = values.shape[1]
    zeros = jnp.zeros((width, channels), BF16)
    for k in range(3):
        moved = values if k == 1 else shift_cols(values, step * (k - 1), width)
        moved = moved.astype(BF16)
        for b in range(images):
            target_ref[k, b, 0:width, :] = zeros
            target_ref[k, b, area + width : area + 2 * width, :] = zeros
            target_ref[k, b, width : area + width, :] = moved[b * area : (b + 1) * area]


def window_rows(ref, k, first, area, images):
    return jnp.concatenate([ref[k, b, pl.ds(first, area), :] for b in range(images)], axis=0)


def window_kernel(width, height, images, pre_ref, stat_ref, count_ref, param_ref, mask_ref, w_ref, act_ref, out_ref, out_stat_ref, pad_ref):
    r = pl.program_id(0)

    @pl.when(r == 0)
    def _():
        average, inverse, gain, shift = coefficients(stat_ref, count_ref, param_ref)
        norm = (pre_ref[...] - average) * inverse * gain + shift
        act = silu(norm) * column(mask_ref)
        act_ref[...] = act.astype(BF16)
        store_padded(pad_ref, act, 1, width, height, images)

    first = pl.multiple_of(r * width, width)
    part = dot(window_rows(pad_ref, 0, first, width * height, images), w_ref[0, 0])
    for k in (1, 2):
        part += dot(window_rows(pad_ref, k, first, width * height, images), w_ref[0, k])

    @pl.when(r == 0)
    def _():
        out_ref[...] = part

    @pl.when(r > 0)
    def _():
        out_ref[...] += part

    @pl.when(r == 2)
    def _():
        pre = out_ref[...]
        masked = pre * column(mask_ref)
        put(out_stat_ref, stat_tile(masked, masked * pre))


def final_kernel(pre_ref, stat_ref, count_ref, param_ref, mask_ref, first_ref, cot_ref, out_ref, grad_ref, sum_ref):
    average, inverse, gain, shift = coefficients(stat_ref, count_ref, param_ref)
    mask = column(mask_ref)
    hat = (pre_ref[...] - average) * inverse
    final = hat * gain + shift + first_ref[...].astype(F32)
    gate = logistic(final)
    out_ref[...] = (final * gate * mask).astype(BF16)
    grad = cot_ref[...].astype(F32) * mask * (gate * (1.0 + final * (1.0 - gate)))
    grad_ref[...] = grad
    put(sum_ref, stat_tile(grad, grad * hat))


def norm_back(grad, hat, scale, shift_term, gain_term, mask):
    return ((grad - mask * (shift_term + hat * gain_term)) * scale).astype(BF16)


def widen_back_kernel(
    grad_ref, pre_ref, stat_ref, gsum_ref, count_ref, param_ref, mask_ref, w_ref, in_ref, in_stat_ref, in_param_ref,
    gpre_ref, out_ref, sum_ref,
):
    n = pl.program_id(0)
    mask = column(mask_ref)
    average, inverse, gain, _ = coefficients(stat_ref, count_ref, param_ref)
    gsum = total(gsum_ref)
    shift_term, gain_term = back_coefficients(gsum[0:ROWS], gsum[ROWS : 2 * ROWS], count_ref)
    hat = (pre_ref[...] - average) * inverse
    gpre = norm_back(grad_ref[...], hat, inverse * gain, shift_term, gain_term, mask)
    gpre_ref[...] = gpre
    part = dot_nt(gpre, w_ref[...])

    @pl.when(n == 0)
    def _():
        out_ref[...] = part

    @pl.when(n > 0)
    def _():
        out_ref[...] += part

    @pl.when(n == pl.num_programs(0) - 1)
    def _():
        finish_back(in_ref[...], in_stat_ref, count_ref, in_param_ref, mask, out_ref, sum_ref)


def finish_back(pre, stat_ref, count_ref, param_ref, mask, out_ref, sum_ref):
    average, inverse, gain, shift = coefficients(stat_ref, count_ref, param_ref)
    hat = (pre - average) * inverse
    grad = out_ref[...] * mask * slope(hat * gain + shift)
    out_ref[...] = grad
    put(sum_ref, stat_tile(grad, grad * hat))


def pre_grad(grad_ref, pre_ref, stat_ref, gsum_ref, count_ref, param_ref, mask):
    average, inverse, gain, _ = coefficients(stat_ref, count_ref, param_ref)
    gsum = total(gsum_ref)
    shift_term, gain_term = back_coefficients(gsum[0:ROWS], gsum[ROWS : 2 * ROWS], count_ref)
    hat = (pre_ref[...] - average) * inverse
    return norm_back(grad_ref[...], hat, inverse * gain, shift_term, gain_term, mask)


def window_back_kernel(
    width, height, images,
    grad_ref, pre_ref, stat_ref, gsum_ref, count_ref, param_ref, mask_ref, w_ref, in_ref, in_stat_ref, in_param_ref,
    pad_ref, out_ref, sum_ref,
):
    r = pl.program_id(0)
    mask = column(mask_ref)

    @pl.when(r == 0)
    def _():
        gpre = pre_grad(grad_ref, pre_ref, stat_ref, gsum_ref, count_ref, param_ref, mask)
        store_padded(pad_ref, gpre.astype(F32), -1, width, height, images)

    first = pl.multiple_of((2 - r) * width, width)
    part = dot_nt(window_rows(pad_ref, 0, first, width * height, images), w_ref[0, 0])
    for k in (1, 2):
        part += dot_nt(window_rows(pad_ref, k, first, width * height, images), w_ref[0, k])

    @pl.when(r == 0)
    def _():
        out_ref[...] = part

    @pl.when(r > 0)
    def _():
        out_ref[...] += part

    @pl.when(r == 2)
    def _():
        finish_back(in_ref[...], in_stat_ref, count_ref, in_param_ref, mask, out_ref, sum_ref)


def squeeze_back_kernel(
    grad_ref, pre_ref, stat_ref, gsum_ref, count_ref, param_ref, mask_ref, w_ref,
    gfinal_ref, pe_ref, ps_ref, se_ref, ss_ref, qe_ref, qs_ref,
    gpre_ref, gj_ref, sum_ref,
):
    mask = column(mask_ref)

    @pl.when(pl.program_id(0) == 0)
    def _():
        gpre_ref[...] = pre_grad(grad_ref, pre_ref, stat_ref, gsum_ref, count_ref, param_ref, mask)

    gfirst = gfinal_ref[...] + dot_nt(gpre_ref[...], w_ref[...])
    average_e, inverse_e, gain_e, shift_e = coefficients(se_ref, count_ref, qe_ref)
    average_s, inverse_s, gain_s, shift_s = coefficients(ss_ref, count_ref, qs_ref)
    hat_e = (pe_ref[...] - average_e) * inverse_e
    hat_s = (ps_ref[...] - average_s) * inverse_s
    joined = hat_e * gain_e + shift_e + (hat_s * gain_s + shift_s)
    grad = gfirst * mask * slope(joined)
    gj_ref[...] = grad
    sum_ref[...] = jnp.concatenate(
        [stat_tile(grad, grad * hat_e), pack(col_sum(grad * hat_s)), jnp.zeros((ROWS, LANES), F32)], axis=0
    )


def expand_back_kernel(
    gj_ref, pe_ref, ps_ref, se_ref, ss_ref, gsum_ref, count_ref, qe_ref, qs_ref, mask_ref, w_ref,
    in_ref, in_stat_ref, in_param_ref,
    ge_ref, gs_ref, out_ref, sum_ref,
):
    n = pl.program_id(0)
    mask = column(mask_ref)
    average_e, inverse_e, gain_e, _ = coefficients(se_ref, count_ref, qe_ref)
    average_s, inverse_s, gain_s, _ = coefficients(ss_ref, count_ref, qs_ref)
    gsum = total(gsum_ref)
    shift_term, gain_e_term = back_coefficients(gsum[0:ROWS], gsum[ROWS : 2 * ROWS], count_ref)
    _, gain_s_term = back_coefficients(gsum[0:ROWS], gsum[2 * ROWS : 3 * ROWS], count_ref)
    grad = gj_ref[...]
    hat_e = (pe_ref[...] - average_e) * inverse_e
    hat_s = (ps_ref[...] - average_s) * inverse_s
    ge = norm_back(grad, hat_e, inverse_e * gain_e, shift_term, gain_e_term, mask)
    ge_ref[...] = ge
    gs_ref[...] = norm_back(grad, hat_s, inverse_s * gain_s, shift_term, gain_s_term, mask)
    part = dot_nt(ge, w_ref[...])

    @pl.when(n == 0)
    def _():
        out_ref[...] = part

    @pl.when(n > 0)
    def _():
        out_ref[...] += part

    @pl.when(n == pl.num_programs(0) - 1)
    def _():
        finish_back(in_ref[...], in_stat_ref, count_ref, in_param_ref, mask, out_ref, sum_ref)


def spatial_back_kernel(
    width, height,
    grad_ref, pre_ref, stat_ref, gsum_ref, count_ref, param_ref, mask_ref, w_ref, in_ref, in_stat_ref, in_param_ref,
    shift_ref, out_ref, sum_ref,
):
    r = pl.program_id(0)
    mask = column(mask_ref)

    @pl.when(r == 0)
    def _():
        gpre = pre_grad(grad_ref, pre_ref, stat_ref, gsum_ref, count_ref, param_ref, mask).astype(F32)
        below = shift_rows(gpre, 1, width, height)
        shift_ref[0] = gpre.astype(BF16)
        shift_ref[1] = shift_cols(gpre, 1, width).astype(BF16)
        shift_ref[2] = below.astype(BF16)
        shift_ref[3] = shift_cols(below, 1, width).astype(BF16)

    row_parity = jnp.where(r == 1, 0, 1)
    row_shift = jnp.where(r == 0, 1, 0)
    straight, moved = shift_ref[2 * row_shift], shift_ref[2 * row_shift + 1]
    even = dot_nt(straight, w_ref[0, 1])
    odd = dot_nt(moved, w_ref[0, 0]) + dot_nt(straight, w_ref[0, 2])

    @pl.when(r < 2)
    def _():
        out_ref[2 * row_parity] = even
        out_ref[2 * row_parity + 1] = odd

    @pl.when(r == 2)
    def _():
        out_ref[2] += even
        out_ref[3] += odd
        average, inverse, gain, shift = coefficients(in_stat_ref, count_ref, in_param_ref, 4.0)
        whole_sum = whole_hat = jnp.zeros((1, out_ref.shape[2]), F32)
        for q in range(4):
            hat = (in_ref[q] - average) * inverse
            grad = out_ref[q] * mask * slope(hat * gain + shift)
            out_ref[q] = grad
            whole_sum += col_sum(grad)
            whole_hat += col_sum(grad * hat)
        put(sum_ref, jnp.concatenate([pack(whole_sum), pack(whole_hat)], axis=0))


def short_back_kernel(g_ref, w_ref, out_ref):
    part = dot_nt(g_ref[...], w_ref[...])

    @pl.when(pl.program_id(0) == 0)
    def _():
        out_ref[...] = part

    @pl.when(pl.program_id(0) > 0)
    def _():
        out_ref[...] += part


def reduce_back_kernel(
    quarter, grad_ref, pre_ref, stat_ref, gsum_ref, count_ref, param_ref, mask_ref, w_ref, short_ref, perm_ref,
    gpre_ref, out_ref,
):
    mask = column(mask_ref)
    masking = jnp.concatenate([mask] * 4, axis=0)
    average, inverse, gain, _ = coefficients(stat_ref, count_ref, param_ref, 4.0)
    gsum = total(gsum_ref)
    shift_term, gain_term = back_coefficients(gsum[0:ROWS], gsum[ROWS : 2 * ROWS], count_ref, 4.0)
    grad = jnp.concatenate([grad_ref[q] for q in range(4)], axis=0)
    pre = jnp.concatenate([pre_ref[q] for q in range(4)], axis=0)
    hat = (pre - average) * inverse
    gpre = norm_back(grad, hat, inverse * gain, shift_term, gain_term, masking)
    for q in range(4):
        gpre_ref[q] = gpre[q * quarter : (q + 1) * quarter]
    image = dot_nt(gpre, w_ref[...])
    image = jnp.concatenate([image[0:quarter] + short_ref[...], image[quarter:]], axis=0)
    image = (image * masking).astype(BF16)
    out_ref[...] = dot(perm_ref[...], image).astype(BF16)


def turn_left(left_ref, turned_ref, per_left):
    @pl.when(lax.rem(pl.program_id(0), per_left) == 0)
    def _():
        left = left_ref[...] if len(left_ref.shape) == 2 else left_ref[0]
        turned_ref[...] = left.T


def halves_kernel(pick, per_left, core_ref, left_ref, right_ref, keep_ref, send_ref, turned_ref):
    turn_left(left_ref, turned_ref, per_left)
    half = TILE // 2
    right = pick(right_ref, pl.program_id(0))
    mine = pl.multiple_of(core_ref[0] * half, half)
    away = pl.multiple_of((1 - core_ref[0]) * half, half)
    send_ref[0] = dot(turned_ref[pl.ds(away, half), :], right)
    keep_ref[0] = dot(turned_ref[pl.ds(mine, half), :], right)


def outer_halves(core, left, left_spec, right, right_spec, pick, blocks, per_left):
    half = TILE // 2
    pixels = left_spec.block_shape[-2]
    shape = shaped((blocks, half, TILE))
    out_spec = pl.BlockSpec((1, half, TILE), lambda b, *_: (b, 0, 0))
    return pl.pallas_call(
        functools.partial(halves_kernel, pick, per_left),
        grid_spec=pltpu.PrefetchScalarGridSpec(
            num_scalar_prefetch=1,
            grid=(blocks,),
            in_specs=[left_spec, right_spec],
            out_specs=[out_spec, out_spec],
            scratch_shapes=[pltpu.VMEM((TILE, pixels), BF16)],
        ),
        out_shape=[shape, shape],
        compiler_params=outer_params(),
        cost_estimate=outer_cost(blocks, pixels),
    )(core, left, right)


def outer_params():
    return pltpu.CompilerParams(vmem_limit_bytes=MIB << 20, dimension_semantics=("arbitrary",))


def outer_cost(blocks, pixels):
    return pl.CostEstimate(
        flops=2 * blocks * pixels * TILE * TILE, bytes_accessed=blocks * TILE * TILE * 4, transcendentals=0
    )


def spread_kernel(pick, per_left, left_ref, right_ref, *refs):
    out_ref, turned_ref = refs[-2], refs[-1]
    turn_left(left_ref, turned_ref, per_left)
    out_ref[...] = dot(turned_ref[...], pick(right_ref, pl.program_id(0))).reshape(out_ref.shape)


def outer_spread(shares, left, left_spec, right, right_spec, pick, blocks, per_left, place, total, into):
    rows = TILE // shares
    pixels = left_spec.block_shape[-2]
    extra = () if into is None else (into,)
    return pl.pallas_call(
        functools.partial(spread_kernel, pick, per_left),
        grid=(blocks,),
        in_specs=[left_spec, right_spec] + [pl.BlockSpec(memory_space=pl.ANY)] * len(extra),
        out_specs=pl.BlockSpec((shares, rows, TILE), lambda b: (0, place + b, 0)),
        out_shape=shaped((shares, total * rows, TILE)),
        scratch_shapes=[pltpu.VMEM((TILE, pixels), BF16)],
        input_output_aliases={2: 0} if extra else {},
        compiler_params=outer_params(),
        cost_estimate=outer_cost(blocks, pixels),
    )(left, right, *extra)


def assemble_kernel(chunks, place_ref, own_ref, near_ref, far_ref, both_ref, *refs):
    out_ref = refs[-1]
    rows = TILE // 4 // chunks
    for k, ref in enumerate((own_ref, near_ref, far_ref, both_ref)):
        for c in range(chunks):
            start = pl.multiple_of(place_ref[k * chunks + c], rows)
            out_ref[pl.ds(start, rows), :] = ref[0, c * rows : (c + 1) * rows, :]


def assemble(places, pieces, first, blocks, shape, where, chunks=1, into=None):
    in_spec = pl.BlockSpec((1, TILE // 4, TILE), lambda b, *_: (first + b, 0, 0))
    extra = () if into is None else (into,)
    return pl.pallas_call(
        functools.partial(assemble_kernel, chunks),
        grid_spec=pltpu.PrefetchScalarGridSpec(
            num_scalar_prefetch=1,
            grid=(blocks,),
            in_specs=[in_spec] * 4 + [pl.BlockSpec(memory_space=pl.ANY)] * len(extra),
            out_specs=pl.BlockSpec((TILE, TILE), lambda b, *_: where(b)),
        ),
        out_shape=shaped(shape),
        input_output_aliases={5: 0} if extra else {},
        compiler_params=outer_params(),
        cost_estimate=pl.CostEstimate(
            flops=0, bytes_accessed=2 * blocks * TILE * TILE * 4, transcendentals=0
        ),
    )(places, *pieces, *extra)


def regroup_kernel(starts, rows, down, in_ref, *refs):
    out_ref = refs[-1]
    for j in range(in_ref.shape[1] // rows):
        base, col = (j * TILE, 0) if down else (0, j * TILE)
        for k, start in enumerate(starts):
            out_ref[base + start : base + start + rows, col : col + TILE] = in_ref[k, j * rows : (j + 1) * rows, :]


def regroup(gathered, starts, total, place, blocks, shape, down, first=0, into=None):
    devices, rows = gathered.shape[0], gathered.shape[1] // total
    extra = () if into is None else (into,)
    if rows % 8:
        order = np.argsort(np.asarray(starts))
        gathered = gathered.reshape(devices, total, rows, TILE)[order].transpose(1, 0, 2, 3)
        gathered = gathered.reshape(1, total * TILE, TILE)
        devices, rows, starts = 1, TILE, (0,)
    pair = 2 if all(n % 2 == 0 for n in (place, blocks, first if down else 0)) else 1
    out_block = (pair * TILE, TILE) if down else (TILE, pair * TILE)
    where = (lambda b: (first // pair + b, 0)) if down else (lambda b: (first, b))
    return pl.pallas_call(
        functools.partial(regroup_kernel, starts, rows, down),
        grid=(blocks // pair,),
        in_specs=[pl.BlockSpec((devices, pair * rows, TILE), lambda b: (0, place // pair + b, 0))]
        + [pl.BlockSpec(memory_space=pl.ANY)] * len(extra),
        out_specs=pl.BlockSpec(out_block, where),
        out_shape=shaped(shape),
        input_output_aliases={1: 0} if extra else {},
        compiler_params=outer_params(),
        cost_estimate=pl.CostEstimate(
            flops=0, bytes_accessed=2 * blocks * TILE * TILE * 4, transcendentals=0
        ),
    )(gathered, *extra)


def bits_of(first, size):
    found = []
    while size > 1:
        found.append(first)
        first, size = first * 2, size // 2
    return found


def mesh_bits(dp, rep):
    side = int(round(dp**0.5))
    if side * side == dp:
        return 1, bits_of(rep, side), bits_of(rep * side, side), bits_of(2, rep // 2)
    side = int(round((dp // 2) ** 0.5))
    return rep, bits_of(2 * rep, side), bits_of(2 * rep * side, side), bits_of(1, rep)


def swap(values, bit, devices):
    return lax.ppermute(values, AXES, [(i, i ^ bit) for i in range(devices)])


def sync_all(tile, devices):
    return lax.all_to_all(tile, AXES, 0, 0, tiled=True)


def sync_hops(tile, rounds, devices):
    for bits in rounds:
        near = [swap(tile, bit, devices) for bit in bits]
        if len(bits) == 2:
            across = swap(tile, bits[0] + bits[1], devices)
            tile = (tile + near[0]) + (near[1] + across)
        else:
            tile = tile + near[0]
    return tile


def device_bit(flat, bit):
    return lax.rem(lax.div(flat, bit), 2)


def after(values, *others):
    return lax.optimization_barrier((values,) + others)[0]


def half_sum(keep, received, which):
    rows = keep.shape[1] // 2
    first = lax.dynamic_slice_in_dim(keep, which * rows, rows, axis=1)
    return first + lax.dynamic_slice_in_dim(received, which * rows, rows, axis=1)


def join_halves(own, values, other):
    return jnp.where(
        own == 0, jnp.concatenate([values, other], axis=1), jnp.concatenate([other, values], axis=1)
    )


class Halving:
    def __init__(self, keep, order, flat, devices, send=None, core=None):
        self.keep, self.order, self.flat, self.devices = keep, list(order), flat, devices
        self.received = None
        self.moves = []
        if send is not None:
            self.moves.append(lambda token: self.cross(send, core, token))
        self.moves += [functools.partial(self.halve, bit) for bit in self.order] + [self.add]

    def cross(self, send, core, token):
        send = after(send, token)
        self.received = swap(send, core, self.devices)
        return send

    def halve(self, bit, token):
        own = device_bit(self.flat, bit)
        if self.received is None:
            keep, rows = after(self.keep, token), self.keep.shape[1] // 2
            send = lax.dynamic_slice_in_dim(keep, (1 - own) * rows, rows, axis=1)
            self.received = swap(send, bit, self.devices)
            self.keep = lax.dynamic_slice_in_dim(keep, own * rows, rows, axis=1)
            return send
        keep, received = after((self.keep, self.received), token)
        send = half_sum(keep, received, 1 - own)
        self.received = swap(send, bit, self.devices)
        keep, received = after((keep, received), send)
        self.keep = half_sum(keep, received, own)
        return send

    def add(self, token):
        keep, received = after((self.keep, self.received), token)
        self.keep = keep + received
        return self.keep


class Return:
    def __init__(self, source, core, flat, devices):
        self.source, self.core, self.flat, self.devices = source, core, flat, devices
        self.order = source.order
        back = list(reversed(self.order))
        self.moves = [functools.partial(self.widen, a, b) for a, b in zip([None] + back[:-1], back)]
        self.moves.append(self.cross)

    def widen(self, joined, bit, token):
        if joined is None:
            self.own = after(self.source.keep, token)
        else:
            own, other = after((self.own, self.near), token)
            self.own = join_halves(device_bit(self.flat, joined), own, other)
        self.near = swap(self.own, bit, self.devices)
        if bit == self.order[0]:
            self.far = swap(self.own, self.core, self.devices)
        return self.own

    def cross(self, token):
        self.near = after(self.near, token)
        self.both = swap(self.near, self.core, self.devices)
        return self.near

    def pieces(self):
        return self.own, self.near, self.far, self.both

    def places(self):
        half, quarter = TILE // 2, TILE // 4
        core, own = device_bit(self.flat, self.core), device_bit(self.flat, self.order[0])
        return jnp.stack(
            [c * half + o * quarter for c in (core, 1 - core) for o in (own, 1 - own)]
        ).astype(jnp.int32)


class Later:
    def __init__(self):
        self.moves = []


class Early:
    def __init__(self, source, make):
        self.source, self.make, self.whole = source, make, None
        self.moves, self.results = [], []

    def add_result(self, **how):
        self.moves.append(functools.partial(self.result, how))

    def gather(self):
        self.whole = lax.all_gather(self.source.keep.reshape(-1, TILE), AXES, axis=0, tiled=False)

    def result(self, how, token):
        if self.whole is None:
            self.gather()
        self.results.append(self.make(after(self.whole, token), **how))
        return self.results[-1]


def run_streams(streams, schedule, token, to_end=True):
    for k in schedule:
        if streams[k].moves:
            token = streams[k].moves.pop(0)(token)
    while to_end and any(s.moves for s in streams):
        for s in streams:
            if s.moves:
                token = s.moves.pop(0)(token)
    return token


def permutation(width):
    size = 8 * 2 * width
    matrix = np.zeros((size, size), np.float32)
    place = 0
    for row_parity in range(2):
        for col_parity in range(2):
            for i in range(4):
                for j in range(width):
                    matrix[place, (2 * i + row_parity) * 2 * width + 2 * j + col_parity] = 1.0
                    place += 1
    return matrix


def param_tiles(gain, shift):
    blocks = gain.shape[0] // TILE
    pair = jnp.stack([gain.reshape(blocks, ROWS, LANES), shift.reshape(blocks, ROWS, LANES)], axis=1)
    return pair.reshape(blocks * 8, LANES)


def vector(tiles, first, step):
    return tiles.reshape(-1, step, LANES)[:, first : first + ROWS].reshape(-1)


def on_device(dp, rep, *arrays):
    (image_input, heights, widths, w_reduce, w_spatial, w_expand, w_shortcut,
     gain_reduce, shift_reduce, gain_spatial, shift_spatial, gain_expand, shift_expand,
     gain_shortcut, shift_shortcut, w_squeeze, w_window, w_widen,
     gain_squeeze, shift_squeeze, gain_window, shift_window, gain_widen, shift_widen, cotangent) = arrays
    images, height, width, c_out = cotangent.shape
    c_in, mid = w_reduce.shape
    pixels = images * height * width
    quarter = 64
    steps = pixels // quarter
    blocks = c_out // TILE
    devices = dp * rep
    core_bit, x_bits, y_bits, z_bits = mesh_bits(dp, rep)
    hop_rounds = [(core_bit,)] + list(zip(y_bits, x_bits))
    hop_rounds += [tuple(z_bits[k : k + 2]) for k in range(0, len(z_bits), 2)]
    xs, ys, zs, rep_bits = x_bits, y_bits, z_bits, bits_of(1, rep)
    flat = lax.axis_index(AXES)
    core = device_bit(flat, core_bit).astype(jnp.int32).reshape(1)
    sync = functools.partial(sync_all, devices=devices)
    sync_wide = functools.partial(sync_hops, rounds=hop_rounds, devices=devices)

    row_ids = lax.broadcasted_iota(jnp.int32, (1, height, 1, LANES), 1)
    col_ids = lax.broadcasted_iota(jnp.int32, (1, 1, width, LANES), 2)
    inside = (row_ids < heights[:, None, None, None]) & (col_ids < widths[:, None, None, None])
    mask = jnp.where(inside, 1.0, 0.0).astype(F32).reshape(pixels, LANES)
    params = jnp.concatenate(
        [
            param_tiles(gain_reduce, shift_reduce), param_tiles(gain_spatial, shift_spatial),
            param_tiles(gain_squeeze, shift_squeeze), param_tiles(gain_window, shift_window),
            param_tiles(gain_expand, shift_expand), param_tiles(gain_shortcut, shift_shortcut),
            param_tiles(gain_widen, shift_widen),
        ],
        axis=0,
    )
    p_reduce, p_spatial, p_squeeze, p_window = (tile_at(k) for k in range(4))
    p_expand, p_short, p_widen = (tile_n(4 + blocks * k) for k in range(3))
    turn = permutation(width)
    perm, perm_back = jnp.asarray(turn, BF16), jnp.asarray(turn.T.copy(), BF16)
    image = image_input.reshape(images * 4 * height * width, c_in)
    cot = cotangent.reshape(pixels, c_out)

    mask_spec, wide_f32 = full((pixels, LANES)), shaped((pixels, c_out))
    mid_f32, mid_spec = shaped((pixels, mid)), full((pixels, mid))
    wide_spec, tap_spec = cols(pixels, TILE), pl.BlockSpec((1, 3, mid, mid), lambda r: (r, 0, 0, 0))
    plane_block = lambda c: pl.BlockSpec((4, quarter, c), lambda k: (0, k, 0))
    area, in_blocks = width * height, c_in // TILE
    left_const = pl.BlockSpec((pixels, TILE), lambda b, *_: (0, 0))
    right_n = pl.BlockSpec((pixels, TILE), lambda b, *_: (0, b))

    def whole(ref, b):
        return ref[...]

    def window_taps(ref, b):
        r, c = lax.div(b, 3), lax.rem(b, 3)
        first = pl.multiple_of((2 - r) * width, width)
        return window_rows(ref, c, first, area, images)

    def spatial_taps(place, ref, b):
        r, c = lax.div(place + b, 3), lax.rem(place + b, 3)
        return ref[2 * jnp.where(r == 0, 1, 0) + jnp.where(c == 0, 1, 0)]

    def spatial_plane(place, b, *_):
        r, c = lax.div(place + b, 3), lax.rem(place + b, 3)
        return (2 * jnp.where(r == 1, 0, 1) + jnp.where(c == 1, 0, 1), 0, 0)

    one_tile, wide_tiles = shaped((devices, 8, LANES)), shaped((8 * blocks, LANES))
    all_tiles = full((devices, 8, LANES))
    count_spec = pl.BlockSpec((devices, 8, LANES), lambda *_: (0, 1, 0))
    padded = (3, images, (height + 2) * width, mid)

    planes, pre_reduce, stat = call(
        functools.partial(reduce_kernel, quarter),
        (steps,),
        [
            pl.BlockSpec((4 * quarter, c_in), lambda k: (k, 0)), full(perm.shape),
            pl.BlockSpec((quarter, LANES), lambda k: (k, 0)), mask_spec, full((c_in, mid)),
        ],
        [plane_block(c_in), plane_block(mid), full((devices, 16, LANES))],
        [shaped((4, pixels, c_in), BF16), shaped((4, pixels, mid)), shaped((devices, 16, LANES))],
        [pltpu.VMEM((8, mid), F32)],
        flops=8 * pixels * c_in * mid, nbytes=8 << 20,
    )(image, perm, mask, mask, w_reduce)
    s_reduce = sync(stat)

    pre_short, stat_short = call(
        product_kernel,
        (blocks,),
        [pl.BlockSpec((1, pixels, c_in), lambda n: (0, 0, 0)), cols(c_in, TILE)],
        [wide_spec, tile_n()],
        [wide_f32, wide_tiles],
        flops=2 * pixels * c_in * c_out, nbytes=6 << 20,
    )(planes, w_shortcut)

    act_reduce, pre_spatial, stat = call(
        functools.partial(spatial_kernel, width, height),
        (3,),
        [full((4, pixels, mid)), all_tiles, count_spec, p_reduce, mask_spec, tap_spec],
        [full((4, pixels, mid)), mid_spec, all_tiles],
        [shaped((4, pixels, mid), BF16), mid_f32, one_tile],
        [pltpu.VMEM((4, pixels, mid), F32)],
        flops=18 * pixels * mid * mid, nbytes=8 << 20,
    )(pre_reduce, s_reduce, s_reduce, params, mask, w_spatial)
    s_spatial = sync(stat)

    def widen_out(pre, stat, p_spec, weights):
        return call(
            expand_kernel,
            (blocks,),
            [mid_spec, all_tiles, count_spec, p_spec, mask_spec, cols(mid, TILE)],
            [mid_spec, wide_spec, tile_n()],
            [shaped((pixels, mid), BF16), wide_f32, wide_tiles],
            flops=2 * pixels * mid * c_out, nbytes=5 << 20,
        )(pre, stat, s_reduce, params, mask, weights)

    act_spatial, pre_expand, stat = widen_out(pre_spatial, s_spatial, p_spatial, w_expand)
    s_both = sync_wide(jnp.concatenate([stat, stat_short], axis=0))
    e_spec, s_spec = tile_n(), tile_n(blocks)

    first_out, pre_squeeze, stat = call(
        join_kernel,
        (blocks,),
        [
            wide_spec, wide_spec, e_spec, s_spec, count_spec, p_expand, p_short, mask_spec,
            pl.BlockSpec((TILE, mid), lambda n: (n, 0)),
        ],
        [wide_spec, mid_spec, all_tiles],
        [shaped((pixels, c_out), BF16), mid_f32, one_tile],
        flops=2 * pixels * mid * c_out, nbytes=8 << 20,
    )(pre_expand, pre_short, s_both, s_both, s_reduce, params, params, mask, w_squeeze)
    s_squeeze = sync(stat)

    act_squeeze, pre_window, stat = call(
        functools.partial(window_kernel, width, height, images),
        (3,),
        [mid_spec, all_tiles, count_spec, p_squeeze, mask_spec, tap_spec],
        [mid_spec, mid_spec, all_tiles],
        [shaped((pixels, mid), BF16), mid_f32, one_tile],
        [pltpu.VMEM(padded, BF16)],
        flops=18 * pixels * mid * mid, nbytes=6 << 20,
    )(pre_squeeze, s_squeeze, s_reduce, params, mask, w_window)
    s_window = sync(stat)

    act_window, pre_widen, stat = widen_out(pre_window, s_window, p_window, w_widen)
    s_widen = sync_wide(stat)

    block_out, grad_final, gsum = call(
        final_kernel,
        (blocks,),
        [wide_spec, tile_n(), count_spec, p_widen, mask_spec, wide_spec, wide_spec],
        [wide_spec, wide_spec, tile_n()],
        [shaped((pixels, c_out), BF16), wide_f32, wide_tiles],
        nbytes=7 << 20,
    )(pre_widen, s_widen, s_reduce, params, mask, first_out, cot)
    g_widen = sync_wide(gsum)

    gpre_widen, grad_window, gsum = call(
        widen_back_kernel,
        (blocks,),
        [
            wide_spec, wide_spec, tile_n(), tile_n(), count_spec, p_widen, mask_spec, cols(mid, TILE),
            mid_spec, all_tiles, p_window,
        ],
        [wide_spec, mid_spec, all_tiles],
        [shaped((pixels, c_out), BF16), mid_f32, one_tile],
        flops=2 * pixels * mid * c_out, nbytes=8 << 20,
    )(grad_final, pre_widen, s_widen, g_widen, s_reduce, params, mask, w_widen, pre_window, s_window, params)
    early_made = outer_spread(dp, act_window, left_const, gpre_widen, right_n, whole, blocks, blocks, 0, 9 + blocks, None)
    g_window = after(sync(gsum), early_made)

    gpad_window, grad_squeeze, gsum = call(
        functools.partial(window_back_kernel, width, height, images),
        (3,),
        [
            mid_spec, mid_spec, all_tiles, all_tiles, count_spec, p_window, mask_spec, tap_spec,
            mid_spec, all_tiles, p_squeeze,
        ],
        [full(padded), mid_spec, all_tiles],
        [shaped(padded, BF16), mid_f32, one_tile],
        flops=18 * pixels * mid * mid, nbytes=8 << 20,
    )(grad_window, pre_window, s_window, g_window, s_reduce, params, mask, w_window, pre_squeeze, s_squeeze, params)
    early_made = outer_spread(
        dp, act_squeeze, left_const, gpad_window, full(padded), window_taps, 9, 9, blocks, 9 + blocks, early_made
    )
    g_squeeze = sync(gsum)
    early_sum = lax.psum_scatter(
        after(early_made, g_squeeze).reshape(-1, TILE), "dp", scatter_dimension=0, tiled=True
    )

    gpre_squeeze, grad_joined, gsum = call(
        squeeze_back_kernel,
        (blocks,),
        [
            mid_spec, mid_spec, all_tiles, all_tiles, count_spec, p_squeeze, mask_spec,
            pl.BlockSpec((TILE, mid), lambda n: (n, 0)),
            wide_spec, wide_spec, wide_spec, e_spec, s_spec, p_expand, p_short,
        ],
        [mid_spec, wide_spec, tile_n(rows=16)],
        [shaped((pixels, mid), BF16), wide_f32, shaped((16 * blocks, LANES))],
        flops=2 * pixels * mid * c_out, nbytes=11 << 20,
    )(
        grad_squeeze, pre_squeeze, s_squeeze, g_squeeze, s_reduce, params, mask, w_squeeze,
        grad_final, pre_expand, pre_short, s_both, s_both, params, params,
    )
    g_both = sync_wide(gsum)
    order_squeeze, order_expand = xs + ys + zs, ys + xs + zs
    order_short = (xs + ys + zs, ys + xs + zs)
    halving = lambda made, order: Halving(made[0], order, flat, devices, made[1], core_bit)
    s_squeeze_grad = halving(
        outer_halves(core, first_out, right_n, gpre_squeeze, full((pixels, mid)), whole, blocks, 1), order_squeeze
    )
    g_both = after(g_both, s_squeeze_grad.keep)
    token = s_squeeze_grad.moves.pop(0)(g_both)

    gpre_expand, gpre_short, grad_spatial, gsum = call(
        expand_back_kernel,
        (blocks,),
        [
            wide_spec, wide_spec, wide_spec, e_spec, s_spec, tile_n(rows=16), count_spec, p_expand, p_short,
            mask_spec, cols(mid, TILE), mid_spec, all_tiles, p_spatial,
        ],
        [wide_spec, wide_spec, mid_spec, all_tiles],
        [shaped((pixels, c_out), BF16), shaped((pixels, c_out), BF16), mid_f32, one_tile],
        flops=2 * pixels * mid * c_out, nbytes=11 << 20,
    )(
        grad_joined, pre_expand, pre_short, s_both, s_both, g_both, s_reduce, params, params, mask, w_expand,
        pre_spatial, s_spatial, params,
    )
    s_expand_grad = halving(
        outer_halves(core, act_spatial, left_const, gpre_expand, right_n, whole, blocks, blocks), order_expand
    )
    s_short_grad = [
        halving(
            outer_halves(
                core, planes.reshape(4 * pixels, c_in), pl.BlockSpec((pixels, TILE), lambda b, *_, k=k: (0, k)),
                gpre_short, right_n, whole, blocks, blocks,
            ),
            order_short[k % 2],
        )
        for k in range(in_blocks)
    ]
    g_spatial = after(
        sync(gsum), s_expand_grad.keep, [s.keep for s in s_short_grad], s_squeeze_grad.received
    )
    for stream in [s_expand_grad] + s_short_grad:
        token = stream.moves.pop(0)(g_spatial)

    gshift_spatial, grad_reduce, gsum = call(
        functools.partial(spatial_back_kernel, width, height),
        (3,),
        [
            mid_spec, mid_spec, all_tiles, all_tiles, count_spec, p_spatial, mask_spec, tap_spec,
            full((4, pixels, mid)), all_tiles, p_reduce,
        ],
        [full((4, pixels, mid)), full((4, pixels, mid)), all_tiles],
        [shaped((4, pixels, mid), BF16), shaped((4, pixels, mid)), one_tile],
        flops=18 * pixels * mid * mid, nbytes=12 << 20,
    )(grad_spatial, pre_spatial, s_spatial, g_spatial, s_reduce, params, mask, w_spatial, pre_reduce, s_reduce, params)
    order_spatial, order_reduce = (xs + ys + zs, ys + xs + zs), zs[:1] + xs + ys + zs[1:]
    spatial_parts = ((0, 5), (5, 4))
    late = [
        halving(
            outer_halves(
                core, act_reduce, pl.BlockSpec((1, pixels, mid), functools.partial(spatial_plane, place)),
                gshift_spatial, full((4, pixels, mid)), functools.partial(spatial_taps, place), count, 1,
            ),
            order,
        )
        for (place, count), order in zip(spatial_parts, order_spatial)
    ]

    back_short = call(
        short_back_kernel,
        (blocks,),
        [wide_spec, cols(c_in, TILE)],
        full((pixels, c_in)),
        shaped((pixels, c_in)),
        flops=2 * pixels * c_in * c_out, nbytes=6 << 20,
    )(gpre_short, w_shortcut)
    crossed = [s.received for s in [s_expand_grad] + s_short_grad]
    g_reduce = after(sync(gsum), [s.keep for s in late], back_short, crossed)
    spread = TILE // dp
    early = Halving(early_sum.reshape(9 + blocks, spread, TILE), rep_bits, flat, devices)
    middle = [s_squeeze_grad, s_expand_grad] + s_short_grad

    reduce_back_call = call(
        functools.partial(reduce_back_kernel, quarter),
        (steps,),
        [
            plane_block(mid), plane_block(mid), all_tiles, all_tiles, count_spec, p_reduce,
            pl.BlockSpec((quarter, LANES), lambda k: (k, 0)), full((c_in, mid)),
            pl.BlockSpec((quarter, c_in), lambda k: (k, 0)), full(perm.shape),
        ],
        [plane_block(mid), pl.BlockSpec((4 * quarter, c_in), lambda k: (k, 0))],
        [shaped((4, pixels, mid), BF16), shaped((images * 4 * height * width, c_in), BF16)],
        flops=8 * pixels * c_in * mid, nbytes=10 << 20,
    )

    def reduce_back(summed):
        return reduce_back_call(
            grad_reduce, pre_reduce, s_reduce, summed, s_reduce, params, mask, w_reduce, back_short, perm_back
        )

    last = Later()

    def input_back(token):
        gpre_reduce, last.image_grad = reduce_back(after(g_reduce, token))
        stream = halving(
            outer_halves(
                core, planes.reshape(4 * pixels, c_in), pl.BlockSpec((4 * pixels, TILE), lambda b, *_: (0, b)),
                gpre_reduce.reshape(4 * pixels, mid), full((4 * pixels, mid)), whole, in_blocks, 1,
            ),
            order_reduce,
        )
        last.stream = stream
        last.moves.extend(stream.moves)
        return stream.keep

    def starts_of(first, order, rows):
        found = []
        for k in range(devices):
            start, left = first(k), rows
            for bit in order:
                left //= 2
                start += (k // bit % 2) * left
            found.append(start)
        return tuple(found)

    spread_starts = starts_of(lambda k: (k // rep) * spread, rep_bits, spread)
    early_out = Early(early, functools.partial(regroup, starts=spread_starts, total=9 + blocks))
    early_out.add_result(place=0, blocks=blocks, shape=(mid, c_out), down=False)
    early_out.add_result(place=blocks, blocks=9, shape=(9 * mid, mid), down=True)
    backs = [Return(stream, core_bit, flat, devices) for stream in late]
    for stream, back in zip(late, backs):
        stream.moves.extend(back.moves)
    input_step = Later()
    input_step.moves.append(input_back)
    token = run_streams(middle + late + [last, early, early_out, input_step], SCHEDULE, g_reduce)

    def gathered(shard):
        everything = lax.all_gather(shard.reshape(-1, TILE), AXES, axis=0, tiled=False)
        return functools.partial(regroup, everything, total=shard.shape[0])

    grad_w_widen, grad_w_window = early_out.results

    half_starts = lambda order: starts_of(lambda k: (k // core_bit % 2) * (TILE // 2), order, TILE // 2)
    regrouped = gathered(jnp.concatenate([s.keep for s in middle + [last.stream]], axis=0))
    grad_w_squeeze = regrouped(half_starts(order_squeeze), place=0, blocks=blocks, shape=(c_out, mid), down=True)
    grad_w_expand = regrouped(
        half_starts(order_expand), place=blocks, blocks=blocks, shape=(mid, c_out), down=False
    )
    grad_w_short = None
    for k in range(in_blocks):
        grad_w_short = regrouped(
            half_starts(order_short[k % 2]), place=(2 + k) * blocks, blocks=blocks, shape=(c_in, c_out),
            down=False, first=k, into=grad_w_short,
        )

    grad_w_spatial = None
    for (place, count), back in zip(spatial_parts, backs):
        grad_w_spatial = assemble(
            back.places(), back.pieces(), 0, count, (9 * mid, mid), lambda b, place=place: (place + b, 0),
            into=grad_w_spatial,
        )
    grad_w_reduce = regrouped(
        half_starts(order_reduce), place=(2 + in_blocks) * blocks, blocks=in_blocks, shape=(c_in, mid), down=True
    )
    grad_w_window, grad_w_spatial = (g.reshape(3, 3, mid, mid) for g in (grad_w_window, grad_w_spatial))

    shift_total = vector(g_both, 0, 16)
    return (
        block_out.reshape(cotangent.shape),
        last.image_grad.reshape(image_input.shape),
        grad_w_reduce,
        grad_w_spatial,
        grad_w_expand,
        grad_w_short,
        vector(jnp.sum(g_reduce, axis=0), ROWS, 8),
        vector(jnp.sum(g_reduce, axis=0), 0, 8),
        vector(jnp.sum(g_spatial, axis=0), ROWS, 8),
        vector(jnp.sum(g_spatial, axis=0), 0, 8),
        vector(g_both, ROWS, 16),
        shift_total,
        vector(g_both, 2 * ROWS, 16),
        shift_total,
        grad_w_squeeze,
        grad_w_window,
        grad_w_widen,
        vector(jnp.sum(g_squeeze, axis=0), ROWS, 8),
        vector(jnp.sum(g_squeeze, axis=0), 0, 8),
        vector(jnp.sum(g_window, axis=0), ROWS, 8),
        vector(jnp.sum(g_window, axis=0), 0, 8),
        vector(g_widen, ROWS, 8),
        vector(g_widen, 0, 8),
    )


def solution(mesh):
    split = P(AXES, None, None, None)
    return jax.shard_map(
        functools.partial(on_device, mesh.shape["dp"], mesh.shape["rep"]),
        mesh=mesh,
        in_specs=(split, P(AXES), P(AXES)) + (P(),) * 21 + (split,),
        out_specs=(split, split) + (P(),) * 21,
        check_vma=False,
    )
```

```python
import functools

import jax
import jax.numpy as jnp
import numpy as np
from jax import lax
from jax.experimental import pallas as pl
from jax.experimental.pallas import tpu as pltpu
from jax.sharding import PartitionSpec as P

EPSILON = 1e-05
F32 = jnp.float32
BF16 = jnp.bfloat16
AXES = ("dp", "rep")
LANES = 128
TILE = 512
ROWS = TILE // LANES
MIB = 60
SCHEDULE = (
    0, 1, 2, 3, 7, 4, 5, 9, 0, 1, 7, 6, 2, 3, 7, 6, 0, 1, 2, 3, 4, 5, 6, 0, 1, 6, 2, 3, 5, 4,
    6, 0, 1, 2, 3, 6, 5, 4, 5, 4, 5, 4, 5, 4, 5, 4, 5, 4, 5, 4, 8, 8, 5, 4,
)


def dot(left, right):
    return jnp.dot(left, right, preferred_element_type=F32)


def dot_nt(left, right):
    return lax.dot_general(left, right, (((1,), (1,)), ((), ())), preferred_element_type=F32)


def pack(vector):
    return jnp.concatenate(
        [vector[:, LANES * k : LANES * (k + 1)] for k in range(vector.shape[1] // LANES)], axis=0
    )


def unpack(rows):
    return jnp.concatenate([rows[k : k + 1, :] for k in range(rows.shape[0])], axis=1)


def col_sum(values):
    return jnp.sum(values, axis=0, keepdims=True)


def stat_tile(first, second):
    return jnp.concatenate([pack(col_sum(first)), pack(col_sum(second))], axis=0)


def put(ref, tile):
    ref[...] = jnp.broadcast_to(tile, ref.shape)


def total(ref):
    return ref[...] if len(ref.shape) == 2 else jnp.sum(ref[...], axis=0)


def coefficients(stat_ref, count_ref, param_ref, factor=1.0):
    stat, param = total(stat_ref), param_ref[...]
    count = total(count_ref)[0:ROWS, :] * factor
    average = stat[0:ROWS] / count
    inverse = lax.rsqrt(stat[ROWS : 2 * ROWS] / count - average * average + EPSILON)
    return (
        unpack(average),
        unpack(inverse),
        unpack(param[0:ROWS]),
        unpack(param[ROWS : 2 * ROWS]),
    )


def back_coefficients(grad_rows_shift, grad_rows_gain, count_ref, factor=1.0):
    count = total(count_ref)[0:ROWS, :] * factor
    return unpack(grad_rows_shift / count), unpack(grad_rows_gain / count)


def logistic(values):
    return 0.5 * jnp.tanh(0.5 * values) + 0.5


def silu(values):
    return values * logistic(values)


def slope(values):
    gate = logistic(values)
    return gate * (1.0 + values * (1.0 - gate))


def column(mask_ref):
    return mask_ref[:, 0:1]


def pixel_ids(pixels, width):
    return lax.broadcasted_iota(jnp.int32, (pixels, 1), 0)


def shift_cols(values, step, width):
    pixels = values.shape[0]
    place = lax.rem(pixel_ids(pixels, width), width)
    rolled = pltpu.roll(values, (-step) % pixels, 0)
    keep = place < width - step if step > 0 else place >= -step
    return jnp.where(keep, rolled, 0.0)


def shift_rows(values, step, width, height):
    pixels = values.shape[0]
    place = lax.rem(lax.div(pixel_ids(pixels, width), width), height)
    rolled = pltpu.roll(values, (-step * width) % pixels, 0)
    keep = place < height - step if step > 0 else place >= -step
    return jnp.where(keep, rolled, 0.0)


def full(shape):
    zeros = (0,) * len(shape)
    return pl.BlockSpec(shape, lambda *_: zeros)


def cols(rows, width):
    return pl.BlockSpec((rows, width), lambda n, *_: (0, n))


def tile_at(index, rows=8):
    return pl.BlockSpec((rows, LANES), lambda *_: (index, 0))


def tile_n(offset=0, rows=8):
    return pl.BlockSpec((rows, LANES), lambda n, *_: (offset + n, 0))


def call(kernel, grid, in_specs, out_specs, out_shape, scratch=(), mib=MIB, flops=0, nbytes=0):
    return pl.pallas_call(
        kernel,
        grid=grid,
        in_specs=in_specs,
        out_specs=out_specs,
        out_shape=out_shape,
        scratch_shapes=scratch,
        compiler_params=pltpu.CompilerParams(
            vmem_limit_bytes=mib << 20, dimension_semantics=("arbitrary",) * len(grid)
        ),
        cost_estimate=pl.CostEstimate(flops=flops, bytes_accessed=nbytes, transcendentals=0),
    )


def shaped(shape, dtype=F32):
    return jax.ShapeDtypeStruct(shape, dtype)


def reduce_kernel(quarter, x_ref, perm_ref, mask_ref, all_mask_ref, w_ref, xp_ref, pre_ref, stat_ref, acc_ref):
    step = pl.program_id(0)
    mask = column(mask_ref)
    masking = jnp.concatenate([mask] * 4, axis=0)
    planes = (dot(perm_ref[...], x_ref[...]) * masking).astype(BF16)
    pre = dot(planes, w_ref[...])
    for q in range(4):
        xp_ref[q] = planes[q * quarter : (q + 1) * quarter]
        pre_ref[q] = pre[q * quarter : (q + 1) * quarter]

    @pl.when(step == 0)
    def _():
        acc_ref[...] = jnp.zeros_like(acc_ref)

    acc_ref[0:1, :] += col_sum(pre)
    acc_ref[1:2, :] += col_sum(pre * pre)

    @pl.when(step == pl.num_programs(0) - 1)
    def _():
        count = jnp.broadcast_to(col_sum(all_mask_ref[...]), (8, LANES))
        put(stat_ref, jnp.concatenate([pack(acc_ref[0:1, :]), pack(acc_ref[1:2, :]), count], axis=0))


def product_kernel(x_ref, w_ref, out_ref, stat_ref):
    pre = dot(x_ref[0], w_ref[...])
    out_ref[...] = pre
    stat_ref[...] = stat_tile(pre, pre * pre)


def spatial_kernel(width, height, pre_ref, stat_ref, count_ref, param_ref, mask_ref, w_ref, act_ref, out_ref, out_stat_ref, y_ref):
    r = pl.program_id(0)
    mask = column(mask_ref)

    @pl.when(r == 0)
    def _():
        average, inverse, gain, shift = coefficients(stat_ref, count_ref, param_ref, 4.0)
        for q in range(4):
            norm = (pre_ref[q] - average) * inverse * gain + shift
            act_ref[q] = (silu(norm) * mask).astype(BF16)

    row_parity = jnp.where(r == 1, 0, 1)
    row_shift = jnp.where(r == 0, 1, 0)
    even, odd = act_ref[2 * row_parity], act_ref[2 * row_parity + 1]
    straight = dot(even, w_ref[0, 1]) + dot(odd, w_ref[0, 2])
    moved = dot(odd, w_ref[0, 0])

    @pl.when(r < 2)
    def _():
        y_ref[2 * row_shift] = straight
        y_ref[2 * row_shift + 1] = moved

    @pl.when(r == 2)
    def _():
        upper = y_ref[2] + shift_cols(y_ref[3], -1, width)
        lower = y_ref[0] + straight + shift_cols(y_ref[1] + moved, -1, width)
        pre = lower + shift_rows(upper, -1, width, height)
        out_ref[...] = pre
        masked = pre * mask
        put(out_stat_ref, stat_tile(masked, masked * pre))


def expand_kernel(pre_ref, stat_ref, count_ref, param_ref, mask_ref, w_ref, act_ref, out_ref, out_stat_ref):
    @pl.when(pl.program_id(0) == 0)
    def _():
        average, inverse, gain, shift = coefficients(stat_ref, count_ref, param_ref)
        norm = (pre_ref[...] - average) * inverse * gain + shift
        act_ref[...] = (silu(norm) * column(mask_ref)).astype(BF16)

    pre = dot(act_ref[...], w_ref[...])
    out_ref[...] = pre
    put(out_stat_ref, stat_tile(pre, pre * pre))


def join_kernel(pe_ref, ps_ref, se_ref, ss_ref, count_ref, qe_ref, qs_ref, mask_ref, w_ref, first_ref, out_ref, out_stat_ref):
    n = pl.program_id(0)
    average_e, inverse_e, gain_e, shift_e = coefficients(se_ref, count_ref, qe_ref)
    average_s, inverse_s, gain_s, shift_s = coefficients(ss_ref, count_ref, qs_ref)
    joined = (pe_ref[...] - average_e) * inverse_e * gain_e + shift_e
    joined += (ps_ref[...] - average_s) * inverse_s * gain_s + shift_s
    first = (silu(joined) * column(mask_ref)).astype(BF16)
    first_ref[...] = first
    part = dot(first, w_ref[...])

    @pl.when(n == 0)
    def _():
        out_ref[...] = part

    @pl.when(n > 0)
    def _():
        out_ref[...] += part

    @pl.when(n == pl.num_programs(0) - 1)
    def _():
        pre = out_ref[...]
        put(out_stat_ref, stat_tile(pre, pre * pre))


def store_padded(target_ref, values, step, width, height, images):
    area = width * height
    channels = values.shape[1]
    zeros = jnp.zeros((width, channels), BF16)
    for k in range(3):
        moved = values if k == 1 else shift_cols(values, step * (k - 1), width)
        moved = moved.astype(BF16)
        for b in range(images):
            target_ref[k, b, 0:width, :] = zeros
            target_ref[k, b, area + width : area + 2 * width, :] = zeros
            target_ref[k, b, width : area + width, :] = moved[b * area : (b + 1) * area]


def window_rows(ref, k, first, area, images):
    return jnp.concatenate([ref[k, b, pl.ds(first, area), :] for b in range(images)], axis=0)


def window_kernel(width, height, images, pre_ref, stat_ref, count_ref, param_ref, mask_ref, w_ref, act_ref, out_ref, out_stat_ref, pad_ref):
    r = pl.program_id(0)

    @pl.when(r == 0)
    def _():
        average, inverse, gain, shift = coefficients(stat_ref, count_ref, param_ref)
        norm = (pre_ref[...] - average) * inverse * gain + shift
        act = silu(norm) * column(mask_ref)
        act_ref[...] = act.astype(BF16)
        store_padded(pad_ref, act, 1, width, height, images)

    first = pl.multiple_of(r * width, width)
    part = dot(window_rows(pad_ref, 0, first, width * height, images), w_ref[0, 0])
    for k in (1, 2):
        part += dot(window_rows(pad_ref, k, first, width * height, images), w_ref[0, k])

    @pl.when(r == 0)
    def _():
        out_ref[...] = part

    @pl.when(r > 0)
    def _():
        out_ref[...] += part

    @pl.when(r == 2)
    def _():
        pre = out_ref[...]
        masked = pre * column(mask_ref)
        put(out_stat_ref, stat_tile(masked, masked * pre))


def final_kernel(pre_ref, stat_ref, count_ref, param_ref, mask_ref, first_ref, cot_ref, out_ref, grad_ref, sum_ref):
    average, inverse, gain, shift = coefficients(stat_ref, count_ref, param_ref)
    mask = column(mask_ref)
    hat = (pre_ref[...] - average) * inverse
    final = hat * gain + shift + first_ref[...].astype(F32)
    gate = logistic(final)
    out_ref[...] = (final * gate * mask).astype(BF16)
    grad = cot_ref[...].astype(F32) * mask * (gate * (1.0 + final * (1.0 - gate)))
    grad_ref[...] = grad
    put(sum_ref, stat_tile(grad, grad * hat))


def norm_back(grad, hat, scale, shift_term, gain_term, mask):
    return ((grad - mask * (shift_term + hat * gain_term)) * scale).astype(BF16)


def widen_back_kernel(
    grad_ref, pre_ref, stat_ref, gsum_ref, count_ref, param_ref, mask_ref, w_ref, in_ref, in_stat_ref, in_param_ref,
    gpre_ref, out_ref, sum_ref,
):
    n = pl.program_id(0)
    mask = column(mask_ref)
    average, inverse, gain, _ = coefficients(stat_ref, count_ref, param_ref)
    gsum = total(gsum_ref)
    shift_term, gain_term = back_coefficients(gsum[0:ROWS], gsum[ROWS : 2 * ROWS], count_ref)
    hat = (pre_ref[...] - average) * inverse
    gpre = norm_back(grad_ref[...], hat, inverse * gain, shift_term, gain_term, mask)
    gpre_ref[...] = gpre
    part = dot_nt(gpre, w_ref[...])

    @pl.when(n == 0)
    def _():
        out_ref[...] = part

    @pl.when(n > 0)
    def _():
        out_ref[...] += part

    @pl.when(n == pl.num_programs(0) - 1)
    def _():
        finish_back(in_ref[...], in_stat_ref, count_ref, in_param_ref, mask, out_ref, sum_ref)


def finish_back(pre, stat_ref, count_ref, param_ref, mask, out_ref, sum_ref):
    average, inverse, gain, shift = coefficients(stat_ref, count_ref, param_ref)
    hat = (pre - average) * inverse
    grad = out_ref[...] * mask * slope(hat * gain + shift)
    out_ref[...] = grad
    put(sum_ref, stat_tile(grad, grad * hat))


def pre_grad(grad_ref, pre_ref, stat_ref, gsum_ref, count_ref, param_ref, mask):
    average, inverse, gain, _ = coefficients(stat_ref, count_ref, param_ref)
    gsum = total(gsum_ref)
    shift_term, gain_term = back_coefficients(gsum[0:ROWS], gsum[ROWS : 2 * ROWS], count_ref)
    hat = (pre_ref[...] - average) * inverse
    return norm_back(grad_ref[...], hat, inverse * gain, shift_term, gain_term, mask)


def window_back_kernel(
    width, height, images,
    grad_ref, pre_ref, stat_ref, gsum_ref, count_ref, param_ref, mask_ref, w_ref, in_ref, in_stat_ref, in_param_ref,
    pad_ref, out_ref, sum_ref,
):
    r = pl.program_id(0)
    mask = column(mask_ref)

    @pl.when(r == 0)
    def _():
        gpre = pre_grad(grad_ref, pre_ref, stat_ref, gsum_ref, count_ref, param_ref, mask)
        store_padded(pad_ref, gpre.astype(F32), -1, width, height, images)

    first = pl.multiple_of((2 - r) * width, width)
    part = dot_nt(window_rows(pad_ref, 0, first, width * height, images), w_ref[0, 0])
    for k in (1, 2):
        part += dot_nt(window_rows(pad_ref, k, first, width * height, images), w_ref[0, k])

    @pl.when(r == 0)
    def _():
        out_ref[...] = part

    @pl.when(r > 0)
    def _():
        out_ref[...] += part

    @pl.when(r == 2)
    def _():
        finish_back(in_ref[...], in_stat_ref, count_ref, in_param_ref, mask, out_ref, sum_ref)


def squeeze_back_kernel(
    grad_ref, pre_ref, stat_ref, gsum_ref, count_ref, param_ref, mask_ref, w_ref,
    gfinal_ref, pe_ref, ps_ref, se_ref, ss_ref, qe_ref, qs_ref,
    gpre_ref, gj_ref, sum_ref,
):
    mask = column(mask_ref)

    @pl.when(pl.program_id(0) == 0)
    def _():
        gpre_ref[...] = pre_grad(grad_ref, pre_ref, stat_ref, gsum_ref, count_ref, param_ref, mask)

    gfirst = gfinal_ref[...] + dot_nt(gpre_ref[...], w_ref[...])
    average_e, inverse_e, gain_e, shift_e = coefficients(se_ref, count_ref, qe_ref)
    average_s, inverse_s, gain_s, shift_s = coefficients(ss_ref, count_ref, qs_ref)
    hat_e = (pe_ref[...] - average_e) * inverse_e
    hat_s = (ps_ref[...] - average_s) * inverse_s
    joined = hat_e * gain_e + shift_e + (hat_s * gain_s + shift_s)
    grad = gfirst * mask * slope(joined)
    gj_ref[...] = grad
    sum_ref[...] = jnp.concatenate(
        [stat_tile(grad, grad * hat_e), pack(col_sum(grad * hat_s)), jnp.zeros((ROWS, LANES), F32)], axis=0
    )


def expand_back_kernel(
    gj_ref, pe_ref, ps_ref, se_ref, ss_ref, gsum_ref, count_ref, qe_ref, qs_ref, mask_ref, w_ref,
    in_ref, in_stat_ref, in_param_ref,
    ge_ref, gs_ref, out_ref, sum_ref,
):
    n = pl.program_id(0)
    mask = column(mask_ref)
    average_e, inverse_e, gain_e, _ = coefficients(se_ref, count_ref, qe_ref)
    average_s, inverse_s, gain_s, _ = coefficients(ss_ref, count_ref, qs_ref)
    gsum = total(gsum_ref)
    shift_term, gain_e_term = back_coefficients(gsum[0:ROWS], gsum[ROWS : 2 * ROWS], count_ref)
    _, gain_s_term = back_coefficients(gsum[0:ROWS], gsum[2 * ROWS : 3 * ROWS], count_ref)
    grad = gj_ref[...]
    hat_e = (pe_ref[...] - average_e) * inverse_e
    hat_s = (ps_ref[...] - average_s) * inverse_s
    ge = norm_back(grad, hat_e, inverse_e * gain_e, shift_term, gain_e_term, mask)
    ge_ref[...] = ge
    gs_ref[...] = norm_back(grad, hat_s, inverse_s * gain_s, shift_term, gain_s_term, mask)
    part = dot_nt(ge, w_ref[...])

    @pl.when(n == 0)
    def _():
        out_ref[...] = part

    @pl.when(n > 0)
    def _():
        out_ref[...] += part

    @pl.when(n == pl.num_programs(0) - 1)
    def _():
        finish_back(in_ref[...], in_stat_ref, count_ref, in_param_ref, mask, out_ref, sum_ref)


def spatial_back_kernel(
    width, height,
    grad_ref, pre_ref, stat_ref, gsum_ref, count_ref, param_ref, mask_ref, w_ref, in_ref, in_stat_ref, in_param_ref,
    shift_ref, out_ref, sum_ref,
):
    r = pl.program_id(0)
    mask = column(mask_ref)

    @pl.when(r == 0)
    def _():
        gpre = pre_grad(grad_ref, pre_ref, stat_ref, gsum_ref, count_ref, param_ref, mask).astype(F32)
        below = shift_rows(gpre, 1, width, height)
        shift_ref[0] = gpre.astype(BF16)
        shift_ref[1] = shift_cols(gpre, 1, width).astype(BF16)
        shift_ref[2] = below.astype(BF16)
        shift_ref[3] = shift_cols(below, 1, width).astype(BF16)

    row_parity = jnp.where(r == 1, 0, 1)
    row_shift = jnp.where(r == 0, 1, 0)
    straight, moved = shift_ref[2 * row_shift], shift_ref[2 * row_shift + 1]
    even = dot_nt(straight, w_ref[0, 1])
    odd = dot_nt(moved, w_ref[0, 0]) + dot_nt(straight, w_ref[0, 2])

    @pl.when(r < 2)
    def _():
        out_ref[2 * row_parity] = even
        out_ref[2 * row_parity + 1] = odd

    @pl.when(r == 2)
    def _():
        out_ref[2] += even
        out_ref[3] += odd
        average, inverse, gain, shift = coefficients(in_stat_ref, count_ref, in_param_ref, 4.0)
        whole_sum = whole_hat = jnp.zeros((1, out_ref.shape[2]), F32)
        for q in range(4):
            hat = (in_ref[q] - average) * inverse
            grad = out_ref[q] * mask * slope(hat * gain + shift)
            out_ref[q] = grad
            whole_sum += col_sum(grad)
            whole_hat += col_sum(grad * hat)
        put(sum_ref, jnp.concatenate([pack(whole_sum), pack(whole_hat)], axis=0))


def short_back_kernel(g_ref, w_ref, out_ref):
    part = dot_nt(g_ref[...], w_ref[...])

    @pl.when(pl.program_id(0) == 0)
    def _():
        out_ref[...] = part

    @pl.when(pl.program_id(0) > 0)
    def _():
        out_ref[...] += part


def reduce_back_kernel(
    quarter, grad_ref, pre_ref, stat_ref, gsum_ref, count_ref, param_ref, mask_ref, w_ref, short_ref, perm_ref,
    gpre_ref, out_ref,
):
    mask = column(mask_ref)
    masking = jnp.concatenate([mask] * 4, axis=0)
    average, inverse, gain, _ = coefficients(stat_ref, count_ref, param_ref, 4.0)
    gsum = total(gsum_ref)
    shift_term, gain_term = back_coefficients(gsum[0:ROWS], gsum[ROWS : 2 * ROWS], count_ref, 4.0)
    grad = jnp.concatenate([grad_ref[q] for q in range(4)], axis=0)
    pre = jnp.concatenate([pre_ref[q] for q in range(4)], axis=0)
    hat = (pre - average) * inverse
    gpre = norm_back(grad, hat, inverse * gain, shift_term, gain_term, masking)
    for q in range(4):
        gpre_ref[q] = gpre[q * quarter : (q + 1) * quarter]
    image = dot_nt(gpre, w_ref[...])
    image = jnp.concatenate([image[0:quarter] + short_ref[...], image[quarter:]], axis=0)
    image = (image * masking).astype(BF16)
    out_ref[...] = dot(perm_ref[...], image).astype(BF16)


def turn_left(left_ref, turned_ref, per_left):
    @pl.when(lax.rem(pl.program_id(0), per_left) == 0)
    def _():
        left = left_ref[...] if len(left_ref.shape) == 2 else left_ref[0]
        turned_ref[...] = left.T


def halves_kernel(pick, per_left, core_ref, left_ref, right_ref, keep_ref, send_ref, turned_ref):
    turn_left(left_ref, turned_ref, per_left)
    half = TILE // 2
    right = pick(right_ref, pl.program_id(0))
    mine = pl.multiple_of(core_ref[0] * half, half)
    away = pl.multiple_of((1 - core_ref[0]) * half, half)
    send_ref[0] = dot(turned_ref[pl.ds(away, half), :], right)
    keep_ref[0] = dot(turned_ref[pl.ds(mine, half), :], right)


def outer_halves(core, left, left_spec, right, right_spec, pick, blocks, per_left):
    half = TILE // 2
    pixels = left_spec.block_shape[-2]
    shape = shaped((blocks, half, TILE))
    out_spec = pl.BlockSpec((1, half, TILE), lambda b, *_: (b, 0, 0))
    return pl.pallas_call(
        functools.partial(halves_kernel, pick, per_left),
        grid_spec=pltpu.PrefetchScalarGridSpec(
            num_scalar_prefetch=1,
            grid=(blocks,),
            in_specs=[left_spec, right_spec],
            out_specs=[out_spec, out_spec],
            scratch_shapes=[pltpu.VMEM((TILE, pixels), BF16)],
        ),
        out_shape=[shape, shape],
        compiler_params=outer_params(),
        cost_estimate=outer_cost(blocks, pixels),
    )(core, left, right)


def outer_params():
    return pltpu.CompilerParams(vmem_limit_bytes=MIB << 20, dimension_semantics=("arbitrary",))


def outer_cost(blocks, pixels):
    return pl.CostEstimate(
        flops=2 * blocks * pixels * TILE * TILE, bytes_accessed=blocks * TILE * TILE * 4, transcendentals=0
    )


def spread_kernel(pick, per_left, left_ref, right_ref, *refs):
    out_ref, turned_ref = refs[-2], refs[-1]
    turn_left(left_ref, turned_ref, per_left)
    out_ref[...] = dot(turned_ref[...], pick(right_ref, pl.program_id(0))).reshape(out_ref.shape)


def outer_spread(shares, left, left_spec, right, right_spec, pick, blocks, per_left, place, total, into):
    rows = TILE // shares
    pixels = left_spec.block_shape[-2]
    extra = () if into is None else (into,)
    return pl.pallas_call(
        functools.partial(spread_kernel, pick, per_left),
        grid=(blocks,),
        in_specs=[left_spec, right_spec] + [pl.BlockSpec(memory_space=pl.ANY)] * len(extra),
        out_specs=pl.BlockSpec((shares, rows, TILE), lambda b: (0, place + b, 0)),
        out_shape=shaped((shares, total * rows, TILE)),
        scratch_shapes=[pltpu.VMEM((TILE, pixels), BF16)],
        input_output_aliases={2: 0} if extra else {},
        compiler_params=outer_params(),
        cost_estimate=outer_cost(blocks, pixels),
    )(left, right, *extra)


def assemble_kernel(chunks, place_ref, own_ref, near_ref, far_ref, both_ref, *refs):
    out_ref = refs[-1]
    rows = TILE // 4 // chunks
    for k, ref in enumerate((own_ref, near_ref, far_ref, both_ref)):
        for c in range(chunks):
            start = pl.multiple_of(place_ref[k * chunks + c], rows)
            out_ref[pl.ds(start, rows), :] = ref[0, c * rows : (c + 1) * rows, :]


def assemble(places, pieces, first, blocks, shape, where, chunks=1, into=None):
    in_spec = pl.BlockSpec((1, TILE // 4, TILE), lambda b, *_: (first + b, 0, 0))
    extra = () if into is None else (into,)
    return pl.pallas_call(
        functools.partial(assemble_kernel, chunks),
        grid_spec=pltpu.PrefetchScalarGridSpec(
            num_scalar_prefetch=1,
            grid=(blocks,),
            in_specs=[in_spec] * 4 + [pl.BlockSpec(memory_space=pl.ANY)] * len(extra),
            out_specs=pl.BlockSpec((TILE, TILE), lambda b, *_: where(b)),
        ),
        out_shape=shaped(shape),
        input_output_aliases={5: 0} if extra else {},
        compiler_params=outer_params(),
        cost_estimate=pl.CostEstimate(
            flops=0, bytes_accessed=2 * blocks * TILE * TILE * 4, transcendentals=0
        ),
    )(places, *pieces, *extra)


def regroup_kernel(starts, rows, down, in_ref, *refs):
    out_ref = refs[-1]
    for j in range(in_ref.shape[1] // rows):
        base, col = (j * TILE, 0) if down else (0, j * TILE)
        for k, start in enumerate(starts):
            out_ref[base + start : base + start + rows, col : col + TILE] = in_ref[k, j * rows : (j + 1) * rows, :]


def regroup(gathered, starts, total, place, blocks, shape, down, first=0, into=None):
    devices, rows = gathered.shape[0], gathered.shape[1] // total
    extra = () if into is None else (into,)
    if rows % 8:
        order = np.argsort(np.asarray(starts))
        gathered = gathered.reshape(devices, total, rows, TILE)[order].transpose(1, 0, 2, 3)
        gathered = gathered.reshape(1, total * TILE, TILE)
        devices, rows, starts = 1, TILE, (0,)
    pair = 2 if all(n % 2 == 0 for n in (place, blocks, first if down else 0)) else 1
    out_block = (pair * TILE, TILE) if down else (TILE, pair * TILE)
    where = (lambda b: (first // pair + b, 0)) if down else (lambda b: (first, b))
    return pl.pallas_call(
        functools.partial(regroup_kernel, starts, rows, down),
        grid=(blocks // pair,),
        in_specs=[pl.BlockSpec((devices, pair * rows, TILE), lambda b: (0, place // pair + b, 0))]
        + [pl.BlockSpec(memory_space=pl.ANY)] * len(extra),
        out_specs=pl.BlockSpec(out_block, where),
        out_shape=shaped(shape),
        input_output_aliases={1: 0} if extra else {},
        compiler_params=outer_params(),
        cost_estimate=pl.CostEstimate(
            flops=0, bytes_accessed=2 * blocks * TILE * TILE * 4, transcendentals=0
        ),
    )(gathered, *extra)


def bits_of(first, size):
    found = []
    while size > 1:
        found.append(first)
        first, size = first * 2, size // 2
    return found


def mesh_bits(dp, rep):
    side = int(round(dp**0.5))
    if side * side == dp:
        return 1, bits_of(rep, side), bits_of(rep * side, side), bits_of(2, rep // 2)
    side = int(round((dp // 2) ** 0.5))
    return rep, bits_of(2 * rep, side), bits_of(2 * rep * side, side), bits_of(1, rep)


def swap(values, bit, devices):
    return lax.ppermute(values, AXES, [(i, i ^ bit) for i in range(devices)])


def sync_all(tile, devices):
    return lax.all_to_all(tile, AXES, 0, 0, tiled=True)


def sync_hops(tile, rounds, devices):
    for bits in rounds:
        near = [swap(tile, bit, devices) for bit in bits]
        if len(bits) == 2:
            across = swap(tile, bits[0] + bits[1], devices)
            tile = (tile + near[0]) + (near[1] + across)
        else:
            tile = tile + near[0]
    return tile


def device_bit(flat, bit):
    return lax.rem(lax.div(flat, bit), 2)


def after(values, *others):
    return lax.optimization_barrier((values,) + others)[0]


def half_sum(keep, received, which):
    rows = keep.shape[1] // 2
    first = lax.dynamic_slice_in_dim(keep, which * rows, rows, axis=1)
    return first + lax.dynamic_slice_in_dim(received, which * rows, rows, axis=1)


def join_halves(own, values, other):
    return jnp.where(
        own == 0, jnp.concatenate([values, other], axis=1), jnp.concatenate([other, values], axis=1)
    )


class Halving:
    def __init__(self, keep, order, flat, devices, send=None, core=None):
        self.keep, self.order, self.flat, self.devices = keep, list(order), flat, devices
        self.received = None
        self.moves = []
        if send is not None:
            self.moves.append(lambda token: self.cross(send, core, token))
        self.moves += [functools.partial(self.halve, bit) for bit in self.order] + [self.add]

    def cross(self, send, core, token):
        send = after(send, token)
        self.received = swap(send, core, self.devices)
        return send

    def halve(self, bit, token):
        own = device_bit(self.flat, bit)
        if self.received is None:
            keep, rows = after(self.keep, token), self.keep.shape[1] // 2
            send = lax.dynamic_slice_in_dim(keep, (1 - own) * rows, rows, axis=1)
            self.received = swap(send, bit, self.devices)
            self.keep = lax.dynamic_slice_in_dim(keep, own * rows, rows, axis=1)
            return send
        keep, received = after((self.keep, self.received), token)
        send = half_sum(keep, received, 1 - own)
        self.received = swap(send, bit, self.devices)
        keep, received = after((keep, received), send)
        self.keep = half_sum(keep, received, own)
        return send

    def add(self, token):
        keep, received = after((self.keep, self.received), token)
        self.keep = keep + received
        return self.keep


class Return:
    def __init__(self, source, core, flat, devices):
        self.source, self.core, self.flat, self.devices = source, core, flat, devices
        self.order = source.order
        back = list(reversed(self.order))
        self.moves = [functools.partial(self.widen, a, b) for a, b in zip([None] + back[:-1], back)]
        self.moves.append(self.cross)

    def widen(self, joined, bit, token):
        if joined is None:
            self.own = after(self.source.keep, token)
        else:
            own, other = after((self.own, self.near), token)
            self.own = join_halves(device_bit(self.flat, joined), own, other)
        self.near = swap(self.own, bit, self.devices)
        if bit == self.order[0]:
            self.far = swap(self.own, self.core, self.devices)
        return self.own

    def cross(self, token):
        self.near = after(self.near, token)
        self.both = swap(self.near, self.core, self.devices)
        return self.near

    def pieces(self):
        return self.own, self.near, self.far, self.both

    def places(self):
        half, quarter = TILE // 2, TILE // 4
        core, own = device_bit(self.flat, self.core), device_bit(self.flat, self.order[0])
        return jnp.stack(
            [c * half + o * quarter for c in (core, 1 - core) for o in (own, 1 - own)]
        ).astype(jnp.int32)


class Later:
    def __init__(self):
        self.moves = []


class Early:
    def __init__(self, source, make):
        self.source, self.make, self.whole = source, make, None
        self.moves, self.results = [], []

    def add_result(self, **how):
        self.moves.append(functools.partial(self.result, how))

    def gather(self):
        self.whole = lax.all_gather(self.source.keep.reshape(-1, TILE), AXES, axis=0, tiled=False)

    def result(self, how, token):
        if self.whole is None:
            self.gather()
        self.results.append(self.make(after(self.whole, token), **how))
        return self.results[-1]


def run_streams(streams, schedule, token, to_end=True):
    for k in schedule:
        if streams[k].moves:
            token = streams[k].moves.pop(0)(token)
    while to_end and any(s.moves for s in streams):
        for s in streams:
            if s.moves:
                token = s.moves.pop(0)(token)
    return token


def permutation(width):
    size = 8 * 2 * width
    matrix = np.zeros((size, size), np.float32)
    place = 0
    for row_parity in range(2):
        for col_parity in range(2):
            for i in range(4):
                for j in range(width):
                    matrix[place, (2 * i + row_parity) * 2 * width + 2 * j + col_parity] = 1.0
                    place += 1
    return matrix


def param_tiles(gain, shift):
    blocks = gain.shape[0] // TILE
    pair = jnp.stack([gain.reshape(blocks, ROWS, LANES), shift.reshape(blocks, ROWS, LANES)], axis=1)
    return pair.reshape(blocks * 8, LANES)


def vector(tiles, first, step):
    return tiles.reshape(-1, step, LANES)[:, first : first + ROWS].reshape(-1)


def on_device(dp, rep, *arrays):
    (image_input, heights, widths, w_reduce, w_spatial, w_expand, w_shortcut,
     gain_reduce, shift_reduce, gain_spatial, shift_spatial, gain_expand, shift_expand,
     gain_shortcut, shift_shortcut, w_squeeze, w_window, w_widen,
     gain_squeeze, shift_squeeze, gain_window, shift_window, gain_widen, shift_widen, cotangent) = arrays
    images, height, width, c_out = cotangent.shape
    c_in, mid = w_reduce.shape
    pixels = images * height * width
    quarter = 64
    steps = pixels // quarter
    blocks = c_out // TILE
    devices = dp * rep
    core_bit, x_bits, y_bits, z_bits = mesh_bits(dp, rep)
    hop_rounds = [(core_bit,)] + list(zip(y_bits, x_bits))
    hop_rounds += [tuple(z_bits[k : k + 2]) for k in range(0, len(z_bits), 2)]
    xs, ys, zs, rep_bits = x_bits, y_bits, z_bits, bits_of(1, rep)
    flat = lax.axis_index(AXES)
    core = device_bit(flat, core_bit).astype(jnp.int32).reshape(1)
    sync = functools.partial(sync_all, devices=devices)
    sync_wide = functools.partial(sync_hops, rounds=hop_rounds, devices=devices)

    row_ids = lax.broadcasted_iota(jnp.int32, (1, height, 1, LANES), 1)
    col_ids = lax.broadcasted_iota(jnp.int32, (1, 1, width, LANES), 2)
    inside = (row_ids < heights[:, None, None, None]) & (col_ids < widths[:, None, None, None])
    mask = jnp.where(inside, 1.0, 0.0).astype(F32).reshape(pixels, LANES)
    params = jnp.concatenate(
        [
            param_tiles(gain_reduce, shift_reduce), param_tiles(gain_spatial, shift_spatial),
            param_tiles(gain_squeeze, shift_squeeze), param_tiles(gain_window, shift_window),
            param_tiles(gain_expand, shift_expand), param_tiles(gain_shortcut, shift_shortcut),
            param_tiles(gain_widen, shift_widen),
        ],
        axis=0,
    )
    p_reduce, p_spatial, p_squeeze, p_window = (tile_at(k) for k in range(4))
    p_expand, p_short, p_widen = (tile_n(4 + blocks * k) for k in range(3))
    turn = permutation(width)
    perm, perm_back = jnp.asarray(turn, BF16), jnp.asarray(turn.T.copy(), BF16)
    image = image_input.reshape(images * 4 * height * width, c_in)
    cot = cotangent.reshape(pixels, c_out)

    mask_spec, wide_f32 = full((pixels, LANES)), shaped((pixels, c_out))
    mid_f32, mid_spec = shaped((pixels, mid)), full((pixels, mid))
    wide_spec, tap_spec = cols(pixels, TILE), pl.BlockSpec((1, 3, mid, mid), lambda r: (r, 0, 0, 0))
    plane_block = lambda c: pl.BlockSpec((4, quarter, c), lambda k: (0, k, 0))
    area, in_blocks = width * height, c_in // TILE
    left_const = pl.BlockSpec((pixels, TILE), lambda b, *_: (0, 0))
    right_n = pl.BlockSpec((pixels, TILE), lambda b, *_: (0, b))

    def whole(ref, b):
        return ref[...]

    def window_taps(ref, b):
        r, c = lax.div(b, 3), lax.rem(b, 3)
        first = pl.multiple_of((2 - r) * width, width)
        return window_rows(ref, c, first, area, images)

    def spatial_taps(place, ref, b):
        r, c = lax.div(place + b, 3), lax.rem(place + b, 3)
        return ref[2 * jnp.where(r == 0, 1, 0) + jnp.where(c == 0, 1, 0)]

    def spatial_plane(place, b, *_):
        r, c = lax.div(place + b, 3), lax.rem(place + b, 3)
        return (2 * jnp.where(r == 1, 0, 1) + jnp.where(c == 1, 0, 1), 0, 0)

    one_tile, wide_tiles = shaped((devices, 8, LANES)), shaped((8 * blocks, LANES))
    all_tiles = full((devices, 8, LANES))
    count_spec = pl.BlockSpec((devices, 8, LANES), lambda *_: (0, 1, 0))
    padded = (3, images, (height + 2) * width, mid)

    planes, pre_reduce, stat = call(
        functools.partial(reduce_kernel, quarter),
        (steps,),
        [
            pl.BlockSpec((4 * quarter, c_in), lambda k: (k, 0)), full(perm.shape),
            pl.BlockSpec((quarter, LANES), lambda k: (k, 0)), mask_spec, full((c_in, mid)),
        ],
        [plane_block(c_in), plane_block(mid), full((devices, 16, LANES))],
        [shaped((4, pixels, c_in), BF16), shaped((4, pixels, mid)), shaped((devices, 16, LANES))],
        [pltpu.VMEM((8, mid), F32)],
        flops=8 * pixels * c_in * mid, nbytes=8 << 20,
    )(image, perm, mask, mask, w_reduce)
    s_reduce = sync(stat)

    pre_short, stat_short = call(
        product_kernel,
        (blocks,),
        [pl.BlockSpec((1, pixels, c_in), lambda n: (0, 0, 0)), cols(c_in, TILE)],
        [wide_spec, tile_n()],
        [wide_f32, wide_tiles],
        flops=2 * pixels * c_in * c_out, nbytes=6 << 20,
    )(planes, w_shortcut)

    act_reduce, pre_spatial, stat = call(
        functools.partial(spatial_kernel, width, height),
        (3,),
        [full((4, pixels, mid)), all_tiles, count_spec, p_reduce, mask_spec, tap_spec],
        [full((4, pixels, mid)), mid_spec, all_tiles],
        [shaped((4, pixels, mid), BF16), mid_f32, one_tile],
        [pltpu.VMEM((4, pixels, mid), F32)],
        flops=18 * pixels * mid * mid, nbytes=8 << 20,
    )(pre_reduce, s_reduce, s_reduce, params, mask, w_spatial)
    s_spatial = sync(stat)

    def widen_out(pre, stat, p_spec, weights):
        return call(
            expand_kernel,
            (blocks,),
            [mid_spec, all_tiles, count_spec, p_spec, mask_spec, cols(mid, TILE)],
            [mid_spec, wide_spec, tile_n()],
            [shaped((pixels, mid), BF16), wide_f32, wide_tiles],
            flops=2 * pixels * mid * c_out, nbytes=5 << 20,
        )(pre, stat, s_reduce, params, mask, weights)

    act_spatial, pre_expand, stat = widen_out(pre_spatial, s_spatial, p_spatial, w_expand)
    s_both = sync_wide(jnp.concatenate([stat, stat_short], axis=0))
    e_spec, s_spec = tile_n(), tile_n(blocks)

    first_out, pre_squeeze, stat = call(
        join_kernel,
        (blocks,),
        [
            wide_spec, wide_spec, e_spec, s_spec, count_spec, p_expand, p_short, mask_spec,
            pl.BlockSpec((TILE, mid), lambda n: (n, 0)),
        ],
        [wide_spec, mid_spec, all_tiles],
        [shaped((pixels, c_out), BF16), mid_f32, one_tile],
        flops=2 * pixels * mid * c_out, nbytes=8 << 20,
    )(pre_expand, pre_short, s_both, s_both, s_reduce, params, params, mask, w_squeeze)
    s_squeeze = sync(stat)

    act_squeeze, pre_window, stat = call(
        functools.partial(window_kernel, width, height, images),
        (3,),
        [mid_spec, all_tiles, count_spec, p_squeeze, mask_spec, tap_spec],
        [mid_spec, mid_spec, all_tiles],
        [shaped((pixels, mid), BF16), mid_f32, one_tile],
        [pltpu.VMEM(padded, BF16)],
        flops=18 * pixels * mid * mid, nbytes=6 << 20,
    )(pre_squeeze, s_squeeze, s_reduce, params, mask, w_window)
    s_window = sync(stat)

    act_window, pre_widen, stat = widen_out(pre_window, s_window, p_window, w_widen)
    s_widen = sync_wide(stat)

    block_out, grad_final, gsum = call(
        final_kernel,
        (blocks,),
        [wide_spec, tile_n(), count_spec, p_widen, mask_spec, wide_spec, wide_spec],
        [wide_spec, wide_spec, tile_n()],
        [shaped((pixels, c_out), BF16), wide_f32, wide_tiles],
        nbytes=7 << 20,
    )(pre_widen, s_widen, s_reduce, params, mask, first_out, cot)
    g_widen = sync_wide(gsum)

    gpre_widen, grad_window, gsum = call(
        widen_back_kernel,
        (blocks,),
        [
            wide_spec, wide_spec, tile_n(), tile_n(), count_spec, p_widen, mask_spec, cols(mid, TILE),
            mid_spec, all_tiles, p_window,
        ],
        [wide_spec, mid_spec, all_tiles],
        [shaped((pixels, c_out), BF16), mid_f32, one_tile],
        flops=2 * pixels * mid * c_out, nbytes=8 << 20,
    )(grad_final, pre_widen, s_widen, g_widen, s_reduce, params, mask, w_widen, pre_window, s_window, params)
    early_made = outer_spread(dp, act_window, left_const, gpre_widen, right_n, whole, blocks, blocks, 0, 9 + blocks, None)
    g_window = after(sync(gsum), early_made)

    gpad_window, grad_squeeze, gsum = call(
        functools.partial(window_back_kernel, width, height, images),
        (3,),
        [
            mid_spec, mid_spec, all_tiles, all_tiles, count_spec, p_window, mask_spec, tap_spec,
            mid_spec, all_tiles, p_squeeze,
        ],
        [full(padded), mid_spec, all_tiles],
        [shaped(padded, BF16), mid_f32, one_tile],
        flops=18 * pixels * mid * mid, nbytes=8 << 20,
    )(grad_window, pre_window, s_window, g_window, s_reduce, params, mask, w_window, pre_squeeze, s_squeeze, params)
    early_made = outer_spread(
        dp, act_squeeze, left_const, gpad_window, full(padded), window_taps, 9, 9, blocks, 9 + blocks, early_made
    )
    g_squeeze = sync(gsum)
    early_sum = lax.psum_scatter(
        after(early_made, g_squeeze).reshape(-1, TILE), "dp", scatter_dimension=0, tiled=True
    )

    gpre_squeeze, grad_joined, gsum = call(
        squeeze_back_kernel,
        (blocks,),
        [
            mid_spec, mid_spec, all_tiles, all_tiles, count_spec, p_squeeze, mask_spec,
            pl.BlockSpec((TILE, mid), lambda n: (n, 0)),
            wide_spec, wide_spec, wide_spec, e_spec, s_spec, p_expand, p_short,
        ],
        [mid_spec, wide_spec, tile_n(rows=16)],
        [shaped((pixels, mid), BF16), wide_f32, shaped((16 * blocks, LANES))],
        flops=2 * pixels * mid * c_out, nbytes=11 << 20,
    )(
        grad_squeeze, pre_squeeze, s_squeeze, g_squeeze, s_reduce, params, mask, w_squeeze,
        grad_final, pre_expand, pre_short, s_both, s_both, params, params,
    )
    g_both = sync_wide(gsum)
    order_squeeze, order_expand = xs + ys + zs, ys + xs + zs
    order_short = (xs + ys + zs, ys + xs + zs)
    halving = lambda made, order: Halving(made[0], order, flat, devices, made[1], core_bit)
    s_squeeze_grad = halving(
        outer_halves(core, first_out, right_n, gpre_squeeze, full((pixels, mid)), whole, blocks, 1), order_squeeze
    )
    g_both = after(g_both, s_squeeze_grad.keep)
    token = s_squeeze_grad.moves.pop(0)(g_both)

    gpre_expand, gpre_short, grad_spatial, gsum = call(
        expand_back_kernel,
        (blocks,),
        [
            wide_spec, wide_spec, wide_spec, e_spec, s_spec, tile_n(rows=16), count_spec, p_expand, p_short,
            mask_spec, cols(mid, TILE), mid_spec, all_tiles, p_spatial,
        ],
        [wide_spec, wide_spec, mid_spec, all_tiles],
        [shaped((pixels, c_out), BF16), shaped((pixels, c_out), BF16), mid_f32, one_tile],
        flops=2 * pixels * mid * c_out, nbytes=11 << 20,
    )(
        grad_joined, pre_expand, pre_short, s_both, s_both, g_both, s_reduce, params, params, mask, w_expand,
        pre_spatial, s_spatial, params,
    )
    s_expand_grad = halving(
        outer_halves(core, act_spatial, left_const, gpre_expand, right_n, whole, blocks, blocks), order_expand
    )
    s_short_grad = [
        halving(
            outer_halves(
                core, planes.reshape(4 * pixels, c_in), pl.BlockSpec((pixels, TILE), lambda b, *_, k=k: (0, k)),
                gpre_short, right_n, whole, blocks, blocks,
            ),
            order_short[k % 2],
        )
        for k in range(in_blocks)
    ]
    g_spatial = after(
        sync(gsum), s_expand_grad.keep, [s.keep for s in s_short_grad], s_squeeze_grad.received
    )
    for stream in [s_expand_grad] + s_short_grad:
        token = stream.moves.pop(0)(g_spatial)

    gshift_spatial, grad_reduce, gsum = call(
        functools.partial(spatial_back_kernel, width, height),
        (3,),
        [
            mid_spec, mid_spec, all_tiles, all_tiles, count_spec, p_spatial, mask_spec, tap_spec,
            full((4, pixels, mid)), all_tiles, p_reduce,
        ],
        [full((4, pixels, mid)), full((4, pixels, mid)), all_tiles],
        [shaped((4, pixels, mid), BF16), shaped((4, pixels, mid)), one_tile],
        flops=18 * pixels * mid * mid, nbytes=12 << 20,
    )(grad_spatial, pre_spatial, s_spatial, g_spatial, s_reduce, params, mask, w_spatial, pre_reduce, s_reduce, params)
    order_spatial, order_reduce = (xs + ys + zs, ys + xs + zs), zs[:1] + xs + ys + zs[1:]
    spatial_parts = ((0, 5), (5, 4))
    late = [
        halving(
            outer_halves(
                core, act_reduce, pl.BlockSpec((1, pixels, mid), functools.partial(spatial_plane, place)),
                gshift_spatial, full((4, pixels, mid)), functools.partial(spatial_taps, place), count, 1,
            ),
            order,
        )
        for (place, count), order in zip(spatial_parts, order_spatial)
    ]

    back_short = call(
        short_back_kernel,
        (blocks,),
        [wide_spec, cols(c_in, TILE)],
        full((pixels, c_in)),
        shaped((pixels, c_in)),
        flops=2 * pixels * c_in * c_out, nbytes=6 << 20,
    )(gpre_short, w_shortcut)
    crossed = [s.received for s in [s_expand_grad] + s_short_grad]
    g_reduce = after(sync(gsum), [s.keep for s in late], back_short, crossed)
    spread = TILE // dp
    early = Halving(early_sum.reshape(9 + blocks, spread, TILE), rep_bits, flat, devices)
    middle = [s_squeeze_grad, s_expand_grad] + s_short_grad

    reduce_back_call = call(
        functools.partial(reduce_back_kernel, quarter),
        (steps,),
        [
            plane_block(mid), plane_block(mid), all_tiles, all_tiles, count_spec, p_reduce,
            pl.BlockSpec((quarter, LANES), lambda k: (k, 0)), full((c_in, mid)),
            pl.BlockSpec((quarter, c_in), lambda k: (k, 0)), full(perm.shape),
        ],
        [plane_block(mid), pl.BlockSpec((4 * quarter, c_in), lambda k: (k, 0))],
        [shaped((4, pixels, mid), BF16), shaped((images * 4 * height * width, c_in), BF16)],
        flops=8 * pixels * c_in * mid, nbytes=10 << 20,
    )

    def reduce_back(summed):
        return reduce_back_call(
            grad_reduce, pre_reduce, s_reduce, summed, s_reduce, params, mask, w_reduce, back_short, perm_back
        )

    last = Later()

    def input_back(token):
        gpre_reduce, last.image_grad = reduce_back(after(g_reduce, token))
        stream = halving(
            outer_halves(
                core, planes.reshape(4 * pixels, c_in), pl.BlockSpec((4 * pixels, TILE), lambda b, *_: (0, b)),
                gpre_reduce.reshape(4 * pixels, mid), full((4 * pixels, mid)), whole, in_blocks, 1,
            ),
            order_reduce,
        )
        last.stream = stream
        last.moves.extend(stream.moves)
        return stream.keep

    def starts_of(first, order, rows):
        found = []
        for k in range(devices):
            start, left = first(k), rows
            for bit in order:
                left //= 2
                start += (k // bit % 2) * left
            found.append(start)
        return tuple(found)

    spread_starts = starts_of(lambda k: (k // rep) * spread, rep_bits, spread)
    early_out = Early(early, functools.partial(regroup, starts=spread_starts, total=9 + blocks))
    early_out.add_result(place=0, blocks=blocks, shape=(mid, c_out), down=False)
    early_out.add_result(place=blocks, blocks=9, shape=(9 * mid, mid), down=True)
    backs = [Return(stream, core_bit, flat, devices) for stream in late]
    for stream, back in zip(late, backs):
        stream.moves.extend(back.moves)
    input_step = Later()
    input_step.moves.append(input_back)
    token = run_streams(middle + late + [last, early, early_out, input_step], SCHEDULE, g_reduce)

    def gathered(shard):
        everything = lax.all_gather(shard.reshape(-1, TILE), AXES, axis=0, tiled=False)
        return functools.partial(regroup, everything, total=shard.shape[0])

    grad_w_widen, grad_w_window = early_out.results

    half_starts = lambda order: starts_of(lambda k: (k // core_bit % 2) * (TILE // 2), order, TILE // 2)
    regrouped = gathered(jnp.concatenate([s.keep for s in middle + [last.stream]], axis=0))
    grad_w_squeeze = regrouped(half_starts(order_squeeze), place=0, blocks=blocks, shape=(c_out, mid), down=True)
    grad_w_expand = regrouped(
        half_starts(order_expand), place=blocks, blocks=blocks, shape=(mid, c_out), down=False
    )
    grad_w_short = None
    for k in range(in_blocks):
        grad_w_short = regrouped(
            half_starts(order_short[k % 2]), place=(2 + k) * blocks, blocks=blocks, shape=(c_in, c_out),
            down=False, first=k, into=grad_w_short,
        )

    grad_w_spatial = None
    for (place, count), back in zip(spatial_parts, backs):
        grad_w_spatial = assemble(
            back.places(), back.pieces(), 0, count, (9 * mid, mid), lambda b, place=place: (place + b, 0),
            into=grad_w_spatial,
        )
    grad_w_reduce = regrouped(
        half_starts(order_reduce), place=(2 + in_blocks) * blocks, blocks=in_blocks, shape=(c_in, mid), down=True
    )
    grad_w_window, grad_w_spatial = (g.reshape(3, 3, mid, mid) for g in (grad_w_window, grad_w_spatial))

    shift_total = vector(g_both, 0, 16)
    return (
        block_out.reshape(cotangent.shape),
        last.image_grad.reshape(image_input.shape),
        grad_w_reduce,
        grad_w_spatial,
        grad_w_expand,
        grad_w_short,
        vector(jnp.sum(g_reduce, axis=0), ROWS, 8),
        vector(jnp.sum(g_reduce, axis=0), 0, 8),
        vector(jnp.sum(g_spatial, axis=0), ROWS, 8),
        vector(jnp.sum(g_spatial, axis=0), 0, 8),
        vector(g_both, ROWS, 16),
        shift_total,
        vector(g_both, 2 * ROWS, 16),
        shift_total,
        grad_w_squeeze,
        grad_w_window,
        grad_w_widen,
        vector(jnp.sum(g_squeeze, axis=0), ROWS, 8),
        vector(jnp.sum(g_squeeze, axis=0), 0, 8),
        vector(jnp.sum(g_window, axis=0), ROWS, 8),
        vector(jnp.sum(g_window, axis=0), 0, 8),
        vector(g_widen, ROWS, 8),
        vector(g_widen, 0, 8),
    )


def solution(mesh):
    split = P(AXES, None, None, None)
    return jax.shard_map(
        functools.partial(on_device, mesh.shape["dp"], mesh.shape["rep"]),
        mesh=mesh,
        in_specs=(split, P(AXES), P(AXES)) + (P(),) * 21 + (split,),
        out_specs=(split, split) + (P(),) * 21,
        check_vma=False,
    )
```
